32 devices in a mesh: stream: 2 (over core), blk: 16 (over z, y, x).
Axes of the slice: x: 2, y: 2, z: 4, core: 2. Of those that a mesh axis runs over, the one named last changes fastest.
Arguments:
- inputs: bfloat16 [2, 2, 2048, 1536], P(None, 'stream', 'blk'), may hold values from -6 to 6
- cotangent: bfloat16 [2, 2, 2048, 1536], P(None, 'stream', 'blk'), may hold values from -6 to 6
- seq_lengths: int32 [2, 2, 9], P(None, 'stream'), may hold values from 1 to 1984, as said below
- gain_attn: bfloat16 [1536], P(('stream', 'blk')), may hold values from 0.5 to 1.5
- gain_ffn: bfloat16 [1536], P(('stream', 'blk')), may hold values from 0.5 to 1.5
- w_query: bfloat16 [1536, 1536], P(('stream', 'blk')), may hold values from -0.15625 to 0.15625
- w_key: bfloat16 [1536, 768], P(('stream', 'blk')), may hold values from -0.15625 to 0.15625
- w_value: bfloat16 [1536, 768], P(('stream', 'blk')), may hold values from -0.15625 to 0.15625
- w_out: bfloat16 [1536, 1536], P(('stream', 'blk')), may hold values from -0.625 to 0.625
- w_gate: bfloat16 [1536, 4096], P(('stream', 'blk')), may hold values from -0.15625 to 0.15625
- w_up: bfloat16 [1536, 4096], P(('stream', 'blk')), may hold values from -0.15625 to 0.15625
- w_down: bfloat16 [4096, 1536], P(('stream', 'blk')), may hold values from -0.09375 to 0.09375
Outputs:
- output: bfloat16 [2, 2, 2048, 1536], P(None, 'stream', 'blk')
- input_grad: float32 [2, 2, 2048, 1536], P(None, 'stream', 'blk')
- grad_gain_attn: float32 [1536], P(('stream', 'blk'))
- grad_gain_ffn: float32 [1536], P(('stream', 'blk'))
- grad_w_query: float32 [1536, 1536], P(('stream', 'blk'))
- grad_w_key: float32 [1536, 768], P(('stream', 'blk'))
- grad_w_value: float32 [1536, 768], P(('stream', 'blk'))
- grad_w_out: float32 [1536, 1536], P(('stream', 'blk'))
- grad_w_gate: float32 [1536, 4096], P(('stream', 'blk'))
- grad_w_up: float32 [1536, 4096], P(('stream', 'blk'))
- grad_w_down: float32 [4096, 1536], P(('stream', 'blk'))
The draws below stay inside these ranges and needn't reach their ends.
Inputs may be any that keep to these rules, and one draw needn't show every extreme that they name: `seq_lengths`: the lengths of a pack sum to 2048; one sequence of each pack, at a place drawn from the seed, is the longest. In the packs of even-numbered micro-batches each other sequence holds at most (127) // 8 positions and together they hold a fixed number. In the packs of odd-numbered micro-batches each other sequence holds 64 to 192 positions and the longest holds exactly 1024.
All inputs are finite; a program needn't handle non-finite values.
Results may differ from the reference program's by a relative error of at most 0.019.
Values may be sent and summed in bfloat16 or wider, within the bound.
No kernel may reach another device: no remote copies, remote signals or barrier semaphores. Data moves between devices by JAX's collectives and lax.ppermute only.
A program may use at most 640 MiB of HBM per device.

```python
import math
import jax
import jax.numpy as jnp
from jax import lax

D = 1536
HQ = 16
HK = 8
DH = 96
FF = 4096
TOK_DEV = 128
MB = 2
NSEQ = 9
PACK_LEN = 2048


def draw_seq_lengths(key, part):
    key = jax.random.fold_in(key, 7)
    tight_key, loose_key, which_key = jax.random.split(key, 3)
    pair_count = (NSEQ - 1) // 2
    short_cap = (TOK_DEV - 1) // (NSEQ - 1)
    short_len = PACK_LEN // (2 * (NSEQ - 1))
    tight_values = jax.random.randint(tight_key, (MB, 2, pair_count), 1, short_cap + 1)
    loose_values = jax.random.randint(loose_key, (MB, 2, pair_count), short_len // 2, short_len + short_len // 2 + 1)
    spanning = (jnp.arange(MB, dtype=jnp.int32) % 2 == 0)[:, None, None]
    pair_values = jnp.where(spanning, tight_values, loose_values)
    pair_sum = jnp.where(spanning, short_cap + 1, 2 * short_len)
    which = jax.random.randint(which_key, (MB, 2, 1), 0, NSEQ)
    slots = jnp.arange(NSEQ, dtype=jnp.int32)[None, None, :]
    is_long = slots == which
    short_rank = slots - (slots > which).astype(jnp.int32)
    pair_index = jnp.broadcast_to(jnp.clip(short_rank // 2, 0, pair_count - 1), (MB, 2, NSEQ)).astype(jnp.int32)
    picked = jnp.take_along_axis(pair_values, pair_index, axis=-1)
    shorts = jnp.where(short_rank % 2 == 0, picked, pair_sum - picked)
    longest = PACK_LEN - pair_count * pair_sum
    return jnp.where(is_long, longest, shorts).astype(jnp.int32)


def level_of(stream_key, shape, shards, low, largest):
    loudness, own = 1.0, jax.random.fold_in(stream_key, 6)
    for dim, blocks in shards:
        draws = jnp.exp(jax.random.uniform(jax.random.fold_in(own, dim), (blocks,), jnp.float32, low / len(shards), largest / len(shards)))
        loudness = loudness * jnp.repeat(draws, shape[dim] // blocks).reshape([-1 if axis == dim else 1 for axis in range(len(shape))])
    return loudness


def centred(rng, shape, deviation, most, cuts=(), kind=jnp.bfloat16):
    array = jax.random.normal(rng, shape, jnp.float32) * deviation
    if len(cuts) > 0:
        array = level_of(rng, shape, cuts, -0.22, 0.18) * array
    return jnp.clip(array, min=-most, max=most).astype(kind)


def setup_inputs(seed: int = 0) -> dict:
    arg_keys = jax.random.split(jax.random.key(seed), 13)
    return {
        "inputs": centred(arg_keys[0], (MB, 2, PACK_LEN, D), 1.0, 6.0, ((1, 2), (2, 16))),
        "cotangent": centred(arg_keys[1], (MB, 2, PACK_LEN, D), 1.0, 6.0, ((1, 2), (2, 16))),
        "seq_lengths": draw_seq_lengths(jax.random.fold_in(arg_keys[12], 71), 0),
        "gain_attn": jnp.clip(1.0 + 0.1 * jax.random.normal(arg_keys[3], (D,), jnp.float32), 0.5, 1.5).astype(jnp.bfloat16),
        "gain_ffn": jnp.clip(1.0 + 0.1 * jax.random.normal(arg_keys[4], (D,), jnp.float32), 0.5, 1.5).astype(jnp.bfloat16),
        "w_query": centred(arg_keys[5], (D, HQ * DH), D ** -0.5, 0.15625, ((0, 32),)),
        "w_key": centred(arg_keys[6], (D, HK * DH), D ** -0.5, 0.15625, ((0, 32),)),
        "w_value": centred(arg_keys[7], (D, HK * DH), D ** -0.5, 0.15625, ((0, 32),)),
        "w_out": centred(arg_keys[8], (HQ * DH, D), (D // 16) ** -0.5, 0.625, ((0, 32),)),
        "w_gate": centred(arg_keys[9], (D, FF), D ** -0.5, 0.15625, ((0, 32),)),
        "w_up": centred(arg_keys[10], (D, FF), D ** -0.5, 0.15625, ((0, 32),)),
        "w_down": centred(arg_keys[11], (FF, D), FF ** -0.5, 0.09375, ((0, 32),)),
    }


@jax.custom_vjp
def low(v):
    return lax.optimization_barrier(v.astype(jnp.bfloat16)).astype(jnp.float32)

@jax.custom_vjp
def low_back(v):
    return v

def low_keep(v):
    return (low(v), None)

def low_pass(kept, grad):
    return (grad,)

def back_keep(v):
    return (v, None)

def back_low(kept, grad):
    return (low(grad),)
low.defvjp(low_keep, low_pass)
low_back.defvjp(back_keep, back_low)
epsilon = 1e-05
rope_base = 100000.0
masked_score = -1e+30

def rms_norm(values, gain_row):
    return values * lax.rsqrt(lax.optimization_barrier(jnp.mean(values * values, axis=-1, keepdims=True)) + epsilon) * gain_row

def project(values, weight):
    return jnp.einsum('bsd,dx->bsx', values, weight, precision=lax.Precision.HIGHEST)

def seq_start(lengths, positions):
    seq_ends = jnp.cumsum(lengths)
    return lax.optimization_barrier(jnp.sum(jnp.where(seq_ends[None, :] <= positions[:, None], lengths[None, :], 0), axis=1)).astype(jnp.int32)

def rope_tables(rope_place):
    half_width = DH // 2
    frequency = rope_base ** (-2.0 * jnp.arange(half_width, dtype=jnp.float32) / DH)
    angles = rope_place.astype(jnp.float32)[..., None] * frequency
    return (jnp.cos(angles), jnp.sin(angles))

def rotate(values, cos_table, sin_table):
    half_width = values.shape[-1] // 2
    first_half = values[..., :half_width]
    second_half = values[..., half_width:]
    return jnp.concatenate([first_half * cos_table - second_half * sin_table, second_half * cos_table + first_half * sin_table], axis=-1)

def attention(query_rot, key_rot, value_low, positions, starts):
    block_rows = math.gcd(PACK_LEN, 512)
    per_group = HQ // HK
    score_scale = 1.0 / math.sqrt(DH)

    def one_pack(pack_args):
        query_pack, key_all, value_all, start_pack = pack_args

        def one_block(block_args):
            query_block, block_place, block_start = block_args
            scores = jnp.einsum('qhgd,khd->hgqk', query_block, key_all, precision=lax.Precision.HIGHEST) * score_scale
            scores = low_back(scores)
            allowed = (positions[None, :] <= block_place[:, None]) & (positions[None, :] >= block_start[:, None])
            scores = jnp.where(allowed, scores, masked_score)
            weights = low(jax.nn.softmax(scores, axis=-1))
            mixed_values = jnp.einsum('hgqk,khd->qhgd', weights, value_all, precision=lax.Precision.HIGHEST)
            return mixed_values.reshape(block_rows, HQ * DH)
        block_count = PACK_LEN // block_rows
        block_args = (query_pack.reshape(block_count, block_rows, HK, per_group, DH), positions.reshape(block_count, block_rows), start_pack.reshape(block_count, block_rows))
        return lax.map(jax.checkpoint(one_block), block_args).reshape(PACK_LEN, HQ * DH)
    return lax.map(one_pack, (query_rot, key_rot, value_low, starts))

def reference(inputs, cotangent, seq_lengths, gain_attn, gain_ffn, w_query, w_key, w_value, w_out, w_gate, w_up, w_down):
    pack_count = MB * 2
    positions = jnp.arange(PACK_LEN, dtype=jnp.int32)
    starts = jax.vmap(lambda lengths: seq_start(lengths, positions))(seq_lengths.reshape(pack_count, NSEQ))
    cos_table, sin_table = rope_tables(positions[None, :] - starts)
    cos_table = cos_table[:, :, None, :]
    sin_table = sin_table[:, :, None, :]
    weights_f = tuple((weight.astype(jnp.float32) for weight in (gain_attn, gain_ffn, w_query, w_key, w_value, w_out, w_gate, w_up, w_down)))
    hidden_in = inputs.astype(jnp.float32).reshape(pack_count, PACK_LEN, D)

    def forward(layer_in, weight_set):
        gain_one, gain_two, query_w, key_w, value_w, out_w, gate_w, up_w, down_w = weight_set
        normed_one = low(rms_norm(layer_in, gain_one))
        query_pre = low_back(project(normed_one, query_w))
        key_pre = low_back(project(normed_one, key_w))
        value_low = low(low_back(project(normed_one, value_w)))
        query_rot = low(rotate(query_pre.reshape(pack_count, PACK_LEN, HQ, DH), cos_table, sin_table))
        key_rot = low(rotate(key_pre.reshape(pack_count, PACK_LEN, HK, DH), cos_table, sin_table))
        attended = attention(query_rot, key_rot, value_low.reshape(pack_count, PACK_LEN, HK, DH), positions, starts)
        attn_low = low(low_back(attended))
        middle = layer_in + low_back(project(attn_low, out_w))
        normed_two = low(rms_norm(middle, gain_two))
        gate_pre = low_back(project(normed_two, gate_w))
        up_pre = low_back(project(normed_two, up_w))
        hidden = low(jax.nn.silu(gate_pre) * up_pre)
        return middle + low_back(project(hidden, down_w))
    result, pull_back = jax.vjp(forward, hidden_in, weights_f)
    grad_in, grad_weights = pull_back(cotangent.astype(jnp.float32).reshape(pack_count, PACK_LEN, D))
    shape_out = (MB, 2, PACK_LEN, D)
    return (result.reshape(shape_out).astype(jnp.bfloat16), grad_in.reshape(shape_out), grad_weights[0], grad_weights[1], grad_weights[2], grad_weights[3], grad_weights[4], grad_weights[5], grad_weights[6], grad_weights[7], grad_weights[8])
```

```python
import math

import jax
import jax.numpy as jnp
import numpy as np
from jax import lax
from jax.experimental import pallas as pl
from jax.experimental.pallas import tpu as pltpu
from jax.sharding import Mesh
from jax.sharding import PartitionSpec as P

HQ = 16
HK = 8
DH = 96
PLANE = 4
LANES = 128
VMEM_BYTES = 50 * 1024 * 1024

epsilon = 1e-05
rope_base = 100000.0
masked_score = -1e30
score_scale = 1.0 / math.sqrt(DH)
exp2_scale = score_scale * math.log2(math.e)

f32 = jnp.float32
bf16 = jnp.bfloat16


def spread(heads):
    table = np.zeros((heads * DH, heads * LANES), np.float32)
    for head in range(heads):
        for i in range(DH):
            lane = i if i < DH // 2 else i + (LANES - DH) // 2
            table[head * DH + i, head * LANES + lane] = 1.0
    return jnp.asarray(table, bf16)


def rms_scale(values):
    return lax.rsqrt(jnp.mean(values * values, axis=-1, keepdims=True) + epsilon)


def dot(a, b):
    return jnp.dot(a, b, preferred_element_type=f32)


def dot_nt(a, b):
    return lax.dot_general(a, b, (((1,), (1,)), ((), ())), preferred_element_type=f32)


def dot_tn(a, b):
    return lax.dot_general(a, b, (((0,), (0,)), ((), ())), preferred_element_type=f32)


def project_kernel(x_ref, gain_ref, w_ref, cos_ref, sin_ref, e_ref, n_ref, q_ref, kv_ref):
    x = x_ref[...].astype(f32)
    normed = (x * rms_scale(x) * gain_ref[...]).astype(bf16)
    n_ref[...] = normed
    pre = dot(normed, w_ref[...])
    cos, sin = cos_ref[...], sin_ref[...]
    parts = []
    for head in range(8):
        piece = pre[:, head * LANES : (head + 1) * LANES]
        if head < 6:
            piece = piece * cos + pltpu.roll(piece, LANES // 2, 1) * sin
        parts.append(piece.astype(bf16))
    q_ref[...] = jnp.concatenate(parts[:4], axis=1)
    kv_ref[...] = dot_nt(jnp.concatenate(parts[4:], axis=1), e_ref[...]).astype(bf16)


def project(x, gain, w_pad, cos, sin, e4):
    rows, width = x.shape
    step = min(256, rows)
    out_w = w_pad.shape[1]
    whole = lambda a: pl.BlockSpec(a.shape, lambda i: (0,) * a.ndim)
    by_row = lambda c: pl.BlockSpec((step, c), lambda i: (i, 0))
    return pl.pallas_call(
        project_kernel,
        grid=(rows // step,),
        in_specs=[by_row(width), whole(gain), whole(w_pad), by_row(LANES), by_row(LANES), whole(e4)],
        out_specs=[by_row(width), by_row(4 * LANES), by_row(4 * DH)],
        out_shape=[
            jax.ShapeDtypeStruct((rows, width), bf16),
            jax.ShapeDtypeStruct((rows, 4 * LANES), bf16),
            jax.ShapeDtypeStruct((rows, 4 * DH), bf16),
        ],
        compiler_params=pltpu.CompilerParams(vmem_limit_bytes=VMEM_BYTES),
        cost_estimate=pl.CostEstimate(
            flops=2 * rows * width * out_w, bytes_accessed=2 * (2 * rows * width + width * out_w), transcendentals=0
        ),
        name="project",
    )(x, gain, w_pad, cos, sin, e4)


def allowed_of(info_ref, k, chunk, qpos_ref, qbeg_ref, kpos_ref):
    kpos = kpos_ref[...] + (info_ref[0] - k) * chunk
    return (kpos <= qpos_ref[...]) & (kpos >= qbeg_ref[0])


def useful_of(info_ref, m, k, chunk):
    z = info_ref[0]
    return (k <= z) & ((z - k + 1) * chunk - 1 >= info_ref[1 + m])


def stack_heads(block, h):
    return jnp.concatenate(
        [block[:, (2 * h) * LANES : (2 * h + 1) * LANES], block[:, (2 * h + 1) * LANES : (2 * h + 2) * LANES]], axis=0
    )


def attend_kernel(
    info_ref, q_ref, kv_ref, qpos_ref, qbeg_ref, kpos_ref, e_ref, att_ref, low_ref, lse_ref, top_s, acc_s
):
    m, k, last = pl.program_id(0), pl.program_id(1), pl.num_programs(1) - 1
    chunk = kv_ref.shape[2]

    @pl.when(k == 0)
    def _():
        top_s[...] = jnp.full(top_s.shape, masked_score, f32)
        acc_s[...] = jnp.zeros(acc_s.shape, f32)

    @pl.when(useful_of(info_ref, m, k, chunk))
    def _():
        allowed = allowed_of(info_ref, k, chunk, qpos_ref, qbeg_ref, kpos_ref)
        kv = kv_ref[0, 0]
        q = q_ref[0]
        one_lane = (lax.broadcasted_iota(jnp.int32, (1, LANES), 1) == DH // 2).astype(f32)
        for h in range(2):
            keys = dot(kv, e_ref[:, h * LANES : (h + 1) * LANES]).astype(bf16)
            vals = (dot(kv, e_ref[:, (2 + h) * LANES : (3 + h) * LANES]) + one_lane).astype(bf16)
            s = jnp.where(allowed, dot_nt(keys, stack_heads(q, h)), masked_score)
            old = top_s[h]
            new = jnp.maximum(old, jnp.max(s, axis=0, keepdims=True))
            w = jnp.where(allowed, jnp.exp2((s - new) * exp2_scale), 0.0).astype(bf16)
            acc_s[h] = acc_s[h] * jnp.exp2((old - new) * exp2_scale) + dot_tn(vals, w)
            top_s[h] = new

    @pl.when(k == last)
    def _():
        parts = []
        for h in range(2):
            acc = acc_s[h]
            total = acc[DH // 2 : DH // 2 + 1, :]
            lse_ref[0, h] = top_s[h] * exp2_scale + jnp.log2(total)
            flat = (acc / total).T
            rows = flat.shape[0] // 2
            parts += [flat[:rows], flat[rows:]]
        att = jnp.concatenate(parts, axis=1)
        att_ref[0] = att
        low_ref[0] = dot_nt(att.astype(bf16), e_ref[...]).astype(bf16)


def attend(info, q, kv, qpos, qbeg, kpos, e4):
    micro, rows, _ = q.shape
    chunks, _, chunk, width = kv.shape
    return pl.pallas_call(
        attend_kernel,
        grid_spec=pltpu.PrefetchScalarGridSpec(
            num_scalar_prefetch=1,
            grid=(micro, chunks),
            in_specs=[
                pl.BlockSpec((1, rows, 4 * LANES), lambda m, k, i: (m, 0, 0)),
                pl.BlockSpec((1, 1, chunk, width), lambda m, k, i: (k, m, 0, 0)),
                pl.BlockSpec((1, 2 * rows), lambda m, k, i: (0, 0)),
                pl.BlockSpec((1, 1, 2 * rows), lambda m, k, i: (m, 0, 0)),
                pl.BlockSpec((chunk, 1), lambda m, k, i: (0, 0)),
                pl.BlockSpec(e4.shape, lambda m, k, i: (0, 0)),
            ],
            out_specs=[
                pl.BlockSpec((1, rows, 4 * LANES), lambda m, k, i: (m, 0, 0)),
                pl.BlockSpec((1, rows, 4 * DH), lambda m, k, i: (m, 0, 0)),
                pl.BlockSpec((1, 2, 1, 2 * rows), lambda m, k, i: (m, 0, 0, 0)),
            ],
            scratch_shapes=[pltpu.VMEM((2, 1, 2 * rows), f32), pltpu.VMEM((2, LANES, 2 * rows), f32)],
        ),
        out_shape=[
            jax.ShapeDtypeStruct((micro, rows, 4 * LANES), f32),
            jax.ShapeDtypeStruct((micro, rows, 4 * DH), bf16),
            jax.ShapeDtypeStruct((micro, 2, 1, 2 * rows), f32),
        ],
        compiler_params=pltpu.CompilerParams(vmem_limit_bytes=VMEM_BYTES),
        cost_estimate=pl.CostEstimate(
            flops=micro * chunks * 16 * rows * chunk * LANES,
            bytes_accessed=4 * micro * rows * 4 * LANES + 2 * kv.size,
            transcendentals=micro * chunks * 4 * rows * chunk,
        ),
        name="attend",
    )(info, q, kv, qpos, qbeg, kpos, e4)


def attend_back_kernel(
    info_ref, q_ref, kv_ref, g_ref, att_ref, lse_ref, qpos_ref, qbeg_ref, kpos_ref, cos_ref, sin_ref, cosk_ref,
    sink_ref, e_ref, dq_ref, dkv_ref, delta_s, go_s, dq_s,
):
    m, k, last = pl.program_id(0), pl.program_id(1), pl.num_programs(1) - 1
    chunk = kv_ref.shape[2]
    useful = useful_of(info_ref, m, k, chunk)

    @pl.when(k == 0)
    def _():
        dq_s[...] = jnp.zeros(dq_s.shape, f32)
        go = dot(g_ref[0], e_ref[...])
        for h in range(2):
            go_h = stack_heads(go, h)
            go_s[h] = go_h.astype(bf16)
            prod = go_h * stack_heads(att_ref[0], h)
            delta_s[h] = jnp.sum(prod.T, axis=0, keepdims=True)

    @pl.when(useful)
    def _():
        allowed = allowed_of(info_ref, k, chunk, qpos_ref, qbeg_ref, kpos_ref)
        kv = kv_ref[0, 0]
        q = q_ref[0]
        cosk, sink = cosk_ref[0, 0], sink_ref[0, 0]
        grad_keys, grad_vals = [], []
        for h in range(2):
            keys = dot(kv, e_ref[:, h * LANES : (h + 1) * LANES]).astype(bf16)
            vals = dot(kv, e_ref[:, (2 + h) * LANES : (3 + h) * LANES]).astype(bf16)
            q_h = stack_heads(q, h)
            go_h = go_s[h]
            s = dot_nt(keys, q_h)
            w = jnp.where(allowed, jnp.exp2(s * exp2_scale - lse_ref[0, h]), 0.0)
            grad_vals.append(dot(w.astype(bf16), go_h).astype(bf16))
            ds = (w * (dot_nt(vals, go_h) - delta_s[h])).astype(bf16)
            dq_s[h] = dq_s[h] + dot_tn(keys, ds)
            gk = dot(ds, q_h) * score_scale
            gk = gk * cosk + pltpu.roll(gk * sink, LANES // 2, 1)
            grad_keys.append(gk.astype(bf16))
        dkv_ref[0, 0] = dot_nt(jnp.concatenate(grad_keys + grad_vals, axis=1), e_ref[...]).astype(bf16)

    @pl.when(jnp.logical_not(useful))
    def _():
        dkv_ref[...] = jnp.zeros(dkv_ref.shape, bf16)

    @pl.when(k == last)
    def _():
        cos, sin = cos_ref[0, 0], sin_ref[0, 0]
        parts = []
        for h in range(2):
            flat = dq_s[h].T * score_scale
            rows = flat.shape[0] // 2
            for piece in (flat[:rows], flat[rows:]):
                parts.append((piece * cos + pltpu.roll(piece * sin, LANES // 2, 1)).astype(bf16))
        dq_ref[0] = dot_nt(jnp.concatenate(parts, axis=1), e_ref[...]).astype(bf16)


def attend_back(info, q, kv, g, att, lse, qpos, qbeg, kpos, cos, sin, e4):
    micro, rows, _ = q.shape
    chunks, _, chunk, width = kv.shape
    per_micro = lambda c: pl.BlockSpec((1, rows, c), lambda m, k, i: (m, 0, 0))
    return pl.pallas_call(
        attend_back_kernel,
        grid_spec=pltpu.PrefetchScalarGridSpec(
            num_scalar_prefetch=1,
            grid=(micro, chunks),
            in_specs=[
                per_micro(4 * LANES),
                pl.BlockSpec((1, 1, chunk, width), lambda m, k, i: (k, m, 0, 0)),
                per_micro(4 * DH),
                per_micro(4 * LANES),
                pl.BlockSpec((1, 2, 1, 2 * rows), lambda m, k, i: (m, 0, 0, 0)),
                pl.BlockSpec((1, 2 * rows), lambda m, k, i: (0, 0)),
                pl.BlockSpec((1, 1, 2 * rows), lambda m, k, i: (m, 0, 0)),
                pl.BlockSpec((chunk, 1), lambda m, k, i: (0, 0)),
                pl.BlockSpec((1, 1, chunk, LANES), lambda m, k, i: (0, m, 0, 0)),
                pl.BlockSpec((1, 1, chunk, LANES), lambda m, k, i: (0, m, 0, 0)),
                pl.BlockSpec((1, 1, chunk, LANES), lambda m, k, i: (k, m, 0, 0)),
                pl.BlockSpec((1, 1, chunk, LANES), lambda m, k, i: (k, m, 0, 0)),
                pl.BlockSpec(e4.shape, lambda m, k, i: (0, 0)),
            ],
            out_specs=[
                per_micro(4 * DH),
                pl.BlockSpec((1, 1, chunk, width), lambda m, k, i: (k, m, 0, 0)),
            ],
            scratch_shapes=[
                pltpu.VMEM((2, 1, 2 * rows), f32),
                pltpu.VMEM((2, 2 * rows, LANES), bf16),
                pltpu.VMEM((2, LANES, 2 * rows), f32),
            ],
        ),
        out_shape=[
            jax.ShapeDtypeStruct((micro, rows, 4 * DH), bf16),
            jax.ShapeDtypeStruct(kv.shape, bf16),
        ],
        compiler_params=pltpu.CompilerParams(vmem_limit_bytes=VMEM_BYTES),
        cost_estimate=pl.CostEstimate(
            flops=micro * chunks * 40 * rows * chunk * LANES,
            bytes_accessed=8 * micro * rows * 4 * LANES + 4 * kv.size,
            transcendentals=micro * chunks * 4 * rows * chunk,
        ),
        name="attend_back",
    )(info, q, kv, g, att, lse, qpos, qbeg, kpos, cos, sin, cos, sin, e4)


def beside(value, bit):
    return lax.ppermute(value, "plane", [(i, i ^ bit) for i in range(PLANE)])


def other_core(value):
    return lax.ppermute(value, "stream", [(0, 1), (1, 0)])


def along(value, step, wrap):
    size = lax.axis_size("zed")
    pairs = [(i, (i + step) % size) for i in range(size) if wrap or 0 <= i + step < size]
    return lax.ppermute(value, "zed", pairs)


def plane_gather(own):
    first, second = own[0], own[1]
    first = jnp.stack([first, beside(first, 1)])
    second = jnp.stack([second, beside(second, 2)])
    first_more, second_more = beside(first, 2), beside(second, 1)
    return jnp.stack(
        [
            jnp.concatenate([first, first_more]),
            jnp.stack([second[0], second_more[0], second[1], second_more[1]]),
        ]
    )


def plane_sum(terms):
    first, second = terms[0], terms[1]
    got_first = beside(jnp.stack([first[1], first[3]]).astype(bf16), 1)
    got_second = beside(second[2:4].astype(bf16), 2)
    more_first = beside((first[2] + got_first[1]).astype(bf16), 2)
    more_second = beside((second[1] + got_second[1]).astype(bf16), 1)
    return jnp.stack([first[0] + got_first[0] + more_first, second[0] + got_second[0] + more_second])


def weight_gather(blocks):
    size = lax.axis_size("zed")
    s, z = lax.axis_index("stream"), lax.axis_index("zed")
    fulls = []
    for block in blocks:
        full = jnp.zeros((2 * size,) + block.shape, block.dtype)
        for k in range(size):
            place = lax.rem(z - k + size, size)
            full = lax.dynamic_update_slice(full, block[None], (s * size + place, 0, 0))
            full = lax.dynamic_update_slice(full, other_core(block)[None], ((1 - s) * size + place, 0, 0))
            if k < size - 1:
                block = along(block, 1, True)
        fulls.append(full.reshape((-1,) + block.shape[1:]))
    return fulls


def weight_scatter(full, kind):
    size = lax.axis_size("zed")
    s, z = lax.axis_index("stream"), lax.axis_index("zed")
    full = full.reshape((2, size, -1) + full.shape[1:])
    mine = lax.dynamic_index_in_dim(full, s, 0, keepdims=False)
    theirs = lax.dynamic_index_in_dim(full, 1 - s, 0, keepdims=False)
    half = (mine.astype(f32) + other_core(theirs).astype(f32)).astype(kind)
    total = lax.dynamic_index_in_dim(half, lax.rem(z + 1, size), 0, keepdims=False).astype(f32)
    for k in range(size - 2, -1, -1):
        moved = along(total.astype(kind), -1, True).astype(f32)
        total = moved + lax.dynamic_index_in_dim(half, lax.rem(z - k + size, size), 0, keepdims=False).astype(f32)
    return total


def plane_swap(value, split, concat):
    return lax.all_to_all(value, "plane", split_axis=split, concat_axis=concat, tiled=True)


def on_device(inputs, cotangent, seq_lengths, gain_attn, gain_ffn, w_query, w_key, w_value, w_out, w_gate, w_up, w_down):
    size = lax.axis_size("zed")
    z, p = lax.axis_index("zed"), lax.axis_index("plane")
    micro, _, tok_rows, width = inputs.shape
    chunk = PLANE * tok_rows
    tokens = micro * chunk
    shard_rows = w_query.shape[0]
    ff_block = w_down.shape[0]
    ff_blocks = 2 * size
    ff_part = ff_blocks * ff_block
    q_part, kv_part = HQ * DH // PLANE, HK * DH // PLANE
    out_part = width // PLANE
    e4, e8 = spread(4), spread(8)

    def by_part(weight):
        return weight.reshape(shard_rows, PLANE, -1)

    def by_ff_part(weight):
        return weight.reshape(shard_rows, ff_blocks, PLANE, ff_block).transpose(0, 2, 1, 3).reshape(shard_rows, PLANE, -1)

    own_in = inputs[:, 0]
    own_cot = cotangent[:, 0]
    gathered_in = plane_gather(own_in).reshape(tokens, width)
    qkv_bundle = jnp.concatenate([by_part(w_query), by_part(w_key), by_part(w_value)], axis=2).reshape(shard_rows, -1)
    qkv_block = plane_swap(qkv_bundle, 1, 0)
    gains = jnp.stack([gain_attn, gain_ffn])
    gains_one = jnp.stack([gains, beside(gains, 1)])
    gains_all = jnp.concatenate([gains_one, beside(gains_one, 2)])
    gains_all = jnp.take(gains_all, jnp.arange(PLANE) ^ p, axis=0)
    full_qkv, full_gains = weight_gather([qkv_block, gains_all.reshape(PLANE, 2 * shard_rows)])
    full_gains = full_gains.reshape(-1, 2, shard_rows).transpose(1, 0, 2).reshape(2, width).astype(f32)
    gain_one, gain_two = full_gains[0:1], full_gains[1:2]
    ffn_bundle = jnp.concatenate([by_ff_part(w_gate), by_ff_part(w_up), by_part(w_out)], axis=2).reshape(shard_rows, -1)
    ffn_block = plane_swap(ffn_bundle, 1, 0)
    full_gu, full_oc, full_down = weight_gather([ffn_block[:, : 2 * ff_part], ffn_block[:, 2 * ff_part :], w_down])
    full_out = plane_swap(full_oc, 0, 1)
    gathered_cot = plane_gather(own_cot).reshape(tokens, width)

    slot_place = ((jnp.arange(PLANE, dtype=jnp.int32) ^ p)[:, None] * tok_rows + jnp.arange(tok_rows, dtype=jnp.int32)[None, :]).reshape(chunk)
    chunk_place = (z - jnp.arange(size, dtype=jnp.int32))[:, None] * chunk + slot_place[None, :]
    lengths = seq_lengths[:, 0]
    seq_ends = jnp.cumsum(lengths, axis=1)
    begins = jnp.sum(
        jnp.where(seq_ends[:, None, None, :] <= chunk_place[None, :, :, None], lengths[:, None, None, :], 0), axis=-1
    )
    own_begin = begins[:, 0]
    lane = np.arange(LANES)
    place_in_half = lane % (LANES // 2)
    real = place_in_half < DH // 2
    frequency = jnp.where(
        real, rope_base ** (-2.0 * jnp.asarray(np.minimum(place_in_half, DH // 2 - 1), f32) / DH), 0.0
    )
    rope_place = (chunk_place[None] - begins).astype(f32)
    angles = jnp.maximum(rope_place, 0.0).transpose(1, 0, 2)[..., None] * frequency
    cos = jnp.where(real, jnp.cos(angles), 0.0)
    sin = jnp.sin(angles) * jnp.asarray(np.where(real, np.where(lane < LANES // 2, -1.0, 1.0), 0.0), f32)
    info = jnp.concatenate([jnp.reshape(z, (1,)).astype(jnp.int32), jnp.min(own_begin, axis=1)])
    qpos = jnp.tile(chunk_place[0], 2)[None]
    qbeg = jnp.tile(own_begin, (1, 2))[:, None]
    kpos = slot_place[:, None]

    w_pad = dot(full_qkv, e8).astype(bf16)
    normed_one, q_rot, kv_own = project(
        gathered_in, gain_one, w_pad, cos[0].reshape(tokens, LANES), sin[0].reshape(tokens, LANES), e4
    )
    q_rot = q_rot.reshape(micro, chunk, 4 * LANES)
    kv_piece = kv_own.reshape(micro, chunk, 4 * DH)
    kv_pieces = [kv_piece]
    for _ in range(size - 1):
        kv_piece = along(kv_piece, 1, False)
        kv_pieces.append(kv_piece)
    kv_all = jnp.stack(kv_pieces)
    attended, attn_low, lse = attend(info, q_rot, kv_all, qpos, qbeg, kpos, e4)
    attn_low = attn_low.reshape(tokens, q_part)
    branch = plane_sum(dot(attn_low, full_out).reshape(micro, PLANE, tok_rows, width))
    layer_in = own_in.astype(f32)
    middle = layer_in + branch

    scale_two = rms_scale(middle)
    normed_two = plane_gather((middle * scale_two * gain_two).astype(bf16)).reshape(tokens, width)
    pre = dot(normed_two, full_gu)
    gate_pre, up_pre = pre[:, :ff_part], pre[:, ff_part:]
    sigmoid_gate = jax.nn.sigmoid(gate_pre)
    silu_gate = gate_pre * sigmoid_gate
    hidden = (silu_gate * up_pre).astype(bf16)
    grad_hidden = dot_nt(gathered_cot, full_down)
    grad_gate = (grad_hidden * up_pre * sigmoid_gate * (1.0 + gate_pre * (1.0 - sigmoid_gate))).astype(bf16)
    grad_up = (grad_hidden * silu_gate).astype(bf16)
    grad_gu = jnp.concatenate([grad_gate, grad_up], axis=1)
    grad_normed_two = plane_sum(dot_nt(grad_gu, full_gu).reshape(micro, PLANE, tok_rows, width))
    result = middle + plane_sum(dot(hidden, full_down).reshape(micro, PLANE, tok_rows, width))
    output = result.astype(bf16)
    term_gu = dot_tn(normed_two, grad_gu).astype(bf16)
    term_down = dot_tn(hidden, gathered_cot).astype(bf16)

    grad_y = own_cot.astype(f32)
    grad_gain_two = jnp.sum(grad_normed_two * middle * scale_two, axis=(0, 1))
    weighted = grad_normed_two * gain_two
    grad_middle = (
        grad_y
        + scale_two * weighted
        - middle * scale_two**3 * jnp.mean(middle * weighted, axis=-1, keepdims=True)
    )
    grad_branch = plane_gather(grad_middle.astype(bf16)).reshape(tokens, width)
    term_out = plane_swap(dot_tn(attn_low, grad_branch).astype(bf16), 1, 0)
    grad_attn = dot_nt(grad_branch, full_out).astype(bf16).reshape(micro, chunk, q_part)

    grad_query, grad_kv = attend_back(info, q_rot, kv_all, grad_attn, attended, lse, qpos, qbeg, kpos, cos, sin, e4)
    own_kv = grad_kv[size - 1].astype(f32)
    for k in range(size - 2, -1, -1):
        own_kv = along(own_kv.astype(bf16), -1, False).astype(f32) + grad_kv[k].astype(f32)
    grad_qkv = jnp.concatenate([grad_query.reshape(tokens, q_part), own_kv.astype(bf16).reshape(tokens, 2 * kv_part)], axis=1)
    grad_normed_part = dot_nt(grad_qkv, full_qkv)
    full_in = gathered_in.astype(f32)
    grad_gain_one = jnp.sum(grad_normed_part * full_in * rms_scale(full_in), axis=0)
    grad_normed_one = plane_sum(grad_normed_part.reshape(micro, PLANE, tok_rows, width))
    term_qkv = dot_tn(normed_one, grad_qkv).astype(bf16)
    scale_one = rms_scale(layer_in)
    weighted = grad_normed_one * gain_one
    input_grad = (
        grad_middle
        + scale_one * weighted
        - layer_in * scale_one**3 * jnp.mean(layer_in * weighted, axis=-1, keepdims=True)
    )

    def from_parts(term):
        return term.reshape(shard_rows, PLANE, -1)

    def from_ff_parts(term):
        return term.reshape(shard_rows, PLANE, ff_blocks, ff_block).transpose(0, 2, 1, 3).reshape(shard_rows, -1)

    sum_gu = plane_swap(weight_scatter(term_gu, bf16).astype(bf16), 0, 1).astype(f32).reshape(shard_rows, PLANE, 2, ff_part)
    sum_down = weight_scatter(term_down, bf16)
    sum_out = plane_swap(weight_scatter(term_out, bf16).astype(bf16), 0, 1).astype(f32)
    sum_qkv = from_parts(plane_swap(weight_scatter(term_qkv, bf16).astype(bf16), 0, 1).astype(f32))
    gain_terms = jnp.stack([grad_gain_one, grad_gain_two]).reshape(2, ff_blocks, PLANE, shard_rows).transpose(1, 2, 0, 3)
    gain_sum = weight_scatter(gain_terms.reshape(ff_blocks * PLANE, 2 * shard_rows), f32)
    for bit in (1, 2):
        gain_sum = gain_sum + beside(gain_sum, bit)
    gain_own = lax.dynamic_index_in_dim(gain_sum, p, 0, keepdims=False).reshape(2, shard_rows)
    return (
        output[:, None],
        input_grad[:, None],
        gain_own[0],
        gain_own[1],
        sum_qkv[:, :, :q_part].reshape(shard_rows, -1),
        sum_qkv[:, :, q_part : q_part + kv_part].reshape(shard_rows, -1),
        sum_qkv[:, :, q_part + kv_part :].reshape(shard_rows, -1),
        sum_out,
        from_ff_parts(sum_gu[:, :, 0]),
        from_ff_parts(sum_gu[:, :, 1]),
        sum_down,
    )


def solution(mesh):
    blocks = mesh.shape["blk"]
    grid = Mesh(mesh.devices.reshape(2, blocks // PLANE, PLANE), ("stream", "zed", "plane"))
    tokens = P(None, "stream", ("zed", "plane"), None)
    vector = P(("stream", "zed", "plane"))
    matrix = P(("stream", "zed", "plane"), None)
    return jax.shard_map(
        on_device,
        mesh=grid,
        in_specs=(tokens, tokens, P(None, "stream", None), vector, vector) + (matrix,) * 7,
        out_specs=(tokens, tokens, vector, vector) + (matrix,) * 7,
        check_vma=False,
    )
```

```python
import math

import jax
import jax.numpy as jnp
import numpy as np
from jax import lax
from jax.experimental import pallas as pl
from jax.experimental.pallas import tpu as pltpu
from jax.sharding import Mesh
from jax.sharding import PartitionSpec as P

HQ = 16
HK = 8
DH = 96
PLANE = 4
LANES = 128
VMEM_BYTES = 50 * 1024 * 1024

epsilon = 1e-05
rope_base = 100000.0
masked_score = -1e30
score_scale = 1.0 / math.sqrt(DH)
exp2_scale = score_scale * math.log2(math.e)

f32 = jnp.float32
bf16 = jnp.bfloat16


def spread(heads):
    table = np.zeros((heads * DH, heads * LANES), np.float32)
    for head in range(heads):
        for i in range(DH):
            lane = i if i < DH // 2 else i + (LANES - DH) // 2
            table[head * DH + i, head * LANES + lane] = 1.0
    return jnp.asarray(table, bf16)


def rms_scale(values):
    return lax.rsqrt(jnp.mean(values * values, axis=-1, keepdims=True) + epsilon)


def dot(a, b):
    return jnp.dot(a, b, preferred_element_type=f32)


def dot_nt(a, b):
    return lax.dot_general(a, b, (((1,), (1,)), ((), ())), preferred_element_type=f32)


def dot_tn(a, b):
    return lax.dot_general(a, b, (((0,), (0,)), ((), ())), preferred_element_type=f32)


def project_kernel(x_ref, gain_ref, w_ref, cos_ref, sin_ref, e_ref, n_ref, q_ref, kv_ref):
    x = x_ref[...].astype(f32)
    normed = (x * rms_scale(x) * gain_ref[...]).astype(bf16)
    n_ref[...] = normed
    pre = dot(normed, w_ref[...])
    cos, sin = cos_ref[...], sin_ref[...]
    parts = []
    for head in range(8):
        piece = pre[:, head * LANES : (head + 1) * LANES]
        if head < 6:
            piece = piece * cos + pltpu.roll(piece, LANES // 2, 1) * sin
        parts.append(piece.astype(bf16))
    q_ref[...] = jnp.concatenate(parts[:4], axis=1)
    kv_ref[...] = dot_nt(jnp.concatenate(parts[4:], axis=1), e_ref[...]).astype(bf16)


def project(x, gain, w_pad, cos, sin, e4):
    rows, width = x.shape
    step = min(256, rows)
    out_w = w_pad.shape[1]
    whole = lambda a: pl.BlockSpec(a.shape, lambda i: (0,) * a.ndim)
    by_row = lambda c: pl.BlockSpec((step, c), lambda i: (i, 0))
    return pl.pallas_call(
        project_kernel,
        grid=(rows // step,),
        in_specs=[by_row(width), whole(gain), whole(w_pad), by_row(LANES), by_row(LANES), whole(e4)],
        out_specs=[by_row(width), by_row(4 * LANES), by_row(4 * DH)],
        out_shape=[
            jax.ShapeDtypeStruct((rows, width), bf16),
            jax.ShapeDtypeStruct((rows, 4 * LANES), bf16),
            jax.ShapeDtypeStruct((rows, 4 * DH), bf16),
        ],
        compiler_params=pltpu.CompilerParams(vmem_limit_bytes=VMEM_BYTES),
        cost_estimate=pl.CostEstimate(
            flops=2 * rows * width * out_w, bytes_accessed=2 * (2 * rows * width + width * out_w), transcendentals=0
        ),
        name="project",
    )(x, gain, w_pad, cos, sin, e4)


def allowed_of(info_ref, k, chunk, qpos_ref, qbeg_ref, kpos_ref):
    kpos = kpos_ref[...] + (info_ref[0] - k) * chunk
    return (kpos <= qpos_ref[...]) & (kpos >= qbeg_ref[0])


def useful_of(info_ref, m, k, chunk):
    z = info_ref[0]
    return (k <= z) & ((z - k + 1) * chunk - 1 >= info_ref[1 + m])


def stack_heads(block, h):
    return jnp.concatenate(
        [block[:, (2 * h) * LANES : (2 * h + 1) * LANES], block[:, (2 * h + 1) * LANES : (2 * h + 2) * LANES]], axis=0
    )


def attend_kernel(
    info_ref, q_ref, kv_ref, qpos_ref, qbeg_ref, kpos_ref, e_ref, att_ref, low_ref, lse_ref, top_s, acc_s
):
    m, k, last = pl.program_id(0), pl.program_id(1), pl.num_programs(1) - 1
    chunk = kv_ref.shape[2]

    @pl.when(k == 0)
    def _():
        top_s[...] = jnp.full(top_s.shape, masked_score, f32)
        acc_s[...] = jnp.zeros(acc_s.shape, f32)

    @pl.when(useful_of(info_ref, m, k, chunk))
    def _():
        allowed = allowed_of(info_ref, k, chunk, qpos_ref, qbeg_ref, kpos_ref)
        kv = kv_ref[0, 0]
        q = q_ref[0]
        one_lane = (lax.broadcasted_iota(jnp.int32, (1, LANES), 1) == DH // 2).astype(f32)
        for h in range(2):
            keys = dot(kv, e_ref[:, h * LANES : (h + 1) * LANES]).astype(bf16)
            vals = (dot(kv, e_ref[:, (2 + h) * LANES : (3 + h) * LANES]) + one_lane).astype(bf16)
            s = jnp.where(allowed, dot_nt(keys, stack_heads(q, h)), masked_score)
            old = top_s[h]
            new = jnp.maximum(old, jnp.max(s, axis=0, keepdims=True))
            w = jnp.where(allowed, jnp.exp2((s - new) * exp2_scale), 0.0).astype(bf16)
            acc_s[h] = acc_s[h] * jnp.exp2((old - new) * exp2_scale) + dot_tn(vals, w)
            top_s[h] = new

    @pl.when(k == last)
    def _():
        parts = []
        for h in range(2):
            acc = acc_s[h]
            total = acc[DH // 2 : DH // 2 + 1, :]
            lse_ref[0, h] = top_s[h] * exp2_scale + jnp.log2(total)
            flat = (acc / total).T
            rows = flat.shape[0] // 2
            parts += [flat[:rows], flat[rows:]]
        att = jnp.concatenate(parts, axis=1)
        att_ref[0] = att
        low_ref[0] = dot_nt(att.astype(bf16), e_ref[...]).astype(bf16)


def attend(info, q, kv, qpos, qbeg, kpos, e4):
    micro, rows, _ = q.shape
    chunks, _, chunk, width = kv.shape
    return pl.pallas_call(
        attend_kernel,
        grid_spec=pltpu.PrefetchScalarGridSpec(
            num_scalar_prefetch=1,
            grid=(micro, chunks),
            in_specs=[
                pl.BlockSpec((1, rows, 4 * LANES), lambda m, k, i: (m, 0, 0)),
                pl.BlockSpec((1, 1, chunk, width), lambda m, k, i: (k, m, 0, 0)),
                pl.BlockSpec((1, 2 * rows), lambda m, k, i: (0, 0)),
                pl.BlockSpec((1, 1, 2 * rows), lambda m, k, i: (m, 0, 0)),
                pl.BlockSpec((chunk, 1), lambda m, k, i: (0, 0)),
                pl.BlockSpec(e4.shape, lambda m, k, i: (0, 0)),
            ],
            out_specs=[
                pl.BlockSpec((1, rows, 4 * LANES), lambda m, k, i: (m, 0, 0)),
                pl.BlockSpec((1, rows, 4 * DH), lambda m, k, i: (m, 0, 0)),
                pl.BlockSpec((1, 2, 1, 2 * rows), lambda m, k, i: (m, 0, 0, 0)),
            ],
            scratch_shapes=[pltpu.VMEM((2, 1, 2 * rows), f32), pltpu.VMEM((2, LANES, 2 * rows), f32)],
        ),
        out_shape=[
            jax.ShapeDtypeStruct((micro, rows, 4 * LANES), f32),
            jax.ShapeDtypeStruct((micro, rows, 4 * DH), bf16),
            jax.ShapeDtypeStruct((micro, 2, 1, 2 * rows), f32),
        ],
        compiler_params=pltpu.CompilerParams(vmem_limit_bytes=VMEM_BYTES),
        cost_estimate=pl.CostEstimate(
            flops=micro * chunks * 16 * rows * chunk * LANES,
            bytes_accessed=4 * micro * rows * 4 * LANES + 2 * kv.size,
            transcendentals=micro * chunks * 4 * rows * chunk,
        ),
        name="attend",
    )(info, q, kv, qpos, qbeg, kpos, e4)


def attend_back_kernel(
    info_ref, q_ref, kv_ref, g_ref, att_ref, lse_ref, qpos_ref, qbeg_ref, kpos_ref, cos_ref, sin_ref, cosk_ref,
    sink_ref, e_ref, dq_ref, dkv_ref, delta_s, go_s, dq_s,
):
    m, k, last = pl.program_id(0), pl.program_id(1), pl.num_programs(1) - 1
    chunk = kv_ref.shape[2]
    useful = useful_of(info_ref, m, k, chunk)

    @pl.when(k == 0)
    def _():
        dq_s[...] = jnp.zeros(dq_s.shape, f32)
        go = dot(g_ref[0], e_ref[...])
        for h in range(2):
            go_h = stack_heads(go, h)
            go_s[h] = go_h.astype(bf16)
            prod = go_h * stack_heads(att_ref[0], h)
            delta_s[h] = jnp.sum(prod.T, axis=0, keepdims=True)

    @pl.when(useful)
    def _():
        allowed = allowed_of(info_ref, k, chunk, qpos_ref, qbeg_ref, kpos_ref)
        kv = kv_ref[0, 0]
        q = q_ref[0]
        cosk, sink = cosk_ref[0, 0], sink_ref[0, 0]
        grad_keys, grad_vals = [], []
        for h in range(2):
            keys = dot(kv, e_ref[:, h * LANES : (h + 1) * LANES]).astype(bf16)
            vals = dot(kv, e_ref[:, (2 + h) * LANES : (3 + h) * LANES]).astype(bf16)
            q_h = stack_heads(q, h)
            go_h = go_s[h]
            s = dot_nt(keys, q_h)
            w = jnp.where(allowed, jnp.exp2(s * exp2_scale - lse_ref[0, h]), 0.0)
            grad_vals.append(dot(w.astype(bf16), go_h).astype(bf16))
            ds = (w * (dot_nt(vals, go_h) - delta_s[h])).astype(bf16)
            dq_s[h] = dq_s[h] + dot_tn(keys, ds)
            gk = dot(ds, q_h) * score_scale
            gk = gk * cosk + pltpu.roll(gk * sink, LANES // 2, 1)
            grad_keys.append(gk.astype(bf16))
        dkv_ref[0, 0] = dot_nt(jnp.concatenate(grad_keys + grad_vals, axis=1), e_ref[...]).astype(bf16)

    @pl.when(jnp.logical_not(useful))
    def _():
        dkv_ref[...] = jnp.zeros(dkv_ref.shape, bf16)

    @pl.when(k == last)
    def _():
        cos, sin = cos_ref[0, 0], sin_ref[0, 0]
        parts = []
        for h in range(2):
            flat = dq_s[h].T * score_scale
            rows = flat.shape[0] // 2
            for piece in (flat[:rows], flat[rows:]):
                parts.append((piece * cos + pltpu.roll(piece * sin, LANES // 2, 1)).astype(bf16))
        dq_ref[0] = dot_nt(jnp.concatenate(parts, axis=1), e_ref[...]).astype(bf16)


def attend_back(info, q, kv, g, att, lse, qpos, qbeg, kpos, cos, sin, e4):
    micro, rows, _ = q.shape
    chunks, _, chunk, width = kv.shape
    per_micro = lambda c: pl.BlockSpec((1, rows, c), lambda m, k, i: (m, 0, 0))
    return pl.pallas_call(
        attend_back_kernel,
        grid_spec=pltpu.PrefetchScalarGridSpec(
            num_scalar_prefetch=1,
            grid=(micro, chunks),
            in_specs=[
                per_micro(4 * LANES),
                pl.BlockSpec((1, 1, chunk, width), lambda m, k, i: (k, m, 0, 0)),
                per_micro(4 * DH),
                per_micro(4 * LANES),
                pl.BlockSpec((1, 2, 1, 2 * rows), lambda m, k, i: (m, 0, 0, 0)),
                pl.BlockSpec((1, 2 * rows), lambda m, k, i: (0, 0)),
                pl.BlockSpec((1, 1, 2 * rows), lambda m, k, i: (m, 0, 0)),
                pl.BlockSpec((chunk, 1), lambda m, k, i: (0, 0)),
                pl.BlockSpec((1, 1, chunk, LANES), lambda m, k, i: (0, m, 0, 0)),
                pl.BlockSpec((1, 1, chunk, LANES), lambda m, k, i: (0, m, 0, 0)),
                pl.BlockSpec((1, 1, chunk, LANES), lambda m, k, i: (k, m, 0, 0)),
                pl.BlockSpec((1, 1, chunk, LANES), lambda m, k, i: (k, m, 0, 0)),
                pl.BlockSpec(e4.shape, lambda m, k, i: (0, 0)),
            ],
            out_specs=[
                per_micro(4 * DH),
                pl.BlockSpec((1, 1, chunk, width), lambda m, k, i: (k, m, 0, 0)),
            ],
            scratch_shapes=[
                pltpu.VMEM((2, 1, 2 * rows), f32),
                pltpu.VMEM((2, 2 * rows, LANES), bf16),
                pltpu.VMEM((2, LANES, 2 * rows), f32),
            ],
        ),
        out_shape=[
            jax.ShapeDtypeStruct((micro, rows, 4 * DH), bf16),
            jax.ShapeDtypeStruct(kv.shape, bf16),
        ],
        compiler_params=pltpu.CompilerParams(vmem_limit_bytes=VMEM_BYTES),
        cost_estimate=pl.CostEstimate(
            flops=micro * chunks * 40 * rows * chunk * LANES,
            bytes_accessed=8 * micro * rows * 4 * LANES + 4 * kv.size,
            transcendentals=micro * chunks * 4 * rows * chunk,
        ),
        name="attend_back",
    )(info, q, kv, g, att, lse, qpos, qbeg, kpos, cos, sin, cos, sin, e4)


def beside(value, bit):
    return lax.ppermute(value, "plane", [(i, i ^ bit) for i in range(PLANE)])


def other_core(value):
    return lax.ppermute(value, "stream", [(0, 1), (1, 0)])


def along(value, step, wrap):
    size = lax.axis_size("zed")
    pairs = [(i, (i + step) % size) for i in range(size) if wrap or 0 <= i + step < size]
    return lax.ppermute(value, "zed", pairs)


def plane_gather(own):
    first, second = own[0], own[1]
    first = jnp.stack([first, beside(first, 1)])
    second = jnp.stack([second, beside(second, 2)])
    first_more, second_more = beside(first, 2), beside(second, 1)
    return jnp.stack(
        [
            jnp.concatenate([first, first_more]),
            jnp.stack([second[0], second_more[0], second[1], second_more[1]]),
        ]
    )


def plane_sum(terms):
    first, second = terms[0], terms[1]
    got_first = beside(jnp.stack([first[1], first[3]]).astype(bf16), 1)
    got_second = beside(second[2:4].astype(bf16), 2)
    more_first = beside((first[2] + got_first[1]).astype(bf16), 2)
    more_second = beside((second[1] + got_second[1]).astype(bf16), 1)
    return jnp.stack([first[0] + got_first[0] + more_first, second[0] + got_second[0] + more_second])


def after(value, *earlier):
    return lax.optimization_barrier((value,) + earlier)[0]


def weight_gather(blocks):
    size = lax.axis_size("zed")
    s, z = lax.axis_index("stream"), lax.axis_index("zed")
    fulls = [jnp.zeros((2 * size,) + block.shape, block.dtype) for block in blocks]
    for k in range(size):
        place = lax.rem(z - k + size, size)
        for i, block in enumerate(blocks):
            full = lax.dynamic_update_slice(fulls[i], block[None], (s * size + place, 0, 0))
            fulls[i] = lax.dynamic_update_slice(full, other_core(block)[None], ((1 - s) * size + place, 0, 0))
        if k < size - 1:
            blocks = lax.optimization_barrier([along(block, 1, True) for block in blocks])
    return [full.reshape((-1,) + full.shape[2:]) for full in fulls], blocks[0]


def core_scatter(fulls, kinds):
    size = lax.axis_size("zed")
    s = lax.axis_index("stream")
    halves = []
    for full, kind in zip(fulls, kinds):
        full = full.reshape((2, size, -1) + full.shape[1:])
        mine = lax.dynamic_index_in_dim(full, s, 0, keepdims=False)
        theirs = lax.dynamic_index_in_dim(full, 1 - s, 0, keepdims=False)
        halves.append((mine.astype(f32) + other_core(theirs).astype(f32)).astype(kind))
    return lax.optimization_barrier(halves)


def ring_scatter(halves, totals, k):
    size = lax.axis_size("zed")
    z = lax.axis_index("zed")
    new = []
    for i, half in enumerate(halves):
        own = lax.dynamic_index_in_dim(half, lax.rem(z - k + size, size), 0, keepdims=False).astype(f32)
        if totals is not None:
            own = along(totals[i], -1, True).astype(f32) + own
        new.append(own if k == 0 else own.astype(half.dtype))
    return lax.optimization_barrier(new)


def plane_swap(value, split, concat):
    return lax.all_to_all(value, "plane", split_axis=split, concat_axis=concat, tiled=True)


def on_device(inputs, cotangent, seq_lengths, gain_attn, gain_ffn, w_query, w_key, w_value, w_out, w_gate, w_up, w_down):
    size = lax.axis_size("zed")
    z, p = lax.axis_index("zed"), lax.axis_index("plane")
    micro, _, tok_rows, width = inputs.shape
    chunk = PLANE * tok_rows
    tokens = micro * chunk
    shard_rows = w_query.shape[0]
    ff_block = w_down.shape[0]
    ff_blocks = 2 * size
    ff_part = ff_blocks * ff_block
    q_part, kv_part = HQ * DH // PLANE, HK * DH // PLANE
    out_part = width // PLANE
    e4, e8 = spread(4), spread(8)

    def by_part(weight):
        return weight.reshape(shard_rows, PLANE, -1)

    def by_ff_part(weight):
        return weight.reshape(shard_rows, ff_blocks, PLANE, ff_block).transpose(0, 2, 1, 3).reshape(shard_rows, PLANE, -1)

    own_in = inputs[:, 0]
    own_cot = cotangent[:, 0]
    qkv_bundle = jnp.concatenate([by_part(w_query), by_part(w_key), by_part(w_value)], axis=2).reshape(shard_rows, -1)
    qkv_block = plane_swap(qkv_bundle, 1, 0)
    gains = jnp.stack([gain_attn, gain_ffn])
    gains_one = jnp.stack([gains, beside(gains, 1)])
    gains_all = jnp.concatenate([gains_one, beside(gains_one, 2)])
    gains_all = jnp.take(gains_all, jnp.arange(PLANE) ^ p, axis=0)
    (full_qkv, full_gains), qkv_there = weight_gather([qkv_block, gains_all.reshape(PLANE, 2 * shard_rows)])
    full_gains = full_gains.reshape(-1, 2, shard_rows).transpose(1, 0, 2).reshape(2, width).astype(f32)
    gain_one, gain_two = full_gains[0:1], full_gains[1:2]
    ffn_bundle = jnp.concatenate([by_ff_part(w_gate), by_ff_part(w_up), by_part(w_out)], axis=2).reshape(shard_rows, -1)
    ffn_block = plane_swap(after(ffn_bundle, qkv_block), 1, 0)
    gathered_in = plane_gather(after(own_in, qkv_block)).reshape(tokens, width)
    (full_oc,), out_there = weight_gather([after(ffn_block[:, 2 * ff_part :], qkv_there)])
    full_out = plane_swap(full_oc, 0, 1)
    gathered_cot = plane_gather(after(own_cot, gathered_in)).reshape(tokens, width)

    slot_place = ((jnp.arange(PLANE, dtype=jnp.int32) ^ p)[:, None] * tok_rows + jnp.arange(tok_rows, dtype=jnp.int32)[None, :]).reshape(chunk)
    chunk_place = (z - jnp.arange(size, dtype=jnp.int32))[:, None] * chunk + slot_place[None, :]
    lengths = seq_lengths[:, 0]
    seq_ends = jnp.cumsum(lengths, axis=1)
    begins = jnp.sum(
        jnp.where(seq_ends[:, None, None, :] <= chunk_place[None, :, :, None], lengths[:, None, None, :], 0), axis=-1
    )
    own_begin = begins[:, 0]
    lane = np.arange(LANES)
    place_in_half = lane % (LANES // 2)
    real = place_in_half < DH // 2
    frequency = jnp.where(
        real, rope_base ** (-2.0 * jnp.asarray(np.minimum(place_in_half, DH // 2 - 1), f32) / DH), 0.0
    )
    rope_place = (chunk_place[None] - begins).astype(f32)
    angles = jnp.maximum(rope_place, 0.0).transpose(1, 0, 2)[..., None] * frequency
    cos = jnp.where(real, jnp.cos(angles), 0.0)
    sin = jnp.sin(angles) * jnp.asarray(np.where(real, np.where(lane < LANES // 2, -1.0, 1.0), 0.0), f32)
    info = jnp.concatenate([jnp.reshape(z, (1,)).astype(jnp.int32), jnp.min(own_begin, axis=1)])
    qpos = jnp.tile(chunk_place[0], 2)[None]
    qbeg = jnp.tile(own_begin, (1, 2))[:, None]
    kpos = slot_place[:, None]

    w_pad = dot(full_qkv, e8).astype(bf16)
    normed_one, q_rot, kv_own = project(
        gathered_in, gain_one, w_pad, cos[0].reshape(tokens, LANES), sin[0].reshape(tokens, LANES), e4
    )
    q_rot = q_rot.reshape(micro, chunk, 4 * LANES)
    kv_piece = after(kv_own.reshape(micro, chunk, 4 * DH), out_there)
    kv_pieces = [kv_piece]
    for _ in range(size - 1):
        kv_piece = along(kv_piece, 1, False)
        kv_pieces.append(kv_piece)
    kv_all = jnp.stack(kv_pieces)
    gu_block, down_block = lax.optimization_barrier((ffn_block[:, : 2 * ff_part], w_down, kv_piece))[:2]
    (full_gu, full_down), _ = weight_gather([gu_block, down_block])
    attended, attn_low, lse = attend(info, q_rot, kv_all, qpos, qbeg, kpos, e4)
    attn_low = attn_low.reshape(tokens, q_part)
    branch = plane_sum(dot(attn_low, full_out).reshape(micro, PLANE, tok_rows, width))
    layer_in = own_in.astype(f32)
    middle = layer_in + branch

    scale_two = rms_scale(middle)
    normed_two = plane_gather((middle * scale_two * gain_two).astype(bf16)).reshape(tokens, width)
    pre = dot(normed_two, full_gu)
    gate_pre, up_pre = pre[:, :ff_part], pre[:, ff_part:]
    sigmoid_gate = jax.nn.sigmoid(gate_pre)
    silu_gate = gate_pre * sigmoid_gate
    hidden = (silu_gate * up_pre).astype(bf16)
    grad_hidden = dot_nt(gathered_cot, full_down)
    grad_gate = (grad_hidden * up_pre * sigmoid_gate * (1.0 + gate_pre * (1.0 - sigmoid_gate))).astype(bf16)
    grad_up = (grad_hidden * silu_gate).astype(bf16)
    grad_gu = jnp.concatenate([grad_gate, grad_up], axis=1)
    grad_normed_two = plane_sum(dot_nt(grad_gu, full_gu).reshape(micro, PLANE, tok_rows, width))
    term_gu = dot_tn(normed_two, grad_gu).astype(bf16)
    term_down = dot_tn(hidden, gathered_cot).astype(bf16)
    ffn_halves = core_scatter([term_gu, term_down], [bf16, bf16])
    ffn_totals = ring_scatter(ffn_halves, None, size - 1)
    result_terms = dot(hidden, full_down)

    grad_y = own_cot.astype(f32)
    grad_gain_two = jnp.sum(grad_normed_two * middle * scale_two, axis=(0, 1))
    weighted = grad_normed_two * gain_two
    grad_middle = (
        grad_y
        + scale_two * weighted
        - middle * scale_two**3 * jnp.mean(middle * weighted, axis=-1, keepdims=True)
    )
    grad_branch = plane_gather(grad_middle.astype(bf16)).reshape(tokens, width)
    term_out = plane_swap(dot_tn(attn_low, grad_branch).astype(bf16), 1, 0)
    ffn_totals = ring_scatter(ffn_halves, ffn_totals, size - 2)
    grad_attn = after(dot_nt(grad_branch, full_out).astype(bf16), ffn_totals[0]).reshape(micro, chunk, q_part)

    grad_query, grad_kv = attend_back(info, q_rot, kv_all, grad_attn, attended, lse, qpos, qbeg, kpos, cos, sin, e4)
    result_terms = after(result_terms, grad_query)
    result = middle + plane_sum(result_terms.reshape(micro, PLANE, tok_rows, width))
    output = result.astype(bf16)
    own_kv = grad_kv[size - 1]
    for k in range(size - 2, -1, -1):
        if k > 0:
            ffn_totals = ring_scatter(ffn_halves, ffn_totals, k - 1)
            own_kv = after(own_kv, ffn_totals[0])
        own_kv = along(own_kv, -1, False).astype(f32) + grad_kv[k].astype(f32)
        own_kv = own_kv.astype(bf16)
    sum_gu, sum_down = ffn_totals
    grad_qkv = jnp.concatenate([grad_query.reshape(tokens, q_part), own_kv.astype(bf16).reshape(tokens, 2 * kv_part)], axis=1)
    grad_normed_part = dot_nt(grad_qkv, full_qkv)
    full_in = gathered_in.astype(f32)
    grad_gain_one = jnp.sum(grad_normed_part * full_in * rms_scale(full_in), axis=0)
    grad_normed_one = plane_sum(grad_normed_part.reshape(micro, PLANE, tok_rows, width))
    term_qkv = dot_tn(normed_one, grad_qkv).astype(bf16)
    scale_one = rms_scale(layer_in)
    weighted = grad_normed_one * gain_one
    input_grad = (
        grad_middle
        + scale_one * weighted
        - layer_in * scale_one**3 * jnp.mean(layer_in * weighted, axis=-1, keepdims=True)
    )

    def from_ff_parts(term):
        return term.reshape(shard_rows, PLANE, ff_blocks, ff_block).transpose(0, 2, 1, 3).reshape(shard_rows, -1)

    sum_gu = plane_swap(sum_gu.astype(bf16), 0, 1).astype(f32).reshape(shard_rows, PLANE, 2, ff_part)
    gain_terms = jnp.stack([grad_gain_one, grad_gain_two]).reshape(2, ff_blocks, PLANE, shard_rows).transpose(1, 2, 0, 3)
    gain_terms = gain_terms.reshape(ff_blocks * PLANE, 2 * shard_rows)
    last_halves = core_scatter([term_qkv, term_out, gain_terms], [bf16, bf16, f32])
    last_totals = None
    for k in range(size - 1, -1, -1):
        last_totals = ring_scatter(last_halves, last_totals, k)
    sum_qkv, sum_out, gain_sum = last_totals
    sum_qkv, sum_out = lax.optimization_barrier((sum_qkv.astype(bf16), sum_out.astype(bf16)))
    sum_qkv = plane_swap(jnp.concatenate([sum_qkv, sum_out], axis=1), 0, 1).astype(f32).reshape(shard_rows, PLANE, -1)
    for bit in (1, 2):
        gain_sum = gain_sum + beside(gain_sum, bit)
    gain_own = lax.dynamic_index_in_dim(gain_sum, p, 0, keepdims=False).reshape(2, shard_rows)
    return (
        output[:, None],
        input_grad[:, None],
        gain_own[0],
        gain_own[1],
        sum_qkv[:, :, :q_part].reshape(shard_rows, -1),
        sum_qkv[:, :, q_part : q_part + kv_part].reshape(shard_rows, -1),
        sum_qkv[:, :, q_part + kv_part : q_part + 2 * kv_part].reshape(shard_rows, -1),
        sum_qkv[:, :, q_part + 2 * kv_part :].reshape(shard_rows, -1),
        from_ff_parts(sum_gu[:, :, 0]),
        from_ff_parts(sum_gu[:, :, 1]),
        sum_down,
    )


def solution(mesh):
    blocks = mesh.shape["blk"]
    grid = Mesh(mesh.devices.reshape(2, blocks // PLANE, PLANE), ("stream", "zed", "plane"))
    tokens = P(None, "stream", ("zed", "plane"), None)
    vector = P(("stream", "zed", "plane"))
    matrix = P(("stream", "zed", "plane"), None)
    return jax.shard_map(
        on_device,
        mesh=grid,
        in_specs=(tokens, tokens, P(None, "stream", None), vector, vector) + (matrix,) * 7,
        out_specs=(tokens, tokens, vector, vector) + (matrix,) * 7,
        check_vma=False,
    )
```

```python
import math

import jax
import jax.numpy as jnp
import numpy as np
from jax import lax
from jax.experimental import pallas as pl
from jax.experimental.pallas import tpu as pltpu
from jax.sharding import Mesh
from jax.sharding import PartitionSpec as P

HQ = 16
HK = 8
DH = 96
PLANE = 4
LANES = 128
VMEM_BYTES = 50 * 1024 * 1024

epsilon = 1e-05
rope_base = 100000.0
masked_score = -1e30
score_scale = 1.0 / math.sqrt(DH)
exp2_scale = score_scale * math.log2(math.e)

f32 = jnp.float32
bf16 = jnp.bfloat16


def spread(heads):
    table = np.zeros((heads * DH, heads * LANES), np.float32)
    for head in range(heads):
        for i in range(DH):
            lane = i if i < DH // 2 else i + (LANES - DH) // 2
            table[head * DH + i, head * LANES + lane] = 1.0
    return jnp.asarray(table, bf16)


def rms_scale(values):
    return lax.rsqrt(jnp.mean(values * values, axis=-1, keepdims=True) + epsilon)


def dot(a, b):
    return jnp.dot(a, b, preferred_element_type=f32)


def dot_nt(a, b):
    return lax.dot_general(a, b, (((1,), (1,)), ((), ())), preferred_element_type=f32)


def dot_tn(a, b):
    return lax.dot_general(a, b, (((0,), (0,)), ((), ())), preferred_element_type=f32)


def project_kernel(size, info_ref, x_ref, cos_ref, sin_ref, e4_ref, e8_ref, *rest):
    blocks, (n_ref, q_ref, kv_ref, w_ref, out_w_ref, gains_ref, pad_s) = rest[: 2 * size], rest[2 * size :]
    rows = blocks[0].shape[0]
    heads = 8 * DH

    @pl.when(pl.program_id(0) == 0)
    def _():
        for i, block in enumerate(blocks):
            core = info_ref[1] if i < size else 1 - info_ref[1]
            start = pl.multiple_of((core * size + lax.rem(info_ref[0] - i % size + size, size)) * rows, rows)
            w_ref[pl.ds(start, rows), :] = block[:, : heads + LANES]
            out_w_ref[pl.ds(start, rows), :] = block[:, heads + LANES :]
            pad_s[pl.ds(start, rows), :] = dot(block[:, :heads], e8_ref[...]).astype(bf16)
        rows_to = lax.broadcasted_iota(jnp.int32, (LANES, LANES), 0)
        same = (rows_to == lax.broadcasted_iota(jnp.int32, (LANES, LANES), 1)).astype(bf16)
        gains_ref[...] = dot_nt(same[:8], w_ref[:, heads:])

    x = x_ref[...].astype(f32)
    normed = (x * rms_scale(x) * gains_ref[0:1, :]).astype(bf16)
    n_ref[...] = normed
    pre = dot(normed, pad_s[...])
    cos, sin = cos_ref[...], sin_ref[...]
    parts = []
    for head in range(8):
        piece = pre[:, head * LANES : (head + 1) * LANES]
        if head < 6:
            piece = piece * cos + pltpu.roll(piece, LANES // 2, 1) * sin
        parts.append(piece.astype(bf16))
    q_ref[...] = jnp.concatenate(parts[:4], axis=1)
    kv_ref[...] = dot_nt(jnp.concatenate(parts[4:], axis=1), e4_ref[...]).astype(bf16)


def project(info, x, blocks, cos, sin, e4, e8):
    rows, width = x.shape
    step = min(256, rows)
    size = len(blocks) // 2
    cols = blocks[0].shape[1]
    first = 8 * DH + LANES
    whole = lambda a: pl.BlockSpec(a.shape, lambda i, n: (0,) * a.ndim)
    by_row = lambda c: pl.BlockSpec((step, c), lambda i, n: (i, 0))
    return pl.pallas_call(
        lambda *refs: project_kernel(size, *refs),
        grid_spec=pltpu.PrefetchScalarGridSpec(
            num_scalar_prefetch=1,
            grid=(rows // step,),
            in_specs=[by_row(width), by_row(LANES), by_row(LANES), whole(e4), whole(e8)] + [whole(b) for b in blocks],
            out_specs=[
                by_row(width),
                by_row(4 * LANES),
                by_row(4 * DH),
                pl.BlockSpec((width, first), lambda i, n: (0, 0)),
                pl.BlockSpec((width, cols - first), lambda i, n: (0, 0)),
                pl.BlockSpec((8, width), lambda i, n: (0, 0)),
            ],
            scratch_shapes=[pltpu.VMEM((width, 8 * LANES), bf16)],
        ),
        out_shape=[
            jax.ShapeDtypeStruct((rows, width), bf16),
            jax.ShapeDtypeStruct((rows, 4 * LANES), bf16),
            jax.ShapeDtypeStruct((rows, 4 * DH), bf16),
            jax.ShapeDtypeStruct((width, first), bf16),
            jax.ShapeDtypeStruct((width, cols - first), bf16),
            jax.ShapeDtypeStruct((8, width), f32),
        ],
        compiler_params=pltpu.CompilerParams(vmem_limit_bytes=VMEM_BYTES),
        cost_estimate=pl.CostEstimate(
            flops=2 * rows * width * 8 * LANES, bytes_accessed=2 * (2 * rows * width + 2 * width * cols), transcendentals=0
        ),
        name="project",
    )(info, x, cos, sin, e4, e8, *blocks)


def assemble_kernel(size, info_ref, *rest):
    blocks, out_ref = rest[: 2 * size], rest[2 * size]
    rows = blocks[0].shape[0]
    for i, block in enumerate(blocks):
        core = info_ref[1] if i < size else 1 - info_ref[1]
        start = pl.multiple_of((core * size + lax.rem(info_ref[0] - i % size + size, size)) * rows, rows)
        out_ref[pl.ds(start, rows), :] = block[...]


def assemble(info, blocks):
    size = len(blocks) // 2
    rows, width = blocks[0].shape
    step = width // 3 if width % 384 == 0 else width // 4
    return pl.pallas_call(
        lambda *refs: assemble_kernel(size, *refs),
        grid_spec=pltpu.PrefetchScalarGridSpec(
            num_scalar_prefetch=1,
            grid=(width // step,),
            in_specs=[pl.BlockSpec((rows, step), lambda i, n: (0, i)) for _ in blocks],
            out_specs=pl.BlockSpec((len(blocks) * rows, step), lambda i, n: (0, i)),
        ),
        out_shape=jax.ShapeDtypeStruct((len(blocks) * rows, width), blocks[0].dtype),
        compiler_params=pltpu.CompilerParams(vmem_limit_bytes=VMEM_BYTES),
        cost_estimate=pl.CostEstimate(flops=0, bytes_accessed=4 * len(blocks) * rows * width, transcendentals=0),
        name="assemble",
    )(info, *blocks)


def allowed_of(info_ref, k, chunk, qpos_ref, qbeg_ref, kpos_ref):
    kpos = kpos_ref[...] + (info_ref[0] - k) * chunk
    return (kpos <= qpos_ref[...]) & (kpos >= qbeg_ref[...])


def useful_of(info_ref, m, k, chunk):
    z = info_ref[0]
    return (k <= z) & ((z - k + 1) * chunk - 1 >= info_ref[2 + m])


def stack_heads(block, h):
    return jnp.concatenate(
        [block[:, (2 * h) * LANES : (2 * h + 1) * LANES], block[:, (2 * h + 1) * LANES : (2 * h + 2) * LANES]], axis=0
    )


def run_kernel(body, info, inputs, outs, aliases, flops, transcendentals, name):
    whole = lambda shape: pl.BlockSpec(shape, lambda i, n: (0,) * len(shape))
    moved = sum(a.size * a.dtype.itemsize for a in inputs) + sum(math.prod(o.shape) * o.dtype.itemsize for o in outs)
    return list(
        pl.pallas_call(
        body,
        grid_spec=pltpu.PrefetchScalarGridSpec(
            num_scalar_prefetch=1,
            grid=(1,),
            in_specs=[whole(a.shape) for a in inputs],
            out_specs=[whole(o.shape) for o in outs],
        ),
        out_shape=outs,
        input_output_aliases=aliases,
        compiler_params=pltpu.CompilerParams(vmem_limit_bytes=VMEM_BYTES),
        cost_estimate=pl.CostEstimate(flops=flops, bytes_accessed=moved, transcendentals=transcendentals),
        name=name,
    )(info, *inputs)
    )


def attend_kernel(m, k, last, info_ref, q_ref, kv_ref, qpos_ref, qbeg_ref, kpos_ref, e_ref, *rest):
    chunk = kv_ref.shape[0]
    if k > 0:
        top_in, acc_in, rest = rest[0], rest[1], rest[2:]
    top_ref, acc_ref = rest[0], rest[1]

    def run():
        allowed = allowed_of(info_ref, k, chunk, qpos_ref, qbeg_ref, kpos_ref)
        kv = kv_ref[...]
        q = q_ref[...]
        one_lane = (lax.broadcasted_iota(jnp.int32, (1, LANES), 1) == DH // 2).astype(f32)
        for h in range(2):
            keys = dot(kv, e_ref[:, h * LANES : (h + 1) * LANES]).astype(bf16)
            vals = (dot(kv, e_ref[:, (2 + h) * LANES : (3 + h) * LANES]) + one_lane).astype(bf16)
            s = jnp.where(allowed, dot_nt(keys, stack_heads(q, h)), masked_score)
            new = jnp.max(s, axis=0, keepdims=True)
            if k > 0:
                old = top_in[h]
                new = jnp.maximum(old, new)
            w = jnp.where(allowed, jnp.exp2((s - new) * exp2_scale), 0.0).astype(bf16)
            acc = dot_tn(vals, w)
            if k > 0:
                acc = acc_in[h] * jnp.exp2((old - new) * exp2_scale) + acc
            acc_ref[h] = acc
            top_ref[h] = new

    if k == 0:
        run()
    else:
        useful = useful_of(info_ref, m, k, chunk)
        pl.when(useful)(run)

        @pl.when(jnp.logical_not(useful))
        def _():
            top_ref[...] = top_in[...]
            acc_ref[...] = acc_in[...]

    if last:
        att_ref, low_ref, lse_ref = rest[2:]
        parts = []
        for h in range(2):
            acc = acc_ref[h]
            total = acc[DH // 2 : DH // 2 + 1, :]
            lse_ref[h] = top_ref[h] * exp2_scale + jnp.log2(total)
            flat = (acc / total).T
            rows = flat.shape[0] // 2
            parts += [flat[:rows], flat[rows:]]
        att = jnp.concatenate(parts, axis=1)
        att_ref[...] = att
        low_ref[...] = dot_nt(att.astype(bf16), e_ref[...]).astype(bf16)


def attend(m, k, last, info, q, kv, qpos, qbeg, kpos, e4, state):
    rows, chunk = q.shape[0], kv.shape[0]
    outs = [jax.ShapeDtypeStruct((2, 1, 2 * rows), f32), jax.ShapeDtypeStruct((2, LANES, 2 * rows), f32)]
    if last:
        outs += [
            jax.ShapeDtypeStruct((rows, 4 * LANES), f32),
            jax.ShapeDtypeStruct((rows, 4 * DH), bf16),
            jax.ShapeDtypeStruct((2, 1, 2 * rows), f32),
        ]
    return run_kernel(
        lambda *refs: attend_kernel(m, k, last, *refs),
        info,
        [q, kv, qpos, qbeg, kpos, e4] + state,
        outs,
        {7: 0, 8: 1} if k > 0 else {},
        16 * rows * chunk * LANES,
        4 * rows * chunk,
        "attend",
    )


def attend_back_kernel(
    m, k, first, last, info_ref, q_ref, kv_ref, lse_ref, qpos_ref, qbeg_ref, kpos_ref, cosk_ref, sink_ref, e_ref, *rest
):
    chunk = kv_ref.shape[0]
    if first:
        g_ref, att_ref, rest = rest[0], rest[1], rest[2:]
        go_ref, delta_ref, dq_ref, dkv_ref = rest[:4]
        go = dot(g_ref[...], e_ref[...])
        for h in range(2):
            go_h = stack_heads(go, h)
            go_ref[h] = go_h.astype(bf16)
            prod = go_h * stack_heads(att_ref[...], h)
            delta_ref[h] = jnp.sum(prod.T, axis=0, keepdims=True)
    else:
        go_ref, delta_ref, dq_in, rest = rest[0], rest[1], rest[2], rest[3:]
        dq_ref, dkv_ref = rest[:2]

    def run():
        allowed = allowed_of(info_ref, k, chunk, qpos_ref, qbeg_ref, kpos_ref)
        kv = kv_ref[...]
        q = q_ref[...]
        cosk, sink = cosk_ref[...], sink_ref[...]
        grad_keys, grad_vals = [], []
        for h in range(2):
            keys = dot(kv, e_ref[:, h * LANES : (h + 1) * LANES]).astype(bf16)
            vals = dot(kv, e_ref[:, (2 + h) * LANES : (3 + h) * LANES]).astype(bf16)
            q_h = stack_heads(q, h)
            go_h = go_ref[h]
            s = dot_nt(keys, q_h)
            w = jnp.where(allowed, jnp.exp2(s * exp2_scale - lse_ref[h]), 0.0)
            grad_vals.append(dot(w.astype(bf16), go_h).astype(bf16))
            ds = (w * (dot_nt(vals, go_h) - delta_ref[h])).astype(bf16)
            dq = dot_tn(keys, ds)
            dq_ref[h] = dq if first else dq_in[h] + dq
            gk = dot(ds, q_h) * score_scale
            gk = gk * cosk + pltpu.roll(gk * sink, LANES // 2, 1)
            grad_keys.append(gk.astype(bf16))
        dkv_ref[...] = dot_nt(jnp.concatenate(grad_keys + grad_vals, axis=1), e_ref[...]).astype(bf16)

    if k == 0:
        run()
    else:
        useful = useful_of(info_ref, m, k, chunk)
        pl.when(useful)(run)

        @pl.when(jnp.logical_not(useful))
        def _():
            dkv_ref[...] = jnp.zeros(dkv_ref.shape, bf16)
            dq_ref[...] = jnp.zeros(dq_ref.shape, f32) if first else dq_in[...]

    if last:
        out_ref = rest[-1]
        parts = []
        for h in range(2):
            flat = dq_ref[h].T * score_scale
            rows = flat.shape[0] // 2
            for piece in (flat[:rows], flat[rows:]):
                parts.append((piece * cosk_ref[...] + pltpu.roll(piece * sink_ref[...], LANES // 2, 1)).astype(bf16))
        out_ref[...] = dot_nt(jnp.concatenate(parts, axis=1), e_ref[...]).astype(bf16)


def attend_back(m, k, first, last, info, q, kv, lse, qpos, qbeg, kpos, cosk, sink, e4, state):
    rows, chunk = q.shape[0], kv.shape[0]
    outs = []
    if first:
        outs += [jax.ShapeDtypeStruct((2, 2 * rows, LANES), bf16), jax.ShapeDtypeStruct((2, 1, 2 * rows), f32)]
    outs += [jax.ShapeDtypeStruct((2, LANES, 2 * rows), f32), jax.ShapeDtypeStruct(kv.shape, bf16)]
    if last:
        outs += [jax.ShapeDtypeStruct((rows, 4 * DH), bf16)]
    return run_kernel(
        lambda *refs: attend_back_kernel(m, k, first, last, *refs),
        info,
        [q, kv, lse, qpos, qbeg, kpos, cosk, sink, e4] + state,
        outs,
        {} if first else {12: 0},
        40 * rows * chunk * LANES,
        4 * rows * chunk,
        "attend_back",
    )


def beside(value, bit):
    return lax.ppermute(value, "plane", [(i, i ^ bit) for i in range(PLANE)])


def other_core(value):
    return lax.ppermute(value, "stream", [(0, 1), (1, 0)])


def along(value, step, wrap):
    size = lax.axis_size("zed")
    pairs = [(i, (i + step) % size) for i in range(size) if wrap or 0 <= i + step < size]
    return lax.ppermute(value, "zed", pairs)


def plane_gather_start(own):
    return [own[0], own[1], beside(own[0], 1), beside(own[1], 2)]


def plane_gather_more(first, second, first_got, second_got):
    pair_one, pair_two = jnp.stack([first, first_got]), jnp.stack([second, second_got])
    return [pair_one, pair_two, beside(pair_one, 2), beside(pair_two, 1)]


def plane_gather_end(pair_one, pair_two, first_more, second_more):
    blocks = [pair_one, first_more, pair_two[:1], second_more[:1], pair_two[1:], second_more[1:]]
    return jnp.concatenate(blocks).reshape(-1, pair_one.shape[-1])


def plane_sum_start(terms):
    got_first = beside(jnp.stack([terms[0, 1], terms[0, 3]]).astype(bf16), 1)
    got_second = beside(terms[1, 2:4].astype(bf16), 2)
    return [got_first, got_second]


def plane_sum_more(terms, got_first, got_second):
    first, second = terms[0], terms[1]
    more_first = beside((first[2] + got_first[1]).astype(bf16), 2)
    more_second = beside((second[1] + got_second[1]).astype(bf16), 1)
    return [got_first[0], got_second[0], more_first, more_second]


def plane_sum_end(terms, got_first, got_second, more_first, more_second):
    return jnp.stack([terms[0, 0] + got_first + more_first, terms[1, 0] + got_second + more_second])


def after(value, *earlier):
    return lax.optimization_barrier((value,) + earlier)[0]


def sync(*values):
    return list(lax.optimization_barrier(values))


def core_halves(full):
    size = lax.axis_size("zed")
    s = lax.axis_index("stream")
    full = full.reshape((2, size, -1) + full.shape[1:])
    mine = lax.dynamic_index_in_dim(full, s, 0, keepdims=False)
    theirs = lax.dynamic_index_in_dim(full, 1 - s, 0, keepdims=False)
    return mine, other_core(theirs)


def core_sum(mine, other):
    return (mine.astype(f32) + other.astype(f32)).astype(bf16)


def ring_part(half, k):
    size = lax.axis_size("zed")
    z = lax.axis_index("zed")
    return lax.dynamic_index_in_dim(half, lax.rem(z - k + size, size), 0, keepdims=False)


def ring_add(half, moved, k):
    return (moved.astype(f32) + ring_part(half, k).astype(f32)).astype(bf16)


def plane_swap(value, split, concat):
    return lax.all_to_all(value, "plane", split_axis=split, concat_axis=concat, tiled=True)


def on_device(inputs, cotangent, seq_lengths, gain_attn, gain_ffn, w_query, w_key, w_value, w_out, w_gate, w_up, w_down):
    size = lax.axis_size("zed")
    s, z, p = lax.axis_index("stream"), lax.axis_index("zed"), lax.axis_index("plane")
    micro, _, tok_rows, width = inputs.shape
    chunk = PLANE * tok_rows
    tokens = micro * chunk
    shard_rows = w_query.shape[0]
    ff_block = w_down.shape[0]
    ff_blocks = 2 * size
    ff_part = ff_blocks * ff_block
    q_part, kv_part = HQ * DH // PLANE, HK * DH // PLANE
    out_part = width // PLANE
    e4, e8 = spread(4), spread(8)

    def by_part(weight):
        return weight.reshape(shard_rows, PLANE, -1)

    def by_ff_part(weight):
        return weight.reshape(shard_rows, ff_blocks, PLANE, ff_block).transpose(0, 2, 1, 3).reshape(shard_rows, PLANE, -1)

    def from_ff_parts(term):
        return term.reshape(shard_rows, PLANE, ff_blocks, ff_block).transpose(0, 2, 1, 3).reshape(shard_rows, -1)

    own_in = inputs[:, 0]
    own_cot = cotangent[:, 0]
    gains = jnp.stack([gain_attn, gain_ffn], axis=1)
    gains = jnp.broadcast_to(jnp.pad(gains, ((0, 0), (0, LANES - 2)))[:, None], (shard_rows, PLANE, LANES))
    qkv_bundle = jnp.concatenate([by_part(w_query), by_part(w_key), by_part(w_value), gains, by_part(w_out)], axis=2)
    qkv_block = plane_swap(qkv_bundle.reshape(shard_rows, -1), 1, 0)
    ffn_bundle = jnp.concatenate([by_ff_part(w_gate), by_ff_part(w_up)], axis=2).reshape(shard_rows, -1)
    qkv_blocks = [qkv_block]
    for _ in range(size - 1):
        qkv_blocks.append(along(qkv_blocks[-1], 1, True))
    qkv_other = [other_core(block) for block in qkv_blocks]
    ffn_block = plane_swap(after(ffn_bundle, qkv_block), 1, 0)
    pieces = sync(*plane_gather_start(after(own_in, qkv_block)))
    gathered_in = plane_gather_end(*sync(*plane_gather_more(*pieces)))
    gu_blocks = [after(ffn_block, qkv_blocks[-1])]
    gu_blocks.append(along(gu_blocks[0], 1, True))

    slot_place = ((jnp.arange(PLANE, dtype=jnp.int32) ^ p)[:, None] * tok_rows + jnp.arange(tok_rows, dtype=jnp.int32)[None, :]).reshape(chunk)
    chunk_place = (z - jnp.arange(size, dtype=jnp.int32))[:, None] * chunk + slot_place[None, :]
    lengths = seq_lengths[:, 0]
    seq_ends = jnp.cumsum(lengths, axis=1)
    begins = jnp.sum(
        jnp.where(seq_ends[:, None, None, :] <= chunk_place[None, :, :, None], lengths[:, None, None, :], 0), axis=-1
    )
    own_begin = begins[:, 0]
    lane = np.arange(LANES)
    place_in_half = lane % (LANES // 2)
    real = place_in_half < DH // 2
    frequency = jnp.where(
        real, rope_base ** (-2.0 * jnp.asarray(np.minimum(place_in_half, DH // 2 - 1), f32) / DH), 0.0
    )
    rope_place = (chunk_place[None] - begins).astype(f32)

    def tables(place):
        angles = jnp.maximum(place, 0.0)[..., None] * frequency
        signs = jnp.asarray(np.where(real, np.where(lane < LANES // 2, -1.0, 1.0), 0.0), f32)
        return jnp.where(real, jnp.cos(angles), 0.0), jnp.sin(angles) * signs

    cos, sin = tables(after(rope_place[:, 0], qkv_block))
    index = jnp.stack([z, s]).astype(jnp.int32)
    info = jnp.concatenate([index, jnp.min(own_begin, axis=1)])
    qpos = jnp.tile(chunk_place[0], 2)[None]
    qbeg = jnp.tile(own_begin, (1, 2))[:, None]
    kpos = slot_place[:, None]

    normed_one, q_rot, kv_own, full_qkv, full_oc, full_gains = project(
        index, gathered_in, qkv_blocks + qkv_other, cos.reshape(tokens, LANES), sin.reshape(tokens, LANES), e4, e8
    )
    full_qkv = full_qkv[:, : q_part + 2 * kv_part]
    gain_one, gain_two = full_gains[0:1], full_gains[1:2]
    q_rot = q_rot.reshape(micro, chunk, 4 * LANES)
    full_out = plane_swap(full_oc, 0, 1)
    cot_pieces = plane_gather_start(after(own_cot, gathered_in, kv_own))
    kv_pieces = [[piece] for piece in kv_own.reshape(micro, chunk, 4 * DH)]
    states = [[] for _ in range(micro)]
    for k in range(size):
        if k < size - 1:
            arrived = [along(kv_pieces[m][k], 1, False) for m in range(micro)]
            if k == 0:
                *cot_pieces, arrived[0], arrived[1], gu_blocks[1] = sync(*cot_pieces, *arrived, gu_blocks[1])
                cot_pieces = plane_gather_more(*cot_pieces)
            elif k == 1:
                *cot_pieces, arrived[0], arrived[1], full_out = sync(*cot_pieces, *arrived, full_out)
            else:
                arrived = sync(*arrived)
        for m in range(micro):
            states[m] = attend(m, k, k == size - 1, info, q_rot[m], kv_pieces[m][k], qpos, qbeg[m], kpos, e4, states[m])
            if k < size - 1:
                kv_pieces[m].append(arrived[m])
    kv_there = [pieces[-1] for pieces in kv_pieces]
    attended, lse = [state[2] for state in states], [state[4] for state in states]
    attn_low = jnp.concatenate([state[3] for state in states], axis=0)
    gathered_cot = plane_gather_end(*cot_pieces)

    gu_blocks[1], down_block, rope_place = sync(gu_blocks[1], w_down, rope_place, *kv_there)[:3]
    down_blocks = [down_block]
    branch_terms = dot(attn_low, full_out).reshape(micro, PLANE, tok_rows, width)
    gu_blocks.append(along(gu_blocks[1], 1, True))
    *got, gu_blocks[2] = sync(*plane_sum_start(branch_terms), gu_blocks[2])
    down_blocks.append(along(after(down_blocks[0], gu_blocks[2]), 1, True))
    cos_all, sin_all = tables(after(rope_place, gu_blocks[2]))
    *got, down_blocks[1], cos_all, sin_all = sync(*plane_sum_more(branch_terms, *got), down_blocks[1], cos_all, sin_all)
    layer_in = own_in.astype(f32)
    middle = layer_in + plane_sum_end(branch_terms, *got)
    scale_two = rms_scale(middle)
    pieces = plane_gather_start((middle * scale_two * gain_two).astype(bf16))
    down_blocks.append(along(down_blocks[1], 1, True))
    *pieces, down_blocks[2] = sync(*pieces, down_blocks[2])
    for k in range(2, size - 1):
        gu_blocks.append(along(after(gu_blocks[k], down_blocks[2]), 1, True))
    *pieces, gu_blocks[-1] = sync(*plane_gather_more(*pieces), gu_blocks[-1])
    for k in range(2, size - 1):
        down_blocks.append(along(after(down_blocks[k], gu_blocks[-1]), 1, True))
    full_gu = assemble(index, gu_blocks + [other_core(block) for block in gu_blocks])
    normed_two = plane_gather_end(*pieces)

    pre = dot(normed_two, full_gu)
    gate_pre, up_pre = pre[:, :ff_part], pre[:, ff_part:]
    full_down = assemble(index, down_blocks + [other_core(block) for block in down_blocks])
    sigmoid_gate = jax.nn.sigmoid(gate_pre)
    silu_gate = gate_pre * sigmoid_gate
    hidden = (silu_gate * up_pre).astype(bf16)
    grad_hidden = dot_nt(gathered_cot, full_down)
    grad_gate = (grad_hidden * up_pre * sigmoid_gate * (1.0 + gate_pre * (1.0 - sigmoid_gate))).astype(bf16)
    grad_up = (grad_hidden * silu_gate).astype(bf16)
    grad_gu = jnp.concatenate([grad_gate, grad_up], axis=1)
    normed_terms = dot_nt(grad_gu, full_gu).reshape(micro, PLANE, tok_rows, width)
    got = plane_sum_start(normed_terms)
    gu_mine, gu_other = core_halves(dot_tn(after(normed_two, normed_terms), grad_gu).astype(bf16))
    *got, gu_mine = sync(*got, gu_mine)
    gu_half = core_sum(gu_mine, gu_other)
    down_mine, down_other = core_halves(dot_tn(after(hidden, gu_mine), gathered_cot).astype(bf16))
    gu_total = ring_part(gu_half, size - 1)
    *got, gu_total, down_mine = sync(*plane_sum_more(normed_terms, *got), gu_total, down_mine)
    grad_normed_two = plane_sum_end(normed_terms, *got)
    down_half = core_sum(down_mine, down_other)
    down_total = ring_part(down_half, size - 1)
    result_terms = dot(after(hidden, gu_total), full_down)

    grad_y = own_cot.astype(f32)
    grad_gain_two = jnp.sum(grad_normed_two * middle * scale_two, axis=(0, 1))
    weighted = grad_normed_two * gain_two
    grad_middle = (
        grad_y
        + scale_two * weighted
        - middle * scale_two**3 * jnp.mean(middle * weighted, axis=-1, keepdims=True)
    )
    pieces = plane_gather_start(grad_middle.astype(bf16))
    gu_moved = along(gu_total, -1, True)
    *pieces, gu_moved, down_total, result_terms = sync(*pieces, gu_moved, down_total, result_terms)
    gu_total = ring_add(gu_half, gu_moved, size - 2)
    gu_moved, down_moved = along(gu_total, -1, True), along(down_total, -1, True)
    *pieces, gu_moved, down_moved = sync(*plane_gather_more(*pieces), gu_moved, down_moved)
    grad_branch = plane_gather_end(*pieces)
    for k in range(size - 3, 0, -1):
        gu_moved = along(ring_add(gu_half, gu_moved, k), -1, True)
        down_moved = along(ring_add(down_half, down_moved, k + 1), -1, True)
    grad_attn = dot_nt(grad_branch, full_out).astype(bf16).reshape(micro, chunk, q_part)

    states = [[grad_attn[m], attended[m]] for m in range(micro)]
    grad_kv = [None] * micro
    grad_query = [None] * micro
    result_terms = result_terms.reshape(micro, PLANE, tok_rows, width)
    for k in range(size - 1, -1, -1):
        first = k == size - 1
        for m in range(micro):
            outs = attend_back(
                m, k, first, k == 0, info, q_rot[m], kv_pieces[m][k], lse[m], qpos, qbeg[m], kpos, cos_all[m, k], sin_all[m, k],
                e4, states[m],
            )
            if first:
                states[m] = outs[:3]
                grad_kv[m] = outs[3]
            else:
                states[m] = states[m][:2] + [outs[0]]
                grad_kv[m] = (grad_kv[m].astype(f32) + outs[1].astype(f32)).astype(bf16)
            if k == 0:
                grad_query[m] = outs[-1]
        if first:
            got = plane_sum_start(after(result_terms, *grad_kv))
        if k > 0:
            moved = [along(grad_kv[m], -1, False) for m in range(micro)]
        if k == size - 1:
            *got, gu_moved, down_moved = sync(*got, gu_moved, down_moved)
            sum_gu, down_last = ring_add(gu_half, gu_moved, 0), ring_add(down_half, down_moved, 1)
            down_moved = along(down_last, -1, True)
            got = plane_sum_more(result_terms, *got)
            term_out = plane_swap(dot_tn(attn_low, after(grad_branch, down_last)).astype(bf16), 1, 0)
        elif k == size - 2:
            *got, down_moved, term_out = sync(*got, down_moved, term_out)
            output = (middle + plane_sum_end(result_terms, *got)).astype(bf16)
            sum_down = ring_add(down_half, down_moved, 0)
            sum_gu = plane_swap(after(sum_gu, sum_down), 0, 1)
            out_mine, out_other = core_halves(term_out)
        if k > 0:
            grad_kv = moved
            if not first:
                *flat, grad_kv[0], grad_kv[1] = sync(*[states[m][2] for m in range(micro)], *grad_kv)
                for m in range(micro):
                    states[m] = states[m][:2] + [flat[m]]
    sum_gu = sum_gu.astype(f32).reshape(shard_rows, PLANE, 2, ff_part)

    grad_qkv = jnp.concatenate([jnp.concatenate(grad_query, axis=0), jnp.concatenate(grad_kv, axis=0)], axis=1)
    term_qkv = dot_tn(normed_one, grad_qkv).astype(bf16)
    qkv_mine, qkv_other = core_halves(term_qkv)
    grad_normed_part = dot_nt(after(grad_qkv, qkv_mine), full_qkv)
    part_terms = grad_normed_part.reshape(micro, PLANE, tok_rows, width)
    got = plane_sum_start(part_terms)
    full_in = gathered_in.astype(f32)
    grad_gain_one = jnp.sum(grad_normed_part * full_in * rms_scale(full_in), axis=0)
    gain_terms = jnp.stack([grad_gain_one, grad_gain_two]).astype(bf16)
    gain_terms = jnp.pad(gain_terms, ((0, LANES - 2), (0, 0))).T
    gain_mine, gain_other = core_halves(gain_terms)
    last_half = jnp.concatenate(
        [core_sum(qkv_mine, qkv_other), core_sum(out_mine, out_other), core_sum(gain_mine, gain_other)], axis=-1
    )
    last_total = ring_part(last_half, size - 1)
    for k in range(size - 2, -1, -1):
        last_moved = along(last_total, -1, True)
        if k == size - 2:
            *got, last_moved = sync(*got, last_moved)
            got = plane_sum_more(part_terms, *got)
        elif k == size - 3:
            *got, last_moved = sync(*got, last_moved)
        last_total = ring_add(last_half, last_moved, k)
    grad_normed_one = plane_sum_end(part_terms, *got)
    last_total = plane_swap(last_total, 0, 1).astype(f32).reshape(shard_rows, PLANE, -1)
    scale_one = rms_scale(layer_in)
    weighted = grad_normed_one * gain_one
    input_grad = (
        grad_middle
        + scale_one * weighted
        - layer_in * scale_one**3 * jnp.mean(layer_in * weighted, axis=-1, keepdims=True)
    )
    cuts = np.cumsum([q_part, kv_part, kv_part, out_part])
    sum_query, sum_key, sum_value, sum_out, gain_sum = jnp.split(last_total, cuts, axis=2)
    gain_sum = jnp.sum(gain_sum, axis=1)
    return (
        output[:, None],
        input_grad[:, None],
        gain_sum[:, 0],
        gain_sum[:, 1],
        sum_query.reshape(shard_rows, -1),
        sum_key.reshape(shard_rows, -1),
        sum_value.reshape(shard_rows, -1),
        sum_out.reshape(shard_rows, -1),
        from_ff_parts(sum_gu[:, :, 0]),
        from_ff_parts(sum_gu[:, :, 1]),
        sum_down.astype(f32),
    )


def solution(mesh):
    blocks = mesh.shape["blk"]
    grid = Mesh(mesh.devices.reshape(2, blocks // PLANE, PLANE), ("stream", "zed", "plane"))
    tokens = P(None, "stream", ("zed", "plane"), None)
    vector = P(("stream", "zed", "plane"))
    matrix = P(("stream", "zed", "plane"), None)
    return jax.shard_map(
        on_device,
        mesh=grid,
        in_specs=(tokens, tokens, P(None, "stream", None), vector, vector) + (matrix,) * 7,
        out_specs=(tokens, tokens, vector, vector) + (matrix,) * 7,
        check_vma=False,
    )
```

```python
import math

import jax
import jax.numpy as jnp
import numpy as np
from jax import lax
from jax.experimental import pallas as pl
from jax.experimental.pallas import tpu as pltpu
from jax.sharding import Mesh
from jax.sharding import PartitionSpec as P

HQ = 16
HK = 8
DH = 96
PLANE = 4
FF_TILES = 4
LANES = 128
VMEM_BYTES = 50 * 1024 * 1024

epsilon = 1e-05
rope_base = 100000.0
masked_score = -1e30
score_scale = 1.0 / math.sqrt(DH)
exp2_scale = score_scale * math.log2(math.e)

LIGHT = pl.CostEstimate(flops=1, bytes_accessed=1, transcendentals=0)
CHUNK_COST = pl.CostEstimate(flops=1, bytes_accessed=6000000, transcendentals=0)

f32 = jnp.float32
bf16 = jnp.bfloat16


def spread(heads):
    table = np.zeros((heads * DH, heads * LANES), np.float32)
    for head in range(heads):
        for i in range(DH):
            lane = i if i < DH // 2 else i + (LANES - DH) // 2
            table[head * DH + i, head * LANES + lane] = 1.0
    return jnp.asarray(table, bf16)


def rms_scale(values):
    return lax.rsqrt(jnp.mean(values * values, axis=-1, keepdims=True) + epsilon)


def dot(a, b):
    return jnp.dot(a, b, preferred_element_type=f32)


def dot_nt(a, b):
    return lax.dot_general(a, b, (((1,), (1,)), ((), ())), preferred_element_type=f32)


def dot_tn(a, b):
    return lax.dot_general(a, b, (((0,), (0,)), ((), ())), preferred_element_type=f32)


def project_kernel(size, info_ref, x_ref, cos_ref, sin_ref, e4_ref, e8_ref, *rest):
    blocks, (n_ref, q_ref, kv_ref, w_ref, out_w_ref, gains_ref, scale_ref, pad_s) = rest[: 2 * size], rest[2 * size :]
    rows = blocks[0].shape[0]
    heads = 8 * DH

    @pl.when(pl.program_id(0) == 0)
    def _():
        for i, block in enumerate(blocks):
            core = info_ref[1] if i < size else 1 - info_ref[1]
            start = pl.multiple_of((core * size + lax.rem(info_ref[0] - i % size + size, size)) * rows, rows)
            w_ref[pl.ds(start, rows), :] = block[:, : heads + LANES]
            out_w_ref[pl.ds(start, rows), :] = block[:, heads + LANES :]
            pad_s[pl.ds(start, rows), :] = dot(block[:, :heads], e8_ref[...]).astype(bf16)
        rows_to = lax.broadcasted_iota(jnp.int32, (LANES, LANES), 0)
        same = (rows_to == lax.broadcasted_iota(jnp.int32, (LANES, LANES), 1)).astype(bf16)
        gains_ref[...] = dot_nt(same[:8], w_ref[:, heads:])

    x = x_ref[...].astype(f32)
    scale = rms_scale(x)
    scale_ref[...] = scale
    normed = (x * scale * gains_ref[0:1, :]).astype(bf16)
    n_ref[...] = normed
    pre = dot(normed, pad_s[...])
    cos, sin = cos_ref[...], sin_ref[...]
    parts = []
    for head in range(8):
        piece = pre[:, head * LANES : (head + 1) * LANES]
        if head < 6:
            piece = piece * cos + pltpu.roll(piece, LANES // 2, 1) * sin
        parts.append(piece.astype(bf16))
    q_ref[...] = jnp.concatenate(parts[:4], axis=1)
    kv_ref[...] = dot_nt(jnp.concatenate(parts[4:], axis=1), e4_ref[...]).astype(bf16)


def project(info, x, blocks, cos, sin, e4, e8):
    rows, width = x.shape
    step = min(256, rows)
    size = len(blocks) // 2
    cols = blocks[0].shape[1]
    first = 8 * DH + LANES
    whole = lambda a: pl.BlockSpec(a.shape, lambda i, n: (0,) * a.ndim)
    by_row = lambda c: pl.BlockSpec((step, c), lambda i, n: (i, 0))
    return pl.pallas_call(
        lambda *refs: project_kernel(size, *refs),
        grid_spec=pltpu.PrefetchScalarGridSpec(
            num_scalar_prefetch=1,
            grid=(rows // step,),
            in_specs=[by_row(width), by_row(LANES), by_row(LANES), whole(e4), whole(e8)] + [whole(b) for b in blocks],
            out_specs=[
                by_row(width),
                by_row(4 * LANES),
                by_row(4 * DH),
                pl.BlockSpec((width, first), lambda i, n: (0, 0)),
                pl.BlockSpec((width, cols - first), lambda i, n: (0, 0)),
                pl.BlockSpec((8, width), lambda i, n: (0, 0)),
                by_row(1),
            ],
            scratch_shapes=[pltpu.VMEM((width, 8 * LANES), bf16)],
        ),
        out_shape=[
            jax.ShapeDtypeStruct((rows, width), bf16),
            jax.ShapeDtypeStruct((rows, 4 * LANES), bf16),
            jax.ShapeDtypeStruct((rows, 4 * DH), bf16),
            jax.ShapeDtypeStruct((width, first), bf16),
            jax.ShapeDtypeStruct((width, cols - first), bf16),
            jax.ShapeDtypeStruct((8, width), f32),
            jax.ShapeDtypeStruct((rows, 1), f32),
        ],
        compiler_params=pltpu.CompilerParams(vmem_limit_bytes=VMEM_BYTES),
        cost_estimate=LIGHT,
        name="project",
    )(info, x, cos, sin, e4, e8, *blocks)


def assemble_kernel(size, info_ref, *rest):
    blocks, out_ref = rest[: 2 * size], rest[2 * size]
    rows = blocks[0].shape[0]
    for i, block in enumerate(blocks):
        core = info_ref[1] if i < size else 1 - info_ref[1]
        start = pl.multiple_of((core * size + lax.rem(info_ref[0] - i % size + size, size)) * rows, rows)
        out_ref[pl.ds(start, rows), :] = block[...]


def assemble(info, blocks):
    size = len(blocks) // 2
    rows, width = blocks[0].shape
    step = width // 3 if width % 384 == 0 else width // 4
    return pl.pallas_call(
        lambda *refs: assemble_kernel(size, *refs),
        grid_spec=pltpu.PrefetchScalarGridSpec(
            num_scalar_prefetch=1,
            grid=(width // step,),
            in_specs=[pl.BlockSpec((rows, step), lambda i, n: (0, i)) for _ in blocks],
            out_specs=pl.BlockSpec((len(blocks) * rows, step), lambda i, n: (0, i)),
        ),
        out_shape=jax.ShapeDtypeStruct((len(blocks) * rows, width), blocks[0].dtype),
        compiler_params=pltpu.CompilerParams(vmem_limit_bytes=VMEM_BYTES),
        cost_estimate=LIGHT,
        name="assemble",
    )(info, *blocks)


def allowed_of(info_ref, k, chunk, qpos_ref, qbeg_ref, kpos_ref):
    kpos = kpos_ref[...] + (info_ref[0] - k) * chunk
    return (kpos <= qpos_ref[...]) & (kpos >= qbeg_ref[...])


def useful_of(info_ref, m, k, chunk):
    z = info_ref[0]
    return (k <= z) & ((z - k + 1) * chunk - 1 >= info_ref[2 + m])


def stack_heads(block, h):
    return jnp.concatenate(
        [block[:, (2 * h) * LANES : (2 * h + 1) * LANES], block[:, (2 * h + 1) * LANES : (2 * h + 2) * LANES]], axis=0
    )


def run_kernel(body, info, inputs, outs, aliases, name):
    def spec(entry):
        if isinstance(entry, tuple):
            return pl.BlockSpec(entry[1], lambda i, n: entry[2])
        return pl.BlockSpec(entry.shape, lambda i, n: (0,) * entry.ndim)

    return list(
        pl.pallas_call(
            body,
            grid_spec=pltpu.PrefetchScalarGridSpec(
                num_scalar_prefetch=1,
                grid=(1,),
                in_specs=[spec(entry) for entry in inputs],
                out_specs=[pl.BlockSpec(o.shape, lambda i, n, o=o: (0,) * len(o.shape)) for o in outs],
            ),
            out_shape=outs,
            input_output_aliases=aliases,
            compiler_params=pltpu.CompilerParams(vmem_limit_bytes=VMEM_BYTES),
            cost_estimate=CHUNK_COST,
            name=name,
        )(info, *[entry[0] if isinstance(entry, tuple) else entry for entry in inputs])
    )


def attend_kernel(m, k, last, info_ref, q_ref, kv_ref, qpos_ref, qbeg_ref, kpos_ref, e_ref, *rest):
    chunk = kv_ref.shape[0]
    if k > 0:
        top_in, acc_in, rest = rest[0], rest[1], rest[2:]
    top_ref, acc_ref = rest[0], rest[1]

    def run():
        allowed = allowed_of(info_ref, k, chunk, qpos_ref, qbeg_ref, kpos_ref)
        kv = kv_ref[...]
        q = q_ref[...]
        one_lane = (lax.broadcasted_iota(jnp.int32, (1, LANES), 1) == DH // 2).astype(f32)
        for h in range(2):
            keys = dot(kv, e_ref[:, h * LANES : (h + 1) * LANES]).astype(bf16)
            vals = (dot(kv, e_ref[:, (2 + h) * LANES : (3 + h) * LANES]) + one_lane).astype(bf16)
            s = jnp.where(allowed, dot_nt(keys, stack_heads(q, h)), masked_score)
            new = jnp.max(s, axis=0, keepdims=True)
            if k > 0:
                old = top_in[h]
                new = jnp.maximum(old, new)
            w = jnp.where(allowed, jnp.exp2((s - new) * exp2_scale), 0.0).astype(bf16)
            acc = dot_tn(vals, w)
            if k > 0:
                acc = acc_in[h] * jnp.exp2((old - new) * exp2_scale) + acc
            acc_ref[h] = acc
            top_ref[h] = new

    if k == 0:
        run()
    else:
        useful = useful_of(info_ref, m, k, chunk)
        pl.when(useful)(run)

        @pl.when(jnp.logical_not(useful))
        def _():
            top_ref[...] = top_in[...]
            acc_ref[...] = acc_in[...]

    if last:
        att_ref, low_ref, lse_ref = rest[2:]
        parts = []
        for h in range(2):
            acc = acc_ref[h]
            total = acc[DH // 2 : DH // 2 + 1, :]
            lse_ref[h] = top_ref[h] * exp2_scale + jnp.log2(total)
            flat = (acc / total).T
            rows = flat.shape[0] // 2
            parts += [flat[:rows], flat[rows:]]
        att = jnp.concatenate(parts, axis=1)
        att_ref[...] = att
        low_ref[...] = dot_nt(att.astype(bf16), e_ref[...]).astype(bf16)


def attend(m, k, last, info, q, kv, qpos, qbeg, kpos, e4, state):
    rows = q[1][0]
    outs = [jax.ShapeDtypeStruct((2, 1, 2 * rows), f32), jax.ShapeDtypeStruct((2, LANES, 2 * rows), f32)]
    if last:
        outs += [
            jax.ShapeDtypeStruct((rows, 4 * LANES), f32),
            jax.ShapeDtypeStruct((rows, 4 * DH), bf16),
            jax.ShapeDtypeStruct((2, 1, 2 * rows), f32),
        ]
    return run_kernel(
        lambda *refs: attend_kernel(m, k, last, *refs),
        info,
        [q, kv, qpos, qbeg, kpos, e4] + state,
        outs,
        {7: 0, 8: 1} if k > 0 else {},
        "attend",
    )


def attend_back_kernel(
    m, k, first, last, info_ref, q_ref, kv_ref, lse_ref, qpos_ref, qbeg_ref, kpos_ref, cosk_ref, sink_ref, e_ref, *rest
):
    chunk = kv_ref.shape[0]
    if first:
        g_ref, att_ref, rest = rest[0], rest[1], rest[2:]
        go_ref, delta_ref, dq_ref, dkv_ref = rest[:4]
        go = dot(g_ref[...], e_ref[...])
        for h in range(2):
            go_h = stack_heads(go, h)
            go_ref[h] = go_h.astype(bf16)
            prod = go_h * stack_heads(att_ref[...], h)
            delta_ref[h] = jnp.sum(prod.T, axis=0, keepdims=True)
    else:
        go_ref, delta_ref, dq_in, moved_ref, rest = rest[0], rest[1], rest[2], rest[3], rest[4:]
        dq_ref, dkv_ref = rest[:2]

    def run():
        allowed = allowed_of(info_ref, k, chunk, qpos_ref, qbeg_ref, kpos_ref)
        kv = kv_ref[...]
        q = q_ref[...]
        cosk, sink = cosk_ref[...], sink_ref[...]
        grad_keys, grad_vals = [], []
        for h in range(2):
            keys = dot(kv, e_ref[:, h * LANES : (h + 1) * LANES]).astype(bf16)
            vals = dot(kv, e_ref[:, (2 + h) * LANES : (3 + h) * LANES]).astype(bf16)
            q_h = stack_heads(q, h)
            go_h = go_ref[h]
            s = dot_nt(keys, q_h)
            w = jnp.where(allowed, jnp.exp2(s * exp2_scale - lse_ref[h]), 0.0)
            grad_vals.append(dot(w.astype(bf16), go_h).astype(bf16))
            ds = (w * (dot_nt(vals, go_h) - delta_ref[h])).astype(bf16)
            dq = dot_tn(keys, ds)
            dq_ref[h] = dq if first else dq_in[h] + dq
            gk = dot(ds, q_h) * score_scale
            gk = gk * cosk + pltpu.roll(gk * sink, LANES // 2, 1)
            grad_keys.append(gk.astype(bf16))
        total = dot_nt(jnp.concatenate(grad_keys + grad_vals, axis=1), e_ref[...])
        if not first:
            total = total + moved_ref[...].astype(f32)
        dkv_ref[...] = total.astype(bf16)

    if k == 0:
        run()
    else:
        useful = useful_of(info_ref, m, k, chunk)
        pl.when(useful)(run)

        @pl.when(jnp.logical_not(useful))
        def _():
            dkv_ref[...] = jnp.zeros(dkv_ref.shape, bf16) if first else moved_ref[...]
            dq_ref[...] = jnp.zeros(dq_ref.shape, f32) if first else dq_in[...]

    if last:
        out_ref = rest[-1]
        parts = []
        for h in range(2):
            flat = dq_ref[h].T * score_scale
            rows = flat.shape[0] // 2
            for piece in (flat[:rows], flat[rows:]):
                parts.append((piece * cosk_ref[...] + pltpu.roll(piece * sink_ref[...], LANES // 2, 1)).astype(bf16))
        out_ref[...] = dot_nt(jnp.concatenate(parts, axis=1), e_ref[...]).astype(bf16)


def attend_back(m, k, first, last, info, q, kv, lse, qpos, qbeg, kpos, cosk, sink, e4, state):
    rows = q[1][0]
    outs = []
    if first:
        outs += [jax.ShapeDtypeStruct((2, 2 * rows, LANES), bf16), jax.ShapeDtypeStruct((2, 1, 2 * rows), f32)]
    outs += [jax.ShapeDtypeStruct((2, LANES, 2 * rows), f32), jax.ShapeDtypeStruct((rows, 4 * DH), bf16)]
    if last:
        outs += [jax.ShapeDtypeStruct((rows, 4 * DH), bf16)]
    return run_kernel(
        lambda *refs: attend_back_kernel(m, k, first, last, *refs),
        info,
        [q, kv, lse, qpos, qbeg, kpos, cosk, sink, e4] + state,
        outs,
        {} if first else {12: 0},
        "attend_back",
    )


def store_split(sum_of, tok_rows, first_ref, second_ref, keep_first_ref, keep_second_ref):
    for i, slot in enumerate((1, 3)):
        first_ref[i] = sum_of(slot * tok_rows, tok_rows).astype(bf16)
        keep_first_ref[i] = sum_of((slot - 1) * tok_rows, tok_rows)
    for i in range(2):
        second_ref[i] = sum_of((PLANE + 2 + i) * tok_rows, tok_rows).astype(bf16)
        keep_second_ref[i] = sum_of((PLANE + i) * tok_rows, tok_rows)


def split_outs(tok_rows, width):
    return [jax.ShapeDtypeStruct((2, tok_rows, width), kind) for kind in (bf16, bf16, f32, f32)]


def dot_split_kernel(tok_rows, a_ref, w_ref, *rest):
    acc_s = rest[-1]
    acc_s[...] = dot(a_ref[...], w_ref[...])
    store_split(lambda start, n: acc_s[start : start + n, :], tok_rows, *rest[:-1])


def dot_split(a, w):
    rows, inner = a.shape
    tok_rows = rows // (2 * PLANE)
    width = w.shape[1]
    step = width // 3
    outs = split_outs(tok_rows, width)
    return list(
        pl.pallas_call(
            lambda *refs: dot_split_kernel(tok_rows, *refs),
            grid=(3,),
            in_specs=[pl.BlockSpec((rows, inner), lambda i: (0, 0)), pl.BlockSpec((inner, step), lambda i: (0, i))],
            out_specs=[pl.BlockSpec((2, tok_rows, step), lambda i: (0, 0, i)) for _ in outs],
            out_shape=outs,
            scratch_shapes=[pltpu.VMEM((rows, step), f32)],
            compiler_params=pltpu.CompilerParams(vmem_limit_bytes=VMEM_BYTES),
            cost_estimate=LIGHT,
            name="dot_split",
        )(a, w)
    )


def ffn_kernel(size, tok_rows, info_ref, n_ref, g_ref, *rest):
    gu_blocks, down_blocks, rest = rest[: 2 * size], rest[2 * size : 4 * size], rest[4 * size :]
    hidden_ref, *outs = rest[:5]
    gu_theirs_ref, gu_mine_ref, down_theirs_ref, down_mine_ref = rest[5:9]
    gu_s, down_s, acc_s, flat_s, grad_s = rest[9:]
    f, last = pl.program_id(0), pl.num_programs(0) - 1
    units = hidden_ref.shape[1]
    half = flat_s.shape[0] // 2

    def place(i, rows):
        core = info_ref[1] if i < size else 1 - info_ref[1]
        return pl.ds(pl.multiple_of((core * size + lax.rem(info_ref[0] - i % size + size, size)) * rows, rows), rows)

    @pl.when(f == 0)
    def _():
        acc_s[...] = jnp.zeros(acc_s.shape, f32)
        flat_s[...] = n_ref[...].T
        for i, block in enumerate(down_blocks):
            down_s[place(i, block.shape[0]), :] = block[...]

    for i, block in enumerate(gu_blocks):
        gu_s[place(i, block.shape[0]), :] = block[...]
    w_down = down_s.at[pl.ds(pl.multiple_of(f * units, units), units)]
    step = 4 * tok_rows

    @pl.loop(0, n_ref.shape[0] // step)
    def _(r):
        at = pl.ds(pl.multiple_of(r * step, step), step)
        pre = dot(n_ref[at, :], gu_s[...])
        grad_hidden = dot_nt(g_ref[at, :], w_down[...])
        gate_pre, up_pre = pre[:, :units], pre[:, units:]
        sigmoid_gate = jax.nn.sigmoid(gate_pre)
        silu_gate = gate_pre * sigmoid_gate
        hidden_ref[at, :] = (silu_gate * up_pre).astype(bf16)
        grad_gate = grad_hidden * up_pre * sigmoid_gate * (1.0 + gate_pre * (1.0 - sigmoid_gate))
        both = jnp.concatenate([grad_gate.astype(bf16), (grad_hidden * silu_gate).astype(bf16)], axis=1)
        grad_s[at, :] = both
        acc_s[at, :] += dot_nt(both, gu_s[...])

    core = info_ref[1]
    gu_mine_ref[...] = dot(flat_s[pl.ds(pl.multiple_of(core * half, half), half), :], grad_s[...]).astype(bf16)
    gu_theirs_ref[...] = dot(flat_s[pl.ds(pl.multiple_of((1 - core) * half, half), half), :], grad_s[...]).astype(bf16)
    term_down = dot_tn(hidden_ref[...], g_ref[...]).astype(bf16)
    is_mine = lax.div(f, pl.num_programs(0) // 2) == core

    @pl.when(is_mine)
    def _():
        down_mine_ref[...] = term_down

    @pl.when(jnp.logical_not(is_mine))
    def _():
        down_theirs_ref[...] = term_down

    @pl.when(f == last)
    def _():
        store_split(lambda start, n: acc_s[start : start + n, :], tok_rows, *outs)


def ffn(info, normed, grad_mlp, gu_blocks, down_blocks):
    rows, width = normed.shape
    size = len(gu_blocks) // 2
    tok_rows = rows // (2 * PLANE)
    ff_part = gu_blocks[0].shape[1] // 2
    units = ff_part // FF_TILES
    whole = lambda a: pl.BlockSpec(a.shape, lambda f, n: (0,) * a.ndim, pipeline_mode=pl.Buffered(1))
    outs = split_outs(tok_rows, width)
    gu_half = pl.BlockSpec((width // 2, 2 * units), lambda f, n: (0, f))

    def down_half(core_of):
        return pl.BlockSpec((units, width), lambda f, n: (jnp.clip(f - core_of(n) * (FF_TILES // 2), 0, FF_TILES // 2 - 1), 0))

    return list(
        pl.pallas_call(
            lambda *refs: ffn_kernel(size, tok_rows, *refs),
            grid_spec=pltpu.PrefetchScalarGridSpec(
                num_scalar_prefetch=1,
                grid=(FF_TILES,),
                in_specs=[whole(normed), whole(grad_mlp)]
                + [pl.BlockSpec((block.shape[0], 2 * units), lambda f, n: (0, f)) for block in gu_blocks]
                + [whole(block) for block in down_blocks],
                out_specs=[pl.BlockSpec((rows, units), lambda f, n: (0, f))]
                + [pl.BlockSpec(o.shape, lambda f, n: (0, 0, 0), pipeline_mode=pl.Buffered(1)) for o in outs]
                + [gu_half, gu_half, down_half(lambda n: 1 - n[1]), down_half(lambda n: n[1])],
                scratch_shapes=[
                    pltpu.VMEM((width, 2 * units), bf16),
                    pltpu.VMEM((ff_part, width), bf16),
                    pltpu.VMEM((rows, width), f32),
                    pltpu.VMEM((width, rows), bf16),
                    pltpu.VMEM((rows, 2 * units), bf16),
                ],
            ),
            out_shape=[jax.ShapeDtypeStruct((rows, ff_part), bf16)]
            + outs
            + [jax.ShapeDtypeStruct((width // 2, 2 * ff_part), bf16)] * 2
            + [jax.ShapeDtypeStruct((ff_part // 2, width), bf16)] * 2,
            compiler_params=pltpu.CompilerParams(vmem_limit_bytes=58 * 1024 * 1024),
            cost_estimate=LIGHT,
            name="ffn",
        )(info, normed, grad_mlp, *gu_blocks, *down_blocks)
    )


def project_back_kernel(tok_rows, info_ref, g_ref, w_ref, n_ref, x_ref, scale_ref, *rest):
    first_ref, second_ref, keep_first_ref, keep_second_ref, gain_ref, theirs_ref, mine_ref, acc_s = rest
    rows = 2 * tok_rows
    total = jnp.zeros((1, acc_s.shape[1]), f32)
    for i in range(g_ref.shape[0] // rows):
        at = slice(i * rows, (i + 1) * rows)
        acc = dot_nt(g_ref[at, :], w_ref[...])
        acc_s[at, :] = acc
        total = total + jnp.sum(acc * x_ref[at, :].astype(f32) * scale_ref[at, :], axis=0, keepdims=True)
    gain_ref[...] = jnp.broadcast_to(total, gain_ref.shape)
    store_split(lambda start, n: acc_s[start : start + n, :], tok_rows, first_ref, second_ref, keep_first_ref, keep_second_ref)
    term = dot_tn(n_ref[...], g_ref[...]).astype(bf16)
    is_mine = pl.program_id(0) == info_ref[1]

    @pl.when(is_mine)
    def _():
        mine_ref[...] = term

    @pl.when(jnp.logical_not(is_mine))
    def _():
        theirs_ref[...] = term


def project_back(info, grads, w, normed, x, scale):
    rows, inner = grads.shape
    tok_rows = rows // (2 * PLANE)
    width = w.shape[0]
    half = width // 2
    outs = split_outs(tok_rows, width)
    column = pl.BlockSpec((rows, half), lambda i, n: (0, i))
    out_whole = pl.BlockSpec((half, inner), lambda i, n: (0, 0))
    return list(
        pl.pallas_call(
            lambda *refs: project_back_kernel(tok_rows, *refs),
            grid_spec=pltpu.PrefetchScalarGridSpec(
                num_scalar_prefetch=1,
                grid=(2,),
                in_specs=[
                    pl.BlockSpec((rows, inner), lambda i, n: (0, 0)),
                    pl.BlockSpec((half, inner), lambda i, n: (i, 0)),
                    column,
                    column,
                    pl.BlockSpec((rows, 1), lambda i, n: (0, 0)),
                ],
                out_specs=[pl.BlockSpec((2, tok_rows, half), lambda i, n: (0, 0, i)) for _ in outs]
                + [pl.BlockSpec((8, half), lambda i, n: (0, i)), out_whole, out_whole],
                scratch_shapes=[pltpu.VMEM((rows, half), f32)],
            ),
            out_shape=outs
            + [jax.ShapeDtypeStruct((8, width), f32)]
            + [jax.ShapeDtypeStruct((half, inner), bf16)] * 2,
            compiler_params=pltpu.CompilerParams(vmem_limit_bytes=VMEM_BYTES),
            cost_estimate=LIGHT,
            name="project_back",
        )(info, grads, w, normed, x, scale)
    )


def beside(value, bit):
    return lax.ppermute(value, "plane", [(i, i ^ bit) for i in range(PLANE)])


def other_core(value):
    return lax.ppermute(value, "stream", [(0, 1), (1, 0)])


def along(value, step, wrap):
    size = lax.axis_size("zed")
    pairs = [(i, (i + step) % size) for i in range(size) if wrap or 0 <= i + step < size]
    return lax.ppermute(value, "zed", pairs)


def plane_gather_start(own):
    return [own[0], own[1], beside(own[0], 1), beside(own[1], 2)]


def plane_gather_more(first, second, first_got, second_got):
    pair_one, pair_two = jnp.stack([first, first_got]), jnp.stack([second, second_got])
    return [pair_one, pair_two, beside(pair_one, 2), beside(pair_two, 1)]


def plane_gather_end(pair_one, pair_two, first_more, second_more):
    blocks = [pair_one, first_more, pair_two[:1], second_more[:1], pair_two[1:], second_more[1:]]
    return jnp.concatenate(blocks).reshape(-1, pair_one.shape[-1])


def plane_sum_start(split):
    return [beside(split[0], 1), beside(split[1], 2)]


def plane_sum_more(split, got_first, got_second):
    keep_first, keep_second = split[2], split[3]
    more_first = beside((keep_first[1] + got_first[1]).astype(bf16), 2)
    more_second = beside((keep_second[1] + got_second[1]).astype(bf16), 1)
    return [got_first[0], got_second[0], more_first, more_second]


def plane_sum_end(split, got_first, got_second, more_first, more_second):
    return jnp.stack([split[2][0] + got_first + more_first, split[3][0] + got_second + more_second])


def after(value, *earlier):
    return lax.optimization_barrier((value,) + earlier)[0]


def sync(*values):
    return list(lax.optimization_barrier(values))


def core_halves(full):
    size = lax.axis_size("zed")
    s = lax.axis_index("stream")
    full = full.reshape((2, size, -1) + full.shape[1:])
    mine = lax.dynamic_index_in_dim(full, s, 0, keepdims=False)
    theirs = lax.dynamic_index_in_dim(full, 1 - s, 0, keepdims=False)
    return mine, other_core(theirs)


def core_sum(mine, other):
    return (mine.astype(f32) + other.astype(f32)).astype(bf16)


def ring_part(half, k):
    size = lax.axis_size("zed")
    z = lax.axis_index("zed")
    return lax.dynamic_index_in_dim(half, lax.rem(z - k + size, size), 0, keepdims=False)


def ring_add(half, moved, k):
    return (moved.astype(f32) + ring_part(half, k).astype(f32)).astype(bf16)


def plane_swap(value, split, concat):
    return lax.all_to_all(value, "plane", split_axis=split, concat_axis=concat, tiled=True)


def on_device(inputs, cotangent, seq_lengths, gain_attn, gain_ffn, w_query, w_key, w_value, w_out, w_gate, w_up, w_down):
    size = lax.axis_size("zed")
    s, z, p = lax.axis_index("stream"), lax.axis_index("zed"), lax.axis_index("plane")
    micro, _, tok_rows, width = inputs.shape
    chunk = PLANE * tok_rows
    tokens = micro * chunk
    shard_rows = w_query.shape[0]
    ff_block = w_down.shape[0]
    ff_blocks = 2 * size
    ff_part = ff_blocks * ff_block
    q_part, kv_part = HQ * DH // PLANE, HK * DH // PLANE
    out_part = width // PLANE
    e4, e8 = spread(4), spread(8)

    def by_part(weight):
        return weight.reshape(shard_rows, PLANE, -1)

    def by_ff_part(weight):
        return weight.reshape(shard_rows, ff_blocks, PLANE, ff_block).transpose(0, 2, 1, 3).reshape(shard_rows, PLANE, -1)

    def from_ff_parts(term):
        return term.reshape(shard_rows, PLANE, ff_blocks, ff_block).transpose(0, 2, 1, 3).reshape(shard_rows, -1)

    own_in = inputs[:, 0]
    own_cot = cotangent[:, 0]
    gains = jnp.stack([gain_attn, gain_ffn], axis=1)
    gains = jnp.broadcast_to(jnp.pad(gains, ((0, 0), (0, LANES - 2)))[:, None], (shard_rows, PLANE, LANES))
    qkv_bundle = jnp.concatenate([by_part(w_query), by_part(w_key), by_part(w_value), gains, by_part(w_out)], axis=2)
    qkv_block = plane_swap(qkv_bundle.reshape(shard_rows, -1), 1, 0)
    tiled = (shard_rows, PLANE, FF_TILES, ff_part // FF_TILES)
    ffn_bundle = jnp.stack([by_ff_part(w_gate).reshape(tiled), by_ff_part(w_up).reshape(tiled)], axis=3).reshape(shard_rows, -1)
    qkv_blocks = [qkv_block]
    for _ in range(size - 1):
        qkv_blocks.append(along(qkv_blocks[-1], 1, True))
    qkv_other = [other_core(block) for block in qkv_blocks]
    ffn_block = plane_swap(after(ffn_bundle, qkv_block), 1, 0)
    pieces = sync(*plane_gather_start(after(own_in, qkv_block)))
    gathered_in = plane_gather_end(*sync(*plane_gather_more(*pieces)))
    gu_blocks = [after(ffn_block, qkv_blocks[-1])]
    gu_blocks.append(along(gu_blocks[0], 1, True))

    slot_place = ((jnp.arange(PLANE, dtype=jnp.int32) ^ p)[:, None] * tok_rows + jnp.arange(tok_rows, dtype=jnp.int32)[None, :]).reshape(chunk)
    chunk_place = (z - jnp.arange(size, dtype=jnp.int32))[:, None] * chunk + slot_place[None, :]
    lengths = seq_lengths[:, 0]
    seq_ends = jnp.cumsum(lengths, axis=1)
    begins = jnp.sum(
        jnp.where(seq_ends[:, None, None, :] <= chunk_place[None, :, :, None], lengths[:, None, None, :], 0), axis=-1
    )
    own_begin = begins[:, 0]
    lane = np.arange(LANES)
    place_in_half = lane % (LANES // 2)
    real = place_in_half < DH // 2
    frequency = jnp.where(
        real, rope_base ** (-2.0 * jnp.asarray(np.minimum(place_in_half, DH // 2 - 1), f32) / DH), 0.0
    )
    rope_place = (chunk_place[None] - begins).astype(f32)

    def tables(place):
        angles = jnp.maximum(place, 0.0)[..., None] * frequency
        signs = jnp.asarray(np.where(real, np.where(lane < LANES // 2, -1.0, 1.0), 0.0), f32)
        return jnp.where(real, jnp.cos(angles), 0.0), jnp.sin(angles) * signs

    cos, sin = tables(after(rope_place[:, 0], qkv_block))
    index = jnp.stack([z, s]).astype(jnp.int32)
    info = jnp.concatenate([index, jnp.min(own_begin, axis=1)])
    qpos = jnp.tile(chunk_place[0], 2)[None]
    qbeg = jnp.tile(own_begin, (1, 2))[:, None]
    kpos = slot_place[:, None]

    normed_one, q_rot, kv_own, full_qkv, full_oc, full_gains, in_scale = project(
        index, gathered_in, qkv_blocks + qkv_other, cos.reshape(tokens, LANES), sin.reshape(tokens, LANES), e4, e8
    )
    full_qkv = full_qkv[:, : q_part + 2 * kv_part]
    gain_one, gain_two = full_gains[0:1], full_gains[1:2]
    full_out = plane_swap(full_oc, 0, 1)
    cot_pieces = plane_gather_start(after(own_cot, gathered_in, kv_own))
    q_rot = [(q_rot, (chunk, 4 * LANES), (m, 0)) for m in range(micro)]
    kv_windows = [[(kv_own, (chunk, 4 * DH), (m, 0))] for m in range(micro)]
    kv_pieces = [[piece] for piece in kv_own.reshape(micro, chunk, 4 * DH)]
    qbeg = [(qbeg, (None, 1, 2 * chunk), (m, 0, 0)) for m in range(micro)]
    states = [[] for _ in range(micro)]
    for k in range(size):
        if k < size - 1:
            arrived = [along(kv_pieces[m][k], 1, False) for m in range(micro)]
        for m in range(micro):
            states[m] = attend(m, k, k == size - 1, info, q_rot[m], kv_windows[m][k], qpos, qbeg[m], kpos, e4, states[m])
        if k < size - 1:
            tops = [state[0] for state in states]
            if k == 0:
                tops[0], tops[1], arrived[0], arrived[1], gu_blocks[1], *cot_pieces = sync(
                    *tops, *arrived, gu_blocks[1], *cot_pieces
                )
                cot_pieces = plane_gather_more(*cot_pieces)
            elif k == 1:
                tops[0], tops[1], arrived[0], arrived[1], full_out, *cot_pieces = sync(*tops, *arrived, full_out, *cot_pieces)
            else:
                tops[0], tops[1], arrived[0], arrived[1] = sync(*tops, *arrived)
            for m in range(micro):
                states[m] = [tops[m], states[m][1]]
                kv_pieces[m].append(arrived[m])
                kv_windows[m].append(arrived[m])
    kv_there = [pieces[-1] for pieces in kv_pieces]
    attended, lse = [state[2] for state in states], [state[4] for state in states]
    attn_low = jnp.concatenate([state[3] for state in states], axis=0)
    gathered_cot = plane_gather_end(*cot_pieces)

    gu_blocks[1], down_block, rope_place = sync(gu_blocks[1], w_down, rope_place, *kv_there)[:3]
    down_blocks = [down_block, along(down_block, 1, True)]
    branch_split = dot_split(attn_low, full_out)
    branch_split = sync(*branch_split, down_blocks[1])
    down_blocks[1] = branch_split.pop()
    gu_blocks.append(along(after(gu_blocks[1], down_blocks[1]), 1, True))
    *got, gu_blocks[2] = sync(*plane_sum_start(branch_split), gu_blocks[2])
    down_blocks.append(along(after(down_blocks[1], gu_blocks[2]), 1, True))
    cos_all, sin_all = tables(after(rope_place, gu_blocks[2]))
    *got, down_blocks[2], cos_all, sin_all = sync(*plane_sum_more(branch_split, *got), down_blocks[2], cos_all, sin_all)
    layer_in = own_in.astype(f32)
    middle = layer_in + plane_sum_end(branch_split, *got)
    scale_two = rms_scale(middle)
    pieces = plane_gather_start((middle * scale_two * gain_two).astype(bf16))
    for k in range(2, size - 1):
        down_blocks.append(along(down_blocks[k], 1, True))
    *pieces, down_blocks[-1] = sync(*pieces, down_blocks[-1])
    for k in range(2, size - 1):
        gu_blocks.append(along(after(gu_blocks[k], down_blocks[-1]), 1, True))
    *pieces, gu_blocks[-1] = sync(*plane_gather_more(*pieces), gu_blocks[-1])
    normed_two = plane_gather_end(*pieces)

    gu_all = gu_blocks + [other_core(block) for block in gu_blocks]
    down_all = down_blocks + [other_core(block) for block in down_blocks]
    hidden, *outs = ffn(index, normed_two, gathered_cot, gu_all, down_all)
    normed_split, (gu_theirs, gu_mine, down_theirs, down_mine) = outs[:4], outs[4:]
    got = plane_sum_start(normed_split)
    gu_half = core_sum(gu_mine, other_core(gu_theirs)).reshape(size, -1, 2 * ff_part)
    down_half = core_sum(down_mine, other_core(down_theirs)).reshape(size, -1, width)
    gu_total, down_total = ring_part(gu_half, size - 1), ring_part(down_half, size - 1)
    *got, gu_total, down_total = sync(*got, gu_total, down_total)
    gu_moved, down_moved = along(gu_total, -1, True), along(down_total, -1, True)
    got = sync(*plane_sum_more(normed_split, *got))
    grad_normed_two = plane_sum_end(normed_split, *got)
    grad_y = own_cot.astype(f32)
    grad_gain_two = jnp.sum(grad_normed_two * middle * scale_two, axis=(0, 1))
    weighted = grad_normed_two * gain_two
    grad_middle = (
        grad_y
        + scale_two * weighted
        - middle * scale_two**3 * jnp.mean(middle * weighted, axis=-1, keepdims=True)
    )
    pieces = plane_gather_start(grad_middle.astype(bf16))
    *pieces, gu_moved, down_moved = sync(*pieces, gu_moved, down_moved)
    gu_total, down_total = ring_add(gu_half, gu_moved, size - 2), ring_add(down_half, down_moved, size - 2)
    gu_moved, down_moved = along(gu_total, -1, True), along(down_total, -1, True)
    full_down = assemble(index, [after(down_all[0], gu_total)] + down_all[1:])
    result_split = dot_split(after(hidden, gu_total), full_down)
    pieces = plane_gather_more(*pieces)
    for k in range(size - 3, -1, -1):
        gu_total, down_total = ring_add(gu_half, gu_moved, k), ring_add(down_half, down_moved, k)
        if k == size - 3:
            *pieces, gu_total, down_total, result_split[0] = sync(*pieces, gu_total, down_total, result_split[0])
        if k > 0:
            gu_moved, down_moved = along(gu_total, -1, True), along(down_total, -1, True)
    sum_gu, sum_down = gu_total, down_total
    grad_branch = plane_gather_end(*pieces)
    grad_attn = dot_nt(grad_branch, full_out).astype(bf16)

    states = [[(grad_attn, (chunk, q_part), (m, 0)), attended[m]] for m in range(micro)]
    grad_query = [None] * micro
    terms = [None] * micro
    for k in range(size - 1, -1, -1):
        first = k == size - 1
        for m in range(micro):
            outs = attend_back(
                m, k, first, k == 0, info, q_rot[m], kv_windows[m][k], lse[m], qpos, qbeg[m], kpos,
                (cos_all, (None, None, chunk, LANES), (m, k, 0, 0)), (sin_all, (None, None, chunk, LANES), (m, k, 0, 0)),
                e4, states[m] if first else states[m] + [moved[m]],
            )
            states[m] = outs[:3] if first else states[m][:2] + [outs[0]]
            terms[m] = outs[3] if first else outs[1]
            if k == 0:
                grad_query[m] = outs[-1]
        if k > 0:
            moved = [along(term, -1, False) for term in terms]
            moved[0] = after(moved[0], terms[-1], *([sum_gu, sum_down] if first else []))
        if first:
            got = plane_sum_start(sync(*result_split[:2], *terms)[:2])
        elif k == size - 2:
            moved[-1], *got = sync(moved[-1], *got)
            got = plane_sum_more(result_split, *got)
            term_out = dot_tn(attn_low, after(grad_branch, *got[:2])).astype(bf16)
        elif k == size - 3:
            moved[-1], term_out, *got = sync(moved[-1], term_out, *got)
            output = (middle + plane_sum_end(result_split, *got)).astype(bf16)
            term_out = plane_swap(after(term_out, output), 1, 0)
            sum_gu = plane_swap(after(sum_gu, *terms, output), 0, 1)

    grad_qkv = jnp.concatenate([jnp.concatenate(grad_query, axis=0), jnp.concatenate(terms, axis=0)], axis=1)
    out_mine, out_other = core_halves(term_out)
    *part_split, gain_rows, qkv_theirs, qkv_mine = project_back(index, grad_qkv, full_qkv, normed_one, gathered_in, in_scale)
    got = plane_sum_start(part_split)
    gain_terms = jnp.stack([gain_rows[0], grad_gain_two]).astype(bf16)
    gain_terms = jnp.pad(gain_terms, ((0, LANES - 2), (0, 0))).T
    gain_mine, gain_other = core_halves(gain_terms)
    qkv_half = core_sum(qkv_mine, other_core(qkv_theirs)).reshape(size, shard_rows * PLANE, -1)
    last_half = jnp.concatenate([qkv_half, core_sum(out_mine, out_other), core_sum(gain_mine, gain_other)], axis=-1)
    last_total = ring_part(last_half, size - 1)
    for k in range(size - 2, -1, -1):
        last_moved = along(last_total, -1, True)
        if k == size - 2:
            *got, last_moved = sync(*got, last_moved)
            got = plane_sum_more(part_split, *got)
        elif k == size - 3:
            *got, last_moved = sync(*got, last_moved)
        last_total = ring_add(last_half, last_moved, k)
    grad_normed_one = plane_sum_end(part_split, *got)
    last_total = plane_swap(last_total, 0, 1).astype(f32).reshape(shard_rows, PLANE, -1)
    scale_one = rms_scale(layer_in)
    weighted = grad_normed_one * gain_one
    input_grad = (
        grad_middle
        + scale_one * weighted
        - layer_in * scale_one**3 * jnp.mean(layer_in * weighted, axis=-1, keepdims=True)
    )
    sum_gu = sum_gu.astype(f32).reshape(shard_rows, PLANE, FF_TILES, 2, ff_part // FF_TILES)
    cuts = np.cumsum([q_part, kv_part, kv_part, out_part])
    sum_query, sum_key, sum_value, sum_out, gain_sum = jnp.split(last_total, cuts, axis=2)
    gain_sum = jnp.sum(gain_sum, axis=1)
    return (
        output[:, None],
        input_grad[:, None],
        gain_sum[:, 0],
        gain_sum[:, 1],
        sum_query.reshape(shard_rows, -1),
        sum_key.reshape(shard_rows, -1),
        sum_value.reshape(shard_rows, -1),
        sum_out.reshape(shard_rows, -1),
        from_ff_parts(sum_gu[:, :, :, 0]),
        from_ff_parts(sum_gu[:, :, :, 1]),
        sum_down.astype(f32),
    )


def solution(mesh):
    blocks = mesh.shape["blk"]
    grid = Mesh(mesh.devices.reshape(2, blocks // PLANE, PLANE), ("stream", "zed", "plane"))
    tokens = P(None, "stream", ("zed", "plane"), None)
    vector = P(("stream", "zed", "plane"))
    matrix = P(("stream", "zed", "plane"), None)
    return jax.shard_map(
        on_device,
        mesh=grid,
        in_specs=(tokens, tokens, P(None, "stream", None), vector, vector) + (matrix,) * 7,
        out_specs=(tokens, tokens, vector, vector) + (matrix,) * 7,
        check_vma=False,
    )
```

```python
import math

import jax
import jax.numpy as jnp
import numpy as np
from jax import lax
from jax.experimental import pallas as pl
from jax.experimental.pallas import tpu as pltpu
from jax.sharding import Mesh
from jax.sharding import PartitionSpec as P

HQ = 16
HK = 8
DH = 96
PLANE = 4
FF_TILES = 4
LANES = 128
VMEM_BYTES = 50 * 1024 * 1024

epsilon = 1e-05
rope_base = 100000.0
masked_score = -1e30
score_scale = 1.0 / math.sqrt(DH)
exp2_scale = score_scale * math.log2(math.e)

LIGHT = pl.CostEstimate(flops=1, bytes_accessed=1, transcendentals=0)
CHUNK_COST = pl.CostEstimate(flops=1, bytes_accessed=6000000, transcendentals=0)

f32 = jnp.float32
bf16 = jnp.bfloat16


def spread(heads):
    table = np.zeros((heads * DH, heads * LANES), np.float32)
    for head in range(heads):
        for i in range(DH):
            lane = i if i < DH // 2 else i + (LANES - DH) // 2
            table[head * DH + i, head * LANES + lane] = 1.0
    return jnp.asarray(table, bf16)


def rms_scale(values):
    return lax.rsqrt(jnp.mean(values * values, axis=-1, keepdims=True) + epsilon)


def dot(a, b):
    return jnp.dot(a, b, preferred_element_type=f32)


def dot_nt(a, b):
    return lax.dot_general(a, b, (((1,), (1,)), ((), ())), preferred_element_type=f32)


def dot_tn(a, b):
    return lax.dot_general(a, b, (((0,), (0,)), ((), ())), preferred_element_type=f32)


def project_kernel(size, info_ref, x_ref, cos_ref, sin_ref, e4_ref, e8_ref, *rest):
    blocks, (n_ref, q_ref, kv_ref, w_ref, out_w_ref, gains_ref, scale_ref, pad_s) = rest[: 2 * size], rest[2 * size :]
    rows = blocks[0].shape[0]
    heads = 8 * DH

    @pl.when(pl.program_id(0) == 0)
    def _():
        for i, block in enumerate(blocks):
            core = info_ref[1] if i < size else 1 - info_ref[1]
            start = pl.multiple_of((core * size + lax.rem(info_ref[0] - i % size + size, size)) * rows, rows)
            w_ref[pl.ds(start, rows), :] = block[:, : heads + LANES]
            out_w_ref[pl.ds(start, rows), :] = block[:, heads + LANES :]
            pad_s[pl.ds(start, rows), :] = dot(block[:, :heads], e8_ref[...]).astype(bf16)
        rows_to = lax.broadcasted_iota(jnp.int32, (LANES, LANES), 0)
        same = (rows_to == lax.broadcasted_iota(jnp.int32, (LANES, LANES), 1)).astype(bf16)
        gains_ref[...] = dot_nt(same[:8], w_ref[:, heads:])

    x = x_ref[...].astype(f32)
    scale = rms_scale(x)
    scale_ref[...] = scale
    normed = (x * scale * gains_ref[0:1, :]).astype(bf16)
    n_ref[...] = normed
    pre = dot(normed, pad_s[...])
    cos, sin = cos_ref[...], sin_ref[...]
    parts = []
    for head in range(8):
        piece = pre[:, head * LANES : (head + 1) * LANES]
        if head < 6:
            piece = piece * cos + pltpu.roll(piece, LANES // 2, 1) * sin
        parts.append(piece.astype(bf16))
    q_ref[...] = jnp.concatenate(parts[:4], axis=1)
    kv_ref[...] = dot_nt(jnp.concatenate(parts[4:], axis=1), e4_ref[...]).astype(bf16)


def project(info, x, blocks, cos, sin, e4, e8):
    rows, width = x.shape
    step = min(256, rows)
    size = len(blocks) // 2
    cols = blocks[0].shape[1]
    first = 8 * DH + LANES
    whole = lambda a: pl.BlockSpec(a.shape, lambda i, n: (0,) * a.ndim)
    by_row = lambda c: pl.BlockSpec((step, c), lambda i, n: (i, 0))
    return pl.pallas_call(
        lambda *refs: project_kernel(size, *refs),
        grid_spec=pltpu.PrefetchScalarGridSpec(
            num_scalar_prefetch=1,
            grid=(rows // step,),
            in_specs=[by_row(width), by_row(LANES), by_row(LANES), whole(e4), whole(e8)] + [whole(b) for b in blocks],
            out_specs=[
                by_row(width),
                by_row(4 * LANES),
                by_row(4 * DH),
                pl.BlockSpec((width, first), lambda i, n: (0, 0)),
                pl.BlockSpec((width, cols - first), lambda i, n: (0, 0)),
                pl.BlockSpec((8, width), lambda i, n: (0, 0)),
                by_row(1),
            ],
            scratch_shapes=[pltpu.VMEM((width, 8 * LANES), bf16)],
        ),
        out_shape=[
            jax.ShapeDtypeStruct((rows, width), bf16),
            jax.ShapeDtypeStruct((rows, 4 * LANES), bf16),
            jax.ShapeDtypeStruct((rows, 4 * DH), bf16),
            jax.ShapeDtypeStruct((width, first), bf16),
            jax.ShapeDtypeStruct((width, cols - first), bf16),
            jax.ShapeDtypeStruct((8, width), f32),
            jax.ShapeDtypeStruct((rows, 1), f32),
        ],
        compiler_params=pltpu.CompilerParams(vmem_limit_bytes=VMEM_BYTES),
        cost_estimate=LIGHT,
        name="project",
    )(info, x, cos, sin, e4, e8, *blocks)


def assemble_kernel(size, info_ref, *rest):
    blocks, out_ref = rest[: 2 * size], rest[2 * size]
    rows = blocks[0].shape[0]
    for i, block in enumerate(blocks):
        core = info_ref[1] if i < size else 1 - info_ref[1]
        start = pl.multiple_of((core * size + lax.rem(info_ref[0] - i % size + size, size)) * rows, rows)
        out_ref[pl.ds(start, rows), :] = block[...]


def assemble(info, blocks):
    size = len(blocks) // 2
    rows, width = blocks[0].shape
    step = width // 3 if width % 384 == 0 else width // 4
    return pl.pallas_call(
        lambda *refs: assemble_kernel(size, *refs),
        grid_spec=pltpu.PrefetchScalarGridSpec(
            num_scalar_prefetch=1,
            grid=(width // step,),
            in_specs=[pl.BlockSpec((rows, step), lambda i, n: (0, i)) for _ in blocks],
            out_specs=pl.BlockSpec((len(blocks) * rows, step), lambda i, n: (0, i)),
        ),
        out_shape=jax.ShapeDtypeStruct((len(blocks) * rows, width), blocks[0].dtype),
        compiler_params=pltpu.CompilerParams(vmem_limit_bytes=VMEM_BYTES),
        cost_estimate=LIGHT,
        name="assemble",
    )(info, *blocks)


def allowed_of(info_ref, k, chunk, qpos_ref, qbeg_ref, kpos_ref):
    kpos = kpos_ref[...] + (info_ref[0] - k) * chunk
    return (kpos <= qpos_ref[...]) & (kpos >= qbeg_ref[...])


def useful_of(info_ref, m, k, chunk):
    z = info_ref[0]
    return (k <= z) & ((z - k + 1) * chunk - 1 >= info_ref[2 + m])


def stack_heads(block, h):
    return jnp.concatenate(
        [block[:, (2 * h) * LANES : (2 * h + 1) * LANES], block[:, (2 * h + 1) * LANES : (2 * h + 2) * LANES]], axis=0
    )


def run_kernel(body, info, inputs, outs, aliases, name):
    def spec(entry):
        if isinstance(entry, tuple):
            return pl.BlockSpec(entry[1], lambda i, n: entry[2])
        return pl.BlockSpec(entry.shape, lambda i, n: (0,) * entry.ndim)

    return list(
        pl.pallas_call(
            body,
            grid_spec=pltpu.PrefetchScalarGridSpec(
                num_scalar_prefetch=1,
                grid=(1,),
                in_specs=[spec(entry) for entry in inputs],
                out_specs=[pl.BlockSpec(o.shape, lambda i, n, o=o: (0,) * len(o.shape)) for o in outs],
            ),
            out_shape=outs,
            input_output_aliases=aliases,
            compiler_params=pltpu.CompilerParams(vmem_limit_bytes=VMEM_BYTES),
            cost_estimate=CHUNK_COST,
            name=name,
        )(info, *[entry[0] if isinstance(entry, tuple) else entry for entry in inputs])
    )


def attend_kernel(m, k, last, info_ref, q_ref, kv_ref, qpos_ref, qbeg_ref, kpos_ref, e_ref, *rest):
    chunk = kv_ref.shape[0]
    if k > 0:
        top_in, acc_in, rest = rest[0], rest[1], rest[2:]
    top_ref, acc_ref = rest[0], rest[1]

    def run():
        allowed = allowed_of(info_ref, k, chunk, qpos_ref, qbeg_ref, kpos_ref)
        kv = kv_ref[...]
        q = q_ref[...]
        one_lane = (lax.broadcasted_iota(jnp.int32, (1, LANES), 1) == DH // 2).astype(f32)
        for h in range(2):
            keys = dot(kv, e_ref[:, h * LANES : (h + 1) * LANES]).astype(bf16)
            vals = (dot(kv, e_ref[:, (2 + h) * LANES : (3 + h) * LANES]) + one_lane).astype(bf16)
            s = jnp.where(allowed, dot_nt(keys, stack_heads(q, h)), masked_score)
            new = jnp.max(s, axis=0, keepdims=True)
            if k > 0:
                old = top_in[h]
                new = jnp.maximum(old, new)
            w = jnp.where(allowed, jnp.exp2((s - new) * exp2_scale), 0.0).astype(bf16)
            acc = dot_tn(vals, w)
            if k > 0:
                acc = acc_in[h] * jnp.exp2((old - new) * exp2_scale) + acc
            acc_ref[h] = acc
            top_ref[h] = new

    if k == 0:
        run()
    else:
        useful = useful_of(info_ref, m, k, chunk)
        pl.when(useful)(run)

        @pl.when(jnp.logical_not(useful))
        def _():
            top_ref[...] = top_in[...]
            acc_ref[...] = acc_in[...]

    if last:
        att_ref, low_ref, lse_ref = rest[2:]
        parts = []
        for h in range(2):
            acc = acc_ref[h]
            total = acc[DH // 2 : DH // 2 + 1, :]
            lse_ref[h] = top_ref[h] * exp2_scale + jnp.log2(total)
            flat = (acc / total).T
            rows = flat.shape[0] // 2
            parts += [flat[:rows], flat[rows:]]
        att = jnp.concatenate(parts, axis=1)
        att_ref[...] = att
        low_ref[...] = dot_nt(att.astype(bf16), e_ref[...]).astype(bf16)


def attend(m, k, last, info, q, kv, qpos, qbeg, kpos, e4, state):
    rows = q[1][0]
    outs = [jax.ShapeDtypeStruct((2, 1, 2 * rows), f32), jax.ShapeDtypeStruct((2, LANES, 2 * rows), f32)]
    if last:
        outs += [
            jax.ShapeDtypeStruct((rows, 4 * LANES), f32),
            jax.ShapeDtypeStruct((rows, 4 * DH), bf16),
            jax.ShapeDtypeStruct((2, 1, 2 * rows), f32),
        ]
    return run_kernel(
        lambda *refs: attend_kernel(m, k, last, *refs),
        info,
        [q, kv, qpos, qbeg, kpos, e4] + state,
        outs,
        {7: 0, 8: 1} if k > 0 else {},
        "attend",
    )


def attend_back_kernel(
    m, k, first, last, info_ref, q_ref, kv_ref, lse_ref, qpos_ref, qbeg_ref, kpos_ref, cosk_ref, sink_ref, e_ref, *rest
):
    chunk = kv_ref.shape[0]
    if first:
        g_ref, att_ref, rest = rest[0], rest[1], rest[2:]
        go_ref, delta_ref, dq_ref, dkv_ref = rest[:4]
        go = dot(g_ref[...], e_ref[...])
        for h in range(2):
            go_h = stack_heads(go, h)
            go_ref[h] = go_h.astype(bf16)
            prod = go_h * stack_heads(att_ref[...], h)
            delta_ref[h] = jnp.sum(prod.T, axis=0, keepdims=True)
    else:
        go_ref, delta_ref, dq_in, moved_ref, rest = rest[0], rest[1], rest[2], rest[3], rest[4:]
        dq_ref, dkv_ref = rest[:2]

    def run():
        allowed = allowed_of(info_ref, k, chunk, qpos_ref, qbeg_ref, kpos_ref)
        kv = kv_ref[...]
        q = q_ref[...]
        cosk, sink = cosk_ref[...], sink_ref[...]
        grad_keys, grad_vals = [], []
        for h in range(2):
            keys = dot(kv, e_ref[:, h * LANES : (h + 1) * LANES]).astype(bf16)
            vals = dot(kv, e_ref[:, (2 + h) * LANES : (3 + h) * LANES]).astype(bf16)
            q_h = stack_heads(q, h)
            go_h = go_ref[h]
            s = dot_nt(keys, q_h)
            w = jnp.where(allowed, jnp.exp2(s * exp2_scale - lse_ref[h]), 0.0)
            grad_vals.append(dot(w.astype(bf16), go_h).astype(bf16))
            ds = (w * (dot_nt(vals, go_h) - delta_ref[h])).astype(bf16)
            dq = dot_tn(keys, ds)
            dq_ref[h] = dq if first else dq_in[h] + dq
            gk = dot(ds, q_h) * score_scale
            gk = gk * cosk + pltpu.roll(gk * sink, LANES // 2, 1)
            grad_keys.append(gk.astype(bf16))
        total = dot_nt(jnp.concatenate(grad_keys + grad_vals, axis=1), e_ref[...])
        if not first:
            total = total + moved_ref[...].astype(f32)
        dkv_ref[...] = total.astype(bf16)

    if k == 0:
        run()
    else:
        useful = useful_of(info_ref, m, k, chunk)
        pl.when(useful)(run)

        @pl.when(jnp.logical_not(useful))
        def _():
            dkv_ref[...] = jnp.zeros(dkv_ref.shape, bf16) if first else moved_ref[...]
            dq_ref[...] = jnp.zeros(dq_ref.shape, f32) if first else dq_in[...]

    if last:
        out_ref = rest[-1]
        parts = []
        for h in range(2):
            flat = dq_ref[h].T * score_scale
            rows = flat.shape[0] // 2
            for piece in (flat[:rows], flat[rows:]):
                parts.append((piece * cosk_ref[...] + pltpu.roll(piece * sink_ref[...], LANES // 2, 1)).astype(bf16))
        out_ref[...] = dot_nt(jnp.concatenate(parts, axis=1), e_ref[...]).astype(bf16)


def attend_back(m, k, first, last, info, q, kv, lse, qpos, qbeg, kpos, cosk, sink, e4, state):
    rows = q[1][0]
    outs = []
    if first:
        outs += [jax.ShapeDtypeStruct((2, 2 * rows, LANES), bf16), jax.ShapeDtypeStruct((2, 1, 2 * rows), f32)]
    outs += [jax.ShapeDtypeStruct((2, LANES, 2 * rows), f32), jax.ShapeDtypeStruct((rows, 4 * DH), bf16)]
    if last:
        outs += [jax.ShapeDtypeStruct((rows, 4 * DH), bf16)]
    return run_kernel(
        lambda *refs: attend_back_kernel(m, k, first, last, *refs),
        info,
        [q, kv, lse, qpos, qbeg, kpos, cosk, sink, e4] + state,
        outs,
        {} if first else {12: 0},
        "attend_back",
    )


def store_split(sum_of, tok_rows, first_ref, second_ref, keep_first_ref, keep_second_ref):
    for i, slot in enumerate((1, 3)):
        first_ref[i] = sum_of(slot * tok_rows, tok_rows).astype(bf16)
        keep_first_ref[i] = sum_of((slot - 1) * tok_rows, tok_rows)
    for i in range(2):
        second_ref[i] = sum_of((PLANE + 2 + i) * tok_rows, tok_rows).astype(bf16)
        keep_second_ref[i] = sum_of((PLANE + i) * tok_rows, tok_rows)


def split_outs(tok_rows, width):
    return [jax.ShapeDtypeStruct((2, tok_rows, width), kind) for kind in (bf16, bf16, f32, f32)]


def dot_split_kernel(tok_rows, a_ref, w_ref, *rest):
    acc_s = rest[-1]
    acc_s[...] = dot(a_ref[...], w_ref[...])
    store_split(lambda start, n: acc_s[start : start + n, :], tok_rows, *rest[:-1])


def dot_split(a, w):
    rows, inner = a.shape
    tok_rows = rows // (2 * PLANE)
    width = w.shape[1]
    step = width // 3
    outs = split_outs(tok_rows, width)
    return list(
        pl.pallas_call(
            lambda *refs: dot_split_kernel(tok_rows, *refs),
            grid=(3,),
            in_specs=[pl.BlockSpec((rows, inner), lambda i: (0, 0)), pl.BlockSpec((inner, step), lambda i: (0, i))],
            out_specs=[pl.BlockSpec((2, tok_rows, step), lambda i: (0, 0, i)) for _ in outs],
            out_shape=outs,
            scratch_shapes=[pltpu.VMEM((rows, step), f32)],
            compiler_params=pltpu.CompilerParams(vmem_limit_bytes=VMEM_BYTES),
            cost_estimate=LIGHT,
            name="dot_split",
        )(a, w)
    )


def ffn_kernel(size, tok_rows, info_ref, n_ref, g_ref, *rest):
    gu_blocks, down_blocks, rest = rest[: 2 * size], rest[2 * size : 4 * size], rest[4 * size :]
    hidden_ref, *outs = rest[:5]
    gu_theirs_ref, gu_mine_ref, down_theirs_ref, down_mine_ref = rest[5:9]
    gu_s, down_s, acc_s, flat_s, grad_s = rest[9:]
    f, last = pl.program_id(0), pl.num_programs(0) - 1
    units = hidden_ref.shape[1]
    half = flat_s.shape[0] // 2

    def place(i, rows):
        core = info_ref[1] if i < size else 1 - info_ref[1]
        return pl.ds(pl.multiple_of((core * size + lax.rem(info_ref[0] - i % size + size, size)) * rows, rows), rows)

    @pl.when(f == 0)
    def _():
        acc_s[...] = jnp.zeros(acc_s.shape, f32)
        flat_s[...] = n_ref[...].T
        for i, block in enumerate(down_blocks):
            down_s[place(i, block.shape[0]), :] = block[...]

    for i, block in enumerate(gu_blocks):
        gu_s[place(i, block.shape[0]), :] = block[...]
    w_down = down_s.at[pl.ds(pl.multiple_of(f * units, units), units)]
    step = 4 * tok_rows

    @pl.loop(0, n_ref.shape[0] // step)
    def _(r):
        at = pl.ds(pl.multiple_of(r * step, step), step)
        pre = dot(n_ref[at, :], gu_s[...])
        grad_hidden = dot_nt(g_ref[at, :], w_down[...])
        gate_pre, up_pre = pre[:, :units], pre[:, units:]
        sigmoid_gate = jax.nn.sigmoid(gate_pre)
        silu_gate = gate_pre * sigmoid_gate
        hidden_ref[at, :] = (silu_gate * up_pre).astype(bf16)
        grad_gate = grad_hidden * up_pre * sigmoid_gate * (1.0 + gate_pre * (1.0 - sigmoid_gate))
        both = jnp.concatenate([grad_gate.astype(bf16), (grad_hidden * silu_gate).astype(bf16)], axis=1)
        grad_s[at, :] = both
        acc_s[at, :] += dot_nt(both, gu_s[...])

    core = info_ref[1]
    gu_mine_ref[...] = dot(flat_s[pl.ds(pl.multiple_of(core * half, half), half), :], grad_s[...]).astype(bf16)
    gu_theirs_ref[...] = dot(flat_s[pl.ds(pl.multiple_of((1 - core) * half, half), half), :], grad_s[...]).astype(bf16)
    term_down = dot_tn(hidden_ref[...], g_ref[...]).astype(bf16)
    is_mine = lax.div(f, pl.num_programs(0) // 2) == core

    @pl.when(is_mine)
    def _():
        down_mine_ref[...] = term_down

    @pl.when(jnp.logical_not(is_mine))
    def _():
        down_theirs_ref[...] = term_down

    @pl.when(f == last)
    def _():
        store_split(lambda start, n: acc_s[start : start + n, :], tok_rows, *outs)


def ffn(info, normed, grad_mlp, gu_blocks, down_blocks):
    rows, width = normed.shape
    size = len(gu_blocks) // 2
    tok_rows = rows // (2 * PLANE)
    ff_part = gu_blocks[0].shape[1] // 2
    units = ff_part // FF_TILES
    whole = lambda a: pl.BlockSpec(a.shape, lambda f, n: (0,) * a.ndim, pipeline_mode=pl.Buffered(1))
    outs = split_outs(tok_rows, width)
    gu_half = pl.BlockSpec((width // 2, 2 * units), lambda f, n: (0, f))

    def down_half(core_of):
        return pl.BlockSpec((units, width), lambda f, n: (jnp.clip(f - core_of(n) * (FF_TILES // 2), 0, FF_TILES // 2 - 1), 0))

    return list(
        pl.pallas_call(
            lambda *refs: ffn_kernel(size, tok_rows, *refs),
            grid_spec=pltpu.PrefetchScalarGridSpec(
                num_scalar_prefetch=1,
                grid=(FF_TILES,),
                in_specs=[whole(normed), whole(grad_mlp)]
                + [pl.BlockSpec((block.shape[0], 2 * units), lambda f, n: (0, f)) for block in gu_blocks]
                + [whole(block) for block in down_blocks],
                out_specs=[pl.BlockSpec((rows, units), lambda f, n: (0, f))]
                + [pl.BlockSpec(o.shape, lambda f, n: (0, 0, 0), pipeline_mode=pl.Buffered(1)) for o in outs]
                + [gu_half, gu_half, down_half(lambda n: 1 - n[1]), down_half(lambda n: n[1])],
                scratch_shapes=[
                    pltpu.VMEM((width, 2 * units), bf16),
                    pltpu.VMEM((ff_part, width), bf16),
                    pltpu.VMEM((rows, width), f32),
                    pltpu.VMEM((width, rows), bf16),
                    pltpu.VMEM((rows, 2 * units), bf16),
                ],
            ),
            out_shape=[jax.ShapeDtypeStruct((rows, ff_part), bf16)]
            + outs
            + [jax.ShapeDtypeStruct((width // 2, 2 * ff_part), bf16)] * 2
            + [jax.ShapeDtypeStruct((ff_part // 2, width), bf16)] * 2,
            compiler_params=pltpu.CompilerParams(vmem_limit_bytes=58 * 1024 * 1024),
            cost_estimate=LIGHT,
            name="ffn",
        )(info, normed, grad_mlp, *gu_blocks, *down_blocks)
    )


def project_back_kernel(tok_rows, info_ref, g_ref, w_ref, n_ref, x_ref, scale_ref, *rest):
    first_ref, second_ref, keep_first_ref, keep_second_ref, gain_ref, theirs_ref, mine_ref, acc_s = rest
    rows = 2 * tok_rows
    total = jnp.zeros((1, acc_s.shape[1]), f32)
    for i in range(g_ref.shape[0] // rows):
        at = slice(i * rows, (i + 1) * rows)
        acc = dot_nt(g_ref[at, :], w_ref[...])
        acc_s[at, :] = acc
        total = total + jnp.sum(acc * x_ref[at, :].astype(f32) * scale_ref[at, :], axis=0, keepdims=True)
    gain_ref[...] = jnp.broadcast_to(total, gain_ref.shape)
    store_split(lambda start, n: acc_s[start : start + n, :], tok_rows, first_ref, second_ref, keep_first_ref, keep_second_ref)
    term = dot_tn(n_ref[...], g_ref[...]).astype(bf16)
    is_mine = pl.program_id(0) == info_ref[1]

    @pl.when(is_mine)
    def _():
        mine_ref[...] = term

    @pl.when(jnp.logical_not(is_mine))
    def _():
        theirs_ref[...] = term


def project_back(info, grads, w, normed, x, scale):
    rows, inner = grads.shape
    tok_rows = rows // (2 * PLANE)
    width = w.shape[0]
    half = width // 2
    outs = split_outs(tok_rows, width)
    column = pl.BlockSpec((rows, half), lambda i, n: (0, i))
    out_whole = pl.BlockSpec((half, inner), lambda i, n: (0, 0))
    return list(
        pl.pallas_call(
            lambda *refs: project_back_kernel(tok_rows, *refs),
            grid_spec=pltpu.PrefetchScalarGridSpec(
                num_scalar_prefetch=1,
                grid=(2,),
                in_specs=[
                    pl.BlockSpec((rows, inner), lambda i, n: (0, 0)),
                    pl.BlockSpec((half, inner), lambda i, n: (i, 0)),
                    column,
                    column,
                    pl.BlockSpec((rows, 1), lambda i, n: (0, 0)),
                ],
                out_specs=[pl.BlockSpec((2, tok_rows, half), lambda i, n: (0, 0, i)) for _ in outs]
                + [pl.BlockSpec((8, half), lambda i, n: (0, i)), out_whole, out_whole],
                scratch_shapes=[pltpu.VMEM((rows, half), f32)],
            ),
            out_shape=outs
            + [jax.ShapeDtypeStruct((8, width), f32)]
            + [jax.ShapeDtypeStruct((half, inner), bf16)] * 2,
            compiler_params=pltpu.CompilerParams(vmem_limit_bytes=VMEM_BYTES),
            cost_estimate=LIGHT,
            name="project_back",
        )(info, grads, w, normed, x, scale)
    )


def beside(value, bit):
    return lax.ppermute(value, "plane", [(i, i ^ bit) for i in range(PLANE)])


def other_core(value):
    return lax.ppermute(value, "stream", [(0, 1), (1, 0)])


def along(value, step, wrap):
    size = lax.axis_size("zed")
    pairs = [(i, (i + step) % size) for i in range(size) if wrap or 0 <= i + step < size]
    return lax.ppermute(value, "zed", pairs)


def plane_gather_start(own):
    return [own[0], own[1], beside(own[0], 1), beside(own[1], 2)]


def plane_gather_more(first, second, first_got, second_got):
    pair_one, pair_two = jnp.stack([first, first_got]), jnp.stack([second, second_got])
    return [pair_one, pair_two, beside(pair_one, 2), beside(pair_two, 1)]


def plane_gather_end(pair_one, pair_two, first_more, second_more):
    blocks = [pair_one, first_more, pair_two[:1], second_more[:1], pair_two[1:], second_more[1:]]
    return jnp.concatenate(blocks).reshape(-1, pair_one.shape[-1])


def plane_sum_start(split):
    return [beside(split[0], 1), beside(split[1], 2)]


def plane_sum_more(split, got_first, got_second):
    keep_first, keep_second = split[2], split[3]
    more_first = beside((keep_first[1] + got_first[1]).astype(bf16), 2)
    more_second = beside((keep_second[1] + got_second[1]).astype(bf16), 1)
    return [got_first[0], got_second[0], more_first, more_second]


def plane_sum_end(split, got_first, got_second, more_first, more_second):
    return jnp.stack([split[2][0] + got_first + more_first, split[3][0] + got_second + more_second])


def after(value, *earlier):
    return lax.optimization_barrier((value,) + earlier)[0]


def sync(*values):
    return list(lax.optimization_barrier(values))


def core_halves(full):
    size = lax.axis_size("zed")
    s = lax.axis_index("stream")
    full = full.reshape((2, size, -1) + full.shape[1:])
    mine = lax.dynamic_index_in_dim(full, s, 0, keepdims=False)
    theirs = lax.dynamic_index_in_dim(full, 1 - s, 0, keepdims=False)
    return mine, other_core(theirs)


def core_sum(mine, other):
    return (mine.astype(f32) + other.astype(f32)).astype(bf16)


def ring_part(half, k):
    size = lax.axis_size("zed")
    z = lax.axis_index("zed")
    return lax.dynamic_index_in_dim(half, lax.rem(z - k + size, size), 0, keepdims=False)


def ring_add(half, moved, k):
    return (moved.astype(f32) + ring_part(half, k).astype(f32)).astype(bf16)


def plane_swap(value, split, concat):
    return lax.all_to_all(value, "plane", split_axis=split, concat_axis=concat, tiled=True)


def on_device(inputs, cotangent, seq_lengths, gain_attn, gain_ffn, w_query, w_key, w_value, w_out, w_gate, w_up, w_down):
    size = lax.axis_size("zed")
    s, z, p = lax.axis_index("stream"), lax.axis_index("zed"), lax.axis_index("plane")
    micro, _, tok_rows, width = inputs.shape
    chunk = PLANE * tok_rows
    tokens = micro * chunk
    shard_rows = w_query.shape[0]
    ff_block = w_down.shape[0]
    ff_blocks = 2 * size
    ff_part = ff_blocks * ff_block
    q_part, kv_part = HQ * DH // PLANE, HK * DH // PLANE
    out_part = width // PLANE
    e4, e8 = spread(4), spread(8)

    def by_part(weight):
        return weight.reshape(shard_rows, PLANE, -1)

    def by_ff_part(weight):
        return weight.reshape(shard_rows, ff_blocks, PLANE, ff_block).transpose(0, 2, 1, 3).reshape(shard_rows, PLANE, -1)

    def from_ff_parts(term):
        return term.reshape(shard_rows, PLANE, ff_blocks, ff_block).transpose(0, 2, 1, 3).reshape(shard_rows, -1)

    own_in = inputs[:, 0]
    own_cot = cotangent[:, 0]
    gains = jnp.stack([gain_attn, gain_ffn], axis=1)
    gains = jnp.broadcast_to(jnp.pad(gains, ((0, 0), (0, LANES - 2)))[:, None], (shard_rows, PLANE, LANES))
    qkv_bundle = jnp.concatenate([by_part(w_query), by_part(w_key), by_part(w_value), gains, by_part(w_out)], axis=2)
    qkv_block = plane_swap(qkv_bundle.reshape(shard_rows, -1), 1, 0)
    tiled = (shard_rows, PLANE, FF_TILES, ff_part // FF_TILES)
    ffn_bundle = jnp.stack([by_ff_part(w_gate).reshape(tiled), by_ff_part(w_up).reshape(tiled)], axis=3).reshape(shard_rows, -1)
    qkv_blocks = [qkv_block]
    for _ in range(size - 1):
        qkv_blocks.append(along(qkv_blocks[-1], 1, True))
    qkv_other = [other_core(block) for block in qkv_blocks]
    ffn_block = plane_swap(after(ffn_bundle, qkv_block), 1, 0)
    pieces = sync(*plane_gather_start(after(own_in, qkv_block)))
    gathered_in = plane_gather_end(*sync(*plane_gather_more(*pieces)))
    gu_blocks = [after(ffn_block, qkv_blocks[-1])]
    gu_blocks.append(along(gu_blocks[0], 1, True))

    slot_place = ((jnp.arange(PLANE, dtype=jnp.int32) ^ p)[:, None] * tok_rows + jnp.arange(tok_rows, dtype=jnp.int32)[None, :]).reshape(chunk)
    chunk_place = (z - jnp.arange(size, dtype=jnp.int32))[:, None] * chunk + slot_place[None, :]
    lengths = seq_lengths[:, 0]
    seq_ends = jnp.cumsum(lengths, axis=1)
    begins = jnp.sum(
        jnp.where(seq_ends[:, None, None, :] <= chunk_place[None, :, :, None], lengths[:, None, None, :], 0), axis=-1
    )
    own_begin = begins[:, 0]
    lane = np.arange(LANES)
    place_in_half = lane % (LANES // 2)
    real = place_in_half < DH // 2
    frequency = jnp.where(
        real, rope_base ** (-2.0 * jnp.asarray(np.minimum(place_in_half, DH // 2 - 1), f32) / DH), 0.0
    )
    rope_place = (chunk_place[None] - begins).astype(f32)

    def tables(place):
        angles = jnp.maximum(place, 0.0)[..., None] * frequency
        signs = jnp.asarray(np.where(real, np.where(lane < LANES // 2, -1.0, 1.0), 0.0), f32)
        return jnp.where(real, jnp.cos(angles), 0.0), jnp.sin(angles) * signs

    cos, sin = tables(after(rope_place[:, 0], qkv_block))
    index = jnp.stack([z, s]).astype(jnp.int32)
    info = jnp.concatenate([index, jnp.min(own_begin, axis=1)])
    qpos = jnp.tile(chunk_place[0], 2)[None]
    qbeg = jnp.tile(own_begin, (1, 2))[:, None]
    kpos = slot_place[:, None]

    normed_one, q_rot, kv_own, full_qkv, full_oc, full_gains, in_scale = project(
        index, gathered_in, qkv_blocks + qkv_other, cos.reshape(tokens, LANES), sin.reshape(tokens, LANES), e4, e8
    )
    full_qkv = full_qkv[:, : q_part + 2 * kv_part]
    gain_one, gain_two = full_gains[0:1], full_gains[1:2]
    full_out = plane_swap(full_oc, 0, 1)
    cot_pieces = plane_gather_start(after(own_cot, gathered_in, kv_own))
    q_rot = [(q_rot, (chunk, 4 * LANES), (m, 0)) for m in range(micro)]
    kv_windows = [[(kv_own, (chunk, 4 * DH), (m, 0))] for m in range(micro)]
    kv_pieces = [[piece] for piece in kv_own.reshape(micro, chunk, 4 * DH)]
    qbeg = [(qbeg, (None, 1, 2 * chunk), (m, 0, 0)) for m in range(micro)]
    states = [[] for _ in range(micro)]
    for k in range(size):
        if k < size - 1:
            arrived = [along(kv_pieces[m][k], 1, False) for m in range(micro)]
        for m in range(micro):
            states[m] = attend(m, k, k == size - 1, info, q_rot[m], kv_windows[m][k], qpos, qbeg[m], kpos, e4, states[m])
        if k < size - 1:
            tops = [state[0] for state in states]
            if k == 0:
                tops[0], tops[1], arrived[0], arrived[1], gu_blocks[1] = sync(*tops, *arrived, gu_blocks[1])
            elif k == 1:
                tops[0], tops[1], arrived[0], arrived[1], full_out, *cot_pieces = sync(*tops, *arrived, full_out, *cot_pieces)
                cot_pieces = plane_gather_more(*cot_pieces)
            elif k == 2:
                tops[0], tops[1], arrived[0], arrived[1], *cot_pieces = sync(*tops, *arrived, *cot_pieces)
            else:
                tops[0], tops[1], arrived[0], arrived[1] = sync(*tops, *arrived)
            for m in range(micro):
                states[m] = [tops[m], states[m][1]]
                kv_pieces[m].append(arrived[m])
                kv_windows[m].append(arrived[m])
    kv_there = [pieces[-1] for pieces in kv_pieces]
    attended, lse = [state[2] for state in states], [state[4] for state in states]
    attn_low = jnp.concatenate([state[3] for state in states], axis=0)
    gathered_cot = plane_gather_end(*cot_pieces)

    gu_blocks[1], down_block, rope_place = sync(gu_blocks[1], w_down, rope_place, *kv_there)[:3]
    down_blocks = [down_block, along(down_block, 1, True)]
    branch_split = dot_split(attn_low, full_out)
    branch_split = sync(*branch_split, down_blocks[1])
    down_blocks[1] = branch_split.pop()
    gu_blocks.append(along(after(gu_blocks[1], down_blocks[1]), 1, True))
    *got, gu_blocks[2] = sync(*plane_sum_start(branch_split), gu_blocks[2])
    down_blocks.append(along(after(down_blocks[1], gu_blocks[2]), 1, True))
    cos_all, sin_all = tables(after(rope_place, gu_blocks[2]))
    *got, down_blocks[2], cos_all, sin_all = sync(*plane_sum_more(branch_split, *got), down_blocks[2], cos_all, sin_all)
    layer_in = own_in.astype(f32)
    middle = layer_in + plane_sum_end(branch_split, *got)
    scale_two = rms_scale(middle)
    pieces = plane_gather_start((middle * scale_two * gain_two).astype(bf16))
    for k in range(2, size - 1):
        down_blocks.append(along(down_blocks[k], 1, True))
    *pieces, down_blocks[-1] = sync(*pieces, down_blocks[-1])
    for k in range(2, size - 1):
        gu_blocks.append(along(after(gu_blocks[k], down_blocks[-1]), 1, True))
    *pieces, gu_blocks[-1] = sync(*plane_gather_more(*pieces), gu_blocks[-1])
    normed_two = plane_gather_end(*pieces)

    gu_all = gu_blocks + [other_core(block) for block in gu_blocks]
    down_all = down_blocks + [other_core(block) for block in down_blocks]
    hidden, *outs = ffn(index, normed_two, gathered_cot, gu_all, down_all)
    normed_split, (gu_theirs, gu_mine, down_theirs, down_mine) = outs[:4], outs[4:]
    got = plane_sum_start(normed_split)
    gu_half = core_sum(gu_mine, other_core(gu_theirs)).reshape(size, -1, 2 * ff_part)
    down_half = core_sum(down_mine, other_core(down_theirs)).reshape(size, -1, width)
    gu_total, down_total = ring_part(gu_half, size - 1), ring_part(down_half, size - 1)
    *got, gu_total, down_total = sync(*got, gu_total, down_total)
    gu_moved, down_moved = along(gu_total, -1, True), along(down_total, -1, True)
    got = sync(*plane_sum_more(normed_split, *got))
    grad_normed_two = plane_sum_end(normed_split, *got)
    grad_y = own_cot.astype(f32)
    grad_gain_two = jnp.sum(grad_normed_two * middle * scale_two, axis=(0, 1))
    weighted = grad_normed_two * gain_two
    grad_middle = (
        grad_y
        + scale_two * weighted
        - middle * scale_two**3 * jnp.mean(middle * weighted, axis=-1, keepdims=True)
    )
    pieces = plane_gather_start(grad_middle.astype(bf16))
    *pieces, gu_moved, down_moved = sync(*pieces, gu_moved, down_moved)
    gu_total, down_total = ring_add(gu_half, gu_moved, size - 2), ring_add(down_half, down_moved, size - 2)
    gu_moved, down_moved = along(gu_total, -1, True), along(down_total, -1, True)
    full_down = assemble(index, [after(down_all[0], gu_total)] + down_all[1:])
    result_split = dot_split(after(hidden, gu_total), full_down)
    pieces = plane_gather_more(*pieces)
    for k in range(size - 3, -1, -1):
        gu_total, down_total = ring_add(gu_half, gu_moved, k), ring_add(down_half, down_moved, k)
        if k == size - 3:
            *pieces, gu_total, down_total, result_split[0] = sync(*pieces, gu_total, down_total, result_split[0])
        if k > 0:
            gu_moved, down_moved = along(gu_total, -1, True), along(down_total, -1, True)
    sum_gu, sum_down = gu_total, down_total
    grad_branch = plane_gather_end(*pieces)
    grad_attn = dot_nt(grad_branch, full_out).astype(bf16)

    attended[-1] = after(attended[-1], sum_down)
    states = [[(grad_attn, (chunk, q_part), (m, 0)), attended[m]] for m in range(micro)]
    grad_query = [None] * micro
    terms = [None] * micro
    for k in range(size - 1, -1, -1):
        first = k == size - 1
        for m in range(micro):
            outs = attend_back(
                m, k, first, k == 0, info, q_rot[m], kv_windows[m][k], lse[m], qpos, qbeg[m], kpos,
                (cos_all, (None, None, chunk, LANES), (m, k, 0, 0)), (sin_all, (None, None, chunk, LANES), (m, k, 0, 0)),
                e4, states[m] if first else states[m] + [moved[m]],
            )
            states[m] = outs[:3] if first else states[m][:2] + [outs[0]]
            terms[m] = outs[3] if first else outs[1]
            if k == 0:
                grad_query[m] = outs[-1]
        if k > 0:
            moved = [along(term, -1, False) for term in terms]
            moved[0] = after(moved[0], terms[-1], *([sum_gu, sum_down] if first else []))
        if first:
            got = plane_sum_start(sync(*result_split[:2], *terms)[:2])
        elif k == size - 2:
            moved[-1], *got = sync(moved[-1], *got)
            got = plane_sum_more(result_split, *got)
            term_out = dot_tn(attn_low, after(grad_branch, *got[:2])).astype(bf16)
        elif k == size - 3:
            moved[-1], term_out, *got = sync(moved[-1], term_out, *got)
            output = (middle + plane_sum_end(result_split, *got)).astype(bf16)
            term_out = plane_swap(after(term_out, output), 1, 0)

    grad_qkv = jnp.concatenate([jnp.concatenate(grad_query, axis=0), jnp.concatenate(terms, axis=0)], axis=1)
    out_mine, out_other = core_halves(term_out)
    *part_split, gain_rows, qkv_theirs, qkv_mine = project_back(index, grad_qkv, full_qkv, normed_one, gathered_in, in_scale)
    got = plane_sum_start(part_split)
    gain_terms = jnp.stack([gain_rows[0], grad_gain_two]).astype(bf16)
    gain_terms = jnp.pad(gain_terms, ((0, LANES - 2), (0, 0))).T
    gain_mine, gain_other = core_halves(gain_terms)
    qkv_half = core_sum(qkv_mine, other_core(qkv_theirs)).reshape(size, shard_rows * PLANE, -1)
    last_half = jnp.concatenate([qkv_half, core_sum(out_mine, out_other), core_sum(gain_mine, gain_other)], axis=-1)
    last_total = ring_part(last_half, size - 1)
    sum_gu = plane_swap(after(sum_gu, last_total), 0, 1)
    for k in range(size - 2, -1, -1):
        last_moved = along(last_total, -1, True)
        if k == size - 2:
            *got, last_moved = sync(*got, last_moved)
            got = plane_sum_more(part_split, *got)
        elif k == size - 3:
            *got, last_moved, sum_gu = sync(*got, last_moved, sum_gu)
        last_total = ring_add(last_half, last_moved, k)
    grad_normed_one = plane_sum_end(part_split, *got)
    last_total = plane_swap(last_total, 0, 1).astype(f32).reshape(shard_rows, PLANE, -1)
    scale_one = rms_scale(layer_in)
    weighted = grad_normed_one * gain_one
    input_grad = (
        grad_middle
        + scale_one * weighted
        - layer_in * scale_one**3 * jnp.mean(layer_in * weighted, axis=-1, keepdims=True)
    )
    sum_gu = sum_gu.astype(f32).reshape(shard_rows, PLANE, FF_TILES, 2, ff_part // FF_TILES)
    cuts = np.cumsum([q_part, kv_part, kv_part, out_part])
    sum_query, sum_key, sum_value, sum_out, gain_sum = jnp.split(last_total, cuts, axis=2)
    gain_sum = jnp.sum(gain_sum, axis=1)
    return (
        output[:, None],
        input_grad[:, None],
        gain_sum[:, 0],
        gain_sum[:, 1],
        sum_query.reshape(shard_rows, -1),
        sum_key.reshape(shard_rows, -1),
        sum_value.reshape(shard_rows, -1),
        sum_out.reshape(shard_rows, -1),
        from_ff_parts(sum_gu[:, :, :, 0]),
        from_ff_parts(sum_gu[:, :, :, 1]),
        sum_down.astype(f32),
    )


def solution(mesh):
    blocks = mesh.shape["blk"]
    grid = Mesh(mesh.devices.reshape(2, blocks // PLANE, PLANE), ("stream", "zed", "plane"))
    tokens = P(None, "stream", ("zed", "plane"), None)
    vector = P(("stream", "zed", "plane"))
    matrix = P(("stream", "zed", "plane"), None)
    return jax.shard_map(
        on_device,
        mesh=grid,
        in_specs=(tokens, tokens, P(None, "stream", None), vector, vector) + (matrix,) * 7,
        out_specs=(tokens, tokens, vector, vector) + (matrix,) * 7,
        check_vma=False,
    )
```

```python
import math

import jax
import jax.numpy as jnp
import numpy as np
from jax import lax
from jax.experimental import pallas as pl
from jax.experimental.pallas import tpu as pltpu
from jax.sharding import Mesh
from jax.sharding import PartitionSpec as P

HQ = 16
HK = 8
DH = 96
PLANE = 4
FF_TILES = 2
LANES = 128
VMEM_BYTES = 50 * 1024 * 1024

epsilon = 1e-05
rope_base = 100000.0
masked_score = -1e30
score_scale = 1.0 / math.sqrt(DH)
exp2_scale = score_scale * math.log2(math.e)

LIGHT = pl.CostEstimate(flops=1, bytes_accessed=1, transcendentals=0)
CHUNK_COST = pl.CostEstimate(flops=1, bytes_accessed=6000000, transcendentals=0)

f32 = jnp.float32
bf16 = jnp.bfloat16


def spread(heads):
    table = np.zeros((heads * DH, heads * LANES), np.float32)
    for head in range(heads):
        for i in range(DH):
            lane = i if i < DH // 2 else i + (LANES - DH) // 2
            table[head * DH + i, head * LANES + lane] = 1.0
    return jnp.asarray(table, bf16)


def rms_scale(values):
    return lax.rsqrt(jnp.mean(values * values, axis=-1, keepdims=True) + epsilon)


def dot(a, b):
    return jnp.dot(a, b, preferred_element_type=f32)


def dot_nt(a, b):
    return lax.dot_general(a, b, (((1,), (1,)), ((), ())), preferred_element_type=f32)


def dot_tn(a, b):
    return lax.dot_general(a, b, (((0,), (0,)), ((), ())), preferred_element_type=f32)


def project_kernel(size, info_ref, x_ref, cos_ref, sin_ref, e4_ref, e8_ref, *rest):
    blocks, (n_ref, q_ref, kv_ref, w_ref, out_w_ref, gains_ref, scale_ref, pad_s) = rest[: 2 * size], rest[2 * size :]
    rows = blocks[0].shape[0]
    heads = 8 * DH

    @pl.when(pl.program_id(0) == 0)
    def _():
        for i, block in enumerate(blocks):
            core = info_ref[1] if i < size else 1 - info_ref[1]
            start = pl.multiple_of((core * size + lax.rem(info_ref[0] - i % size + size, size)) * rows, rows)
            w_ref[pl.ds(start, rows), :] = block[:, : heads + LANES]
            out_w_ref[pl.ds(start, rows), :] = block[:, heads + LANES :]
            pad_s[pl.ds(start, rows), :] = dot(block[:, :heads], e8_ref[...]).astype(bf16)
        rows_to = lax.broadcasted_iota(jnp.int32, (LANES, LANES), 0)
        same = (rows_to == lax.broadcasted_iota(jnp.int32, (LANES, LANES), 1)).astype(bf16)
        gains_ref[...] = dot_nt(same[:8], w_ref[:, heads:])

    x = x_ref[...].astype(f32)
    scale = rms_scale(x)
    scale_ref[...] = scale
    normed = (x * scale * gains_ref[0:1, :]).astype(bf16)
    n_ref[...] = normed
    pre = dot(normed, pad_s[...])
    cos, sin = cos_ref[...], sin_ref[...]
    parts = []
    for head in range(8):
        piece = pre[:, head * LANES : (head + 1) * LANES]
        if head < 6:
            piece = piece * cos + pltpu.roll(piece, LANES // 2, 1) * sin
        parts.append(piece.astype(bf16))
    q_ref[...] = jnp.concatenate(parts[:4], axis=1)
    kv_ref[...] = dot_nt(jnp.concatenate(parts[4:], axis=1), e4_ref[...]).astype(bf16)


def project(info, x, blocks, cos, sin, e4, e8):
    rows, width = x.shape
    step = min(256, rows)
    size = len(blocks) // 2
    cols = blocks[0].shape[1]
    first = 8 * DH + LANES
    whole = lambda a: pl.BlockSpec(a.shape, lambda i, n: (0,) * a.ndim)
    by_row = lambda c: pl.BlockSpec((step, c), lambda i, n: (i, 0))
    return pl.pallas_call(
        lambda *refs: project_kernel(size, *refs),
        grid_spec=pltpu.PrefetchScalarGridSpec(
            num_scalar_prefetch=1,
            grid=(rows // step,),
            in_specs=[by_row(width), by_row(LANES), by_row(LANES), whole(e4), whole(e8)] + [whole(b) for b in blocks],
            out_specs=[
                by_row(width),
                by_row(4 * LANES),
                by_row(4 * DH),
                pl.BlockSpec((width, first), lambda i, n: (0, 0)),
                pl.BlockSpec((width, cols - first), lambda i, n: (0, 0)),
                pl.BlockSpec((8, width), lambda i, n: (0, 0)),
                by_row(1),
            ],
            scratch_shapes=[pltpu.VMEM((width, 8 * LANES), bf16)],
        ),
        out_shape=[
            jax.ShapeDtypeStruct((rows, width), bf16),
            jax.ShapeDtypeStruct((rows, 4 * LANES), bf16),
            jax.ShapeDtypeStruct((rows, 4 * DH), bf16),
            jax.ShapeDtypeStruct((width, first), bf16),
            jax.ShapeDtypeStruct((width, cols - first), bf16),
            jax.ShapeDtypeStruct((8, width), f32),
            jax.ShapeDtypeStruct((rows, 1), f32),
        ],
        compiler_params=pltpu.CompilerParams(vmem_limit_bytes=VMEM_BYTES),
        cost_estimate=LIGHT,
        name="project",
    )(info, x, cos, sin, e4, e8, *blocks)


def assemble_kernel(size, info_ref, *rest):
    blocks, out_ref = rest[: 2 * size], rest[2 * size]
    rows = blocks[0].shape[0]
    for i, block in enumerate(blocks):
        core = info_ref[1] if i < size else 1 - info_ref[1]
        start = pl.multiple_of((core * size + lax.rem(info_ref[0] - i % size + size, size)) * rows, rows)
        out_ref[pl.ds(start, rows), :] = block[...]


def assemble(info, blocks):
    size = len(blocks) // 2
    rows, width = blocks[0].shape
    step = width // 3 if width % 384 == 0 else width // 4
    return pl.pallas_call(
        lambda *refs: assemble_kernel(size, *refs),
        grid_spec=pltpu.PrefetchScalarGridSpec(
            num_scalar_prefetch=1,
            grid=(width // step,),
            in_specs=[pl.BlockSpec((rows, step), lambda i, n: (0, i)) for _ in blocks],
            out_specs=pl.BlockSpec((len(blocks) * rows, step), lambda i, n: (0, i)),
        ),
        out_shape=jax.ShapeDtypeStruct((len(blocks) * rows, width), blocks[0].dtype),
        compiler_params=pltpu.CompilerParams(vmem_limit_bytes=VMEM_BYTES),
        cost_estimate=LIGHT,
        name="assemble",
    )(info, *blocks)


def allowed_of(info_ref, k, chunk, qpos_ref, qbeg_ref, kpos_ref):
    kpos = kpos_ref[...] + (info_ref[0] - k) * chunk
    return (kpos <= qpos_ref[...]) & (kpos >= qbeg_ref[...])


def useful_of(info_ref, m, k, chunk):
    z = info_ref[0]
    return (k <= z) & ((z - k + 1) * chunk - 1 >= info_ref[2 + m])


def stack_heads(block, h):
    return jnp.concatenate(
        [block[:, (2 * h) * LANES : (2 * h + 1) * LANES], block[:, (2 * h + 1) * LANES : (2 * h + 2) * LANES]], axis=0
    )


def run_kernel(body, info, inputs, outs, aliases, name):
    def spec(entry):
        if isinstance(entry, tuple):
            return pl.BlockSpec(entry[1], lambda i, n: entry[2])
        return pl.BlockSpec(entry.shape, lambda i, n: (0,) * entry.ndim)

    return list(
        pl.pallas_call(
            body,
            grid_spec=pltpu.PrefetchScalarGridSpec(
                num_scalar_prefetch=1,
                grid=(1,),
                in_specs=[spec(entry) for entry in inputs],
                out_specs=[pl.BlockSpec(o.shape, lambda i, n, o=o: (0,) * len(o.shape)) for o in outs],
            ),
            out_shape=outs,
            input_output_aliases=aliases,
            compiler_params=pltpu.CompilerParams(vmem_limit_bytes=VMEM_BYTES),
            cost_estimate=CHUNK_COST,
            name=name,
        )(info, *[entry[0] if isinstance(entry, tuple) else entry for entry in inputs])
    )


def attend_kernel(m, k, last, info_ref, q_ref, kv_ref, qpos_ref, qbeg_ref, kpos_ref, e_ref, *rest):
    chunk = kv_ref.shape[0]
    if k > 0:
        top_in, acc_in, rest = rest[0], rest[1], rest[2:]
    top_ref, acc_ref = rest[0], rest[1]

    def run():
        allowed = allowed_of(info_ref, k, chunk, qpos_ref, qbeg_ref, kpos_ref)
        kv = kv_ref[...]
        q = q_ref[...]
        one_lane = (lax.broadcasted_iota(jnp.int32, (1, LANES), 1) == DH // 2).astype(f32)
        for h in range(2):
            keys = dot(kv, e_ref[:, h * LANES : (h + 1) * LANES]).astype(bf16)
            vals = (dot(kv, e_ref[:, (2 + h) * LANES : (3 + h) * LANES]) + one_lane).astype(bf16)
            s = jnp.where(allowed, dot_nt(keys, stack_heads(q, h)), masked_score)
            new = jnp.max(s, axis=0, keepdims=True)
            if k > 0:
                old = top_in[h]
                new = jnp.maximum(old, new)
            w = jnp.where(allowed, jnp.exp2((s - new) * exp2_scale), 0.0).astype(bf16)
            acc = dot_tn(vals, w)
            if k > 0:
                acc = acc_in[h] * jnp.exp2((old - new) * exp2_scale) + acc
            acc_ref[h] = acc
            top_ref[h] = new

    if k == 0:
        run()
    else:
        useful = useful_of(info_ref, m, k, chunk)
        pl.when(useful)(run)

        @pl.when(jnp.logical_not(useful))
        def _():
            top_ref[...] = top_in[...]
            acc_ref[...] = acc_in[...]

    if last:
        att_ref, low_ref, lse_ref = rest[2:]
        parts = []
        for h in range(2):
            acc = acc_ref[h]
            total = acc[DH // 2 : DH // 2 + 1, :]
            lse_ref[h] = top_ref[h] * exp2_scale + jnp.log2(total)
            flat = (acc / total).T
            rows = flat.shape[0] // 2
            parts += [flat[:rows], flat[rows:]]
        att = jnp.concatenate(parts, axis=1)
        att_ref[...] = att
        low_ref[...] = dot_nt(att.astype(bf16), e_ref[...]).astype(bf16)


def attend(m, k, last, info, q, kv, qpos, qbeg, kpos, e4, state):
    rows = q[1][0]
    outs = [jax.ShapeDtypeStruct((2, 1, 2 * rows), f32), jax.ShapeDtypeStruct((2, LANES, 2 * rows), f32)]
    if last:
        outs += [
            jax.ShapeDtypeStruct((rows, 4 * LANES), f32),
            jax.ShapeDtypeStruct((rows, 4 * DH), bf16),
            jax.ShapeDtypeStruct((2, 1, 2 * rows), f32),
        ]
    return run_kernel(
        lambda *refs: attend_kernel(m, k, last, *refs),
        info,
        [q, kv, qpos, qbeg, kpos, e4] + state,
        outs,
        {7: 0, 8: 1} if k > 0 else {},
        "attend",
    )


def attend_back_kernel(
    m, k, first, last, info_ref, q_ref, kv_ref, lse_ref, qpos_ref, qbeg_ref, kpos_ref, cosk_ref, sink_ref, e_ref, *rest
):
    chunk = kv_ref.shape[0]
    if first:
        g_ref, att_ref, rest = rest[0], rest[1], rest[2:]
        go_ref, delta_ref, dq_ref, dkv_ref = rest[:4]
        go = dot(g_ref[...], e_ref[...])
        for h in range(2):
            go_h = stack_heads(go, h)
            go_ref[h] = go_h.astype(bf16)
            prod = go_h * stack_heads(att_ref[...], h)
            delta_ref[h] = jnp.sum(prod.T, axis=0, keepdims=True)
    else:
        go_ref, delta_ref, dq_in, moved_ref, rest = rest[0], rest[1], rest[2], rest[3], rest[4:]
        dq_ref, dkv_ref = rest[:2]

    def run():
        allowed = allowed_of(info_ref, k, chunk, qpos_ref, qbeg_ref, kpos_ref)
        kv = kv_ref[...]
        q = q_ref[...]
        cosk, sink = cosk_ref[...], sink_ref[...]
        grad_keys, grad_vals = [], []
        for h in range(2):
            keys = dot(kv, e_ref[:, h * LANES : (h + 1) * LANES]).astype(bf16)
            vals = dot(kv, e_ref[:, (2 + h) * LANES : (3 + h) * LANES]).astype(bf16)
            q_h = stack_heads(q, h)
            go_h = go_ref[h]
            s = dot_nt(keys, q_h)
            w = jnp.where(allowed, jnp.exp2(s * exp2_scale - lse_ref[h]), 0.0)
            grad_vals.append(dot(w.astype(bf16), go_h).astype(bf16))
            ds = (w * (dot_nt(vals, go_h) - delta_ref[h])).astype(bf16)
            dq = dot_tn(keys, ds)
            dq_ref[h] = dq if first else dq_in[h] + dq
            gk = dot(ds, q_h) * score_scale
            gk = gk * cosk + pltpu.roll(gk * sink, LANES // 2, 1)
            grad_keys.append(gk.astype(bf16))
        total = dot_nt(jnp.concatenate(grad_keys + grad_vals, axis=1), e_ref[...])
        if not first:
            total = total + moved_ref[...].astype(f32)
        dkv_ref[...] = total.astype(bf16)

    if k == 0:
        run()
    else:
        useful = useful_of(info_ref, m, k, chunk)
        pl.when(useful)(run)

        @pl.when(jnp.logical_not(useful))
        def _():
            dkv_ref[...] = jnp.zeros(dkv_ref.shape, bf16) if first else moved_ref[...]
            dq_ref[...] = jnp.zeros(dq_ref.shape, f32) if first else dq_in[...]

    if last:
        out_ref = rest[-1]
        parts = []
        for h in range(2):
            flat = dq_ref[h].T * score_scale
            rows = flat.shape[0] // 2
            for piece in (flat[:rows], flat[rows:]):
                parts.append((piece * cosk_ref[...] + pltpu.roll(piece * sink_ref[...], LANES // 2, 1)).astype(bf16))
        out_ref[...] = dot_nt(jnp.concatenate(parts, axis=1), e_ref[...]).astype(bf16)


def attend_back(m, k, first, last, info, q, kv, lse, qpos, qbeg, kpos, cosk, sink, e4, state):
    rows = q[1][0]
    outs = []
    if first:
        outs += [jax.ShapeDtypeStruct((2, 2 * rows, LANES), bf16), jax.ShapeDtypeStruct((2, 1, 2 * rows), f32)]
    outs += [jax.ShapeDtypeStruct((2, LANES, 2 * rows), f32), jax.ShapeDtypeStruct((rows, 4 * DH), bf16)]
    if last:
        outs += [jax.ShapeDtypeStruct((rows, 4 * DH), bf16)]
    return run_kernel(
        lambda *refs: attend_back_kernel(m, k, first, last, *refs),
        info,
        [q, kv, lse, qpos, qbeg, kpos, cosk, sink, e4] + state,
        outs,
        {} if first else {12: 0},
        "attend_back",
    )


def store_split(sum_of, tok_rows, first_ref, second_ref, keep_first_ref, keep_second_ref):
    for i, slot in enumerate((1, 3)):
        first_ref[i] = sum_of(slot * tok_rows, tok_rows).astype(bf16)
        keep_first_ref[i] = sum_of((slot - 1) * tok_rows, tok_rows)
    for i in range(2):
        second_ref[i] = sum_of((PLANE + 2 + i) * tok_rows, tok_rows).astype(bf16)
        keep_second_ref[i] = sum_of((PLANE + i) * tok_rows, tok_rows)


def split_outs(tok_rows, width):
    return [jax.ShapeDtypeStruct((2, tok_rows, width), kind) for kind in (bf16, bf16, f32, f32)]


def dot_split_kernel(tok_rows, a_ref, w_ref, *rest):
    acc_s = rest[-1]
    acc_s[...] = dot(a_ref[...], w_ref[...])
    store_split(lambda start, n: acc_s[start : start + n, :], tok_rows, *rest[:-1])


def dot_split(a, w):
    rows, inner = a.shape
    tok_rows = rows // (2 * PLANE)
    width = w.shape[1]
    step = width // 3
    outs = split_outs(tok_rows, width)
    return list(
        pl.pallas_call(
            lambda *refs: dot_split_kernel(tok_rows, *refs),
            grid=(3,),
            in_specs=[pl.BlockSpec((rows, inner), lambda i: (0, 0)), pl.BlockSpec((inner, step), lambda i: (0, i))],
            out_specs=[pl.BlockSpec((2, tok_rows, step), lambda i: (0, 0, i)) for _ in outs],
            out_shape=outs,
            scratch_shapes=[pltpu.VMEM((rows, step), f32)],
            compiler_params=pltpu.CompilerParams(vmem_limit_bytes=VMEM_BYTES),
            cost_estimate=LIGHT,
            name="dot_split",
        )(a, w)
    )


def ffn_kernel(size, tok_rows, info_ref, n_ref, g_ref, *rest):
    gu_blocks, down_blocks, rest = rest[: 2 * size], rest[2 * size : 4 * size], rest[4 * size :]
    hidden_ref, *outs = rest[:5]
    gu_theirs_ref, gu_mine_ref, down_theirs_ref, down_mine_ref = rest[5:9]
    gu_s, down_s, acc_s, flat_s, grad_s = rest[9:]
    f, last = pl.program_id(0), pl.num_programs(0) - 1
    units = hidden_ref.shape[1]
    half = flat_s.shape[0] // 2

    def place(i, rows):
        core = info_ref[1] if i < size else 1 - info_ref[1]
        return pl.ds(pl.multiple_of((core * size + lax.rem(info_ref[0] - i % size + size, size)) * rows, rows), rows)

    @pl.when(f == 0)
    def _():
        acc_s[...] = jnp.zeros(acc_s.shape, f32)
        flat_s[...] = n_ref[...].T
        for i, block in enumerate(down_blocks):
            down_s[place(i, block.shape[0]), :] = block[...]

    for i, block in enumerate(gu_blocks):
        gu_s[place(i, block.shape[0]), :] = block[...]
    w_down = down_s.at[pl.ds(pl.multiple_of(f * units, units), units)]
    step = 4 * tok_rows

    @pl.loop(0, n_ref.shape[0] // step)
    def _(r):
        at = pl.ds(pl.multiple_of(r * step, step), step)
        pre = dot(n_ref[at, :], gu_s[...])
        grad_hidden = dot_nt(g_ref[at, :], w_down[...])
        gate_pre, up_pre = pre[:, :units], pre[:, units:]
        sigmoid_gate = jax.nn.sigmoid(gate_pre)
        silu_gate = gate_pre * sigmoid_gate
        hidden_ref[at, :] = (silu_gate * up_pre).astype(bf16)
        grad_gate = grad_hidden * up_pre * sigmoid_gate * (1.0 + gate_pre * (1.0 - sigmoid_gate))
        both = jnp.concatenate([grad_gate.astype(bf16), (grad_hidden * silu_gate).astype(bf16)], axis=1)
        grad_s[at, :] = both
        acc_s[at, :] += dot_nt(both, gu_s[...])

    core = info_ref[1]
    gu_mine_ref[...] = dot(flat_s[pl.ds(pl.multiple_of(core * half, half), half), :], grad_s[...]).astype(bf16)
    gu_theirs_ref[...] = dot(flat_s[pl.ds(pl.multiple_of((1 - core) * half, half), half), :], grad_s[...]).astype(bf16)
    term_down = dot_tn(hidden_ref[...], g_ref[...]).astype(bf16)
    is_mine = lax.div(f, pl.num_programs(0) // 2) == core

    @pl.when(is_mine)
    def _():
        down_mine_ref[...] = term_down

    @pl.when(jnp.logical_not(is_mine))
    def _():
        down_theirs_ref[...] = term_down

    @pl.when(f == last)
    def _():
        store_split(lambda start, n: acc_s[start : start + n, :], tok_rows, *outs)


def ffn(info, normed, grad_mlp, gu_blocks, down_blocks):
    rows, width = normed.shape
    size = len(gu_blocks) // 2
    tok_rows = rows // (2 * PLANE)
    ff_part = gu_blocks[0].shape[1] // 2
    units = ff_part // FF_TILES
    whole = lambda a: pl.BlockSpec(a.shape, lambda f, n: (0,) * a.ndim, pipeline_mode=pl.Buffered(1))
    outs = split_outs(tok_rows, width)
    gu_half = pl.BlockSpec((width // 2, 2 * units), lambda f, n: (0, f))

    def down_half(core_of):
        return pl.BlockSpec((units, width), lambda f, n: (jnp.clip(f - core_of(n) * (FF_TILES // 2), 0, FF_TILES // 2 - 1), 0))

    return list(
        pl.pallas_call(
            lambda *refs: ffn_kernel(size, tok_rows, *refs),
            grid_spec=pltpu.PrefetchScalarGridSpec(
                num_scalar_prefetch=1,
                grid=(FF_TILES,),
                in_specs=[whole(normed), whole(grad_mlp)]
                + [pl.BlockSpec((block.shape[0], 2 * units), lambda f, n: (0, f)) for block in gu_blocks]
                + [whole(block) for block in down_blocks],
                out_specs=[pl.BlockSpec((rows, units), lambda f, n: (0, f))]
                + [pl.BlockSpec(o.shape, lambda f, n: (0, 0, 0), pipeline_mode=pl.Buffered(1)) for o in outs]
                + [gu_half, gu_half, down_half(lambda n: 1 - n[1]), down_half(lambda n: n[1])],
                scratch_shapes=[
                    pltpu.VMEM((width, 2 * units), bf16),
                    pltpu.VMEM((ff_part, width), bf16),
                    pltpu.VMEM((rows, width), f32),
                    pltpu.VMEM((width, rows), bf16),
                    pltpu.VMEM((rows, 2 * units), bf16),
                ],
            ),
            out_shape=[jax.ShapeDtypeStruct((rows, ff_part), bf16)]
            + outs
            + [jax.ShapeDtypeStruct((width // 2, 2 * ff_part), bf16)] * 2
            + [jax.ShapeDtypeStruct((ff_part // 2, width), bf16)] * 2,
            compiler_params=pltpu.CompilerParams(vmem_limit_bytes=58 * 1024 * 1024),
            cost_estimate=LIGHT,
            name="ffn",
        )(info, normed, grad_mlp, *gu_blocks, *down_blocks)
    )


def project_back_kernel(tok_rows, info_ref, g_ref, w_ref, n_ref, x_ref, scale_ref, *rest):
    first_ref, second_ref, keep_first_ref, keep_second_ref, gain_ref, theirs_ref, mine_ref, acc_s = rest
    rows = 2 * tok_rows
    total = jnp.zeros((1, acc_s.shape[1]), f32)
    for i in range(g_ref.shape[0] // rows):
        at = slice(i * rows, (i + 1) * rows)
        acc = dot_nt(g_ref[at, :], w_ref[...])
        acc_s[at, :] = acc
        total = total + jnp.sum(acc * x_ref[at, :].astype(f32) * scale_ref[at, :], axis=0, keepdims=True)
    gain_ref[...] = jnp.broadcast_to(total, gain_ref.shape)
    store_split(lambda start, n: acc_s[start : start + n, :], tok_rows, first_ref, second_ref, keep_first_ref, keep_second_ref)
    term = dot_tn(n_ref[...], g_ref[...]).astype(bf16)
    is_mine = pl.program_id(0) == info_ref[1]

    @pl.when(is_mine)
    def _():
        mine_ref[...] = term

    @pl.when(jnp.logical_not(is_mine))
    def _():
        theirs_ref[...] = term


def project_back(info, grads, w, normed, x, scale):
    rows, inner = grads.shape
    tok_rows = rows // (2 * PLANE)
    width = w.shape[0]
    half = width // 2
    outs = split_outs(tok_rows, width)
    column = pl.BlockSpec((rows, half), lambda i, n: (0, i))
    out_whole = pl.BlockSpec((half, inner), lambda i, n: (0, 0))
    return list(
        pl.pallas_call(
            lambda *refs: project_back_kernel(tok_rows, *refs),
            grid_spec=pltpu.PrefetchScalarGridSpec(
                num_scalar_prefetch=1,
                grid=(2,),
                in_specs=[
                    pl.BlockSpec((rows, inner), lambda i, n: (0, 0)),
                    pl.BlockSpec((half, inner), lambda i, n: (i, 0)),
                    column,
                    column,
                    pl.BlockSpec((rows, 1), lambda i, n: (0, 0)),
                ],
                out_specs=[pl.BlockSpec((2, tok_rows, half), lambda i, n: (0, 0, i)) for _ in outs]
                + [pl.BlockSpec((8, half), lambda i, n: (0, i)), out_whole, out_whole],
                scratch_shapes=[pltpu.VMEM((rows, half), f32)],
            ),
            out_shape=outs
            + [jax.ShapeDtypeStruct((8, width), f32)]
            + [jax.ShapeDtypeStruct((half, inner), bf16)] * 2,
            compiler_params=pltpu.CompilerParams(vmem_limit_bytes=VMEM_BYTES),
            cost_estimate=LIGHT,
            name="project_back",
        )(info, grads, w, normed, x, scale)
    )


def beside(value, bit):
    return lax.ppermute(value, "plane", [(i, i ^ bit) for i in range(PLANE)])


def other_core(value):
    return lax.ppermute(value, "stream", [(0, 1), (1, 0)])


def along(value, step, wrap):
    size = lax.axis_size("zed")
    pairs = [(i, (i + step) % size) for i in range(size) if wrap or 0 <= i + step < size]
    return lax.ppermute(value, "zed", pairs)


def plane_gather_start(own):
    return [own[0], own[1], beside(own[0], 1), beside(own[1], 2)]


def plane_gather_more(first, second, first_got, second_got):
    pair_one, pair_two = jnp.stack([first, first_got]), jnp.stack([second, second_got])
    return [pair_one, pair_two, beside(pair_one, 2), beside(pair_two, 1)]


def plane_gather_end(pair_one, pair_two, first_more, second_more):
    blocks = [pair_one, first_more, pair_two[:1], second_more[:1], pair_two[1:], second_more[1:]]
    return jnp.concatenate(blocks).reshape(-1, pair_one.shape[-1])


def plane_sum_start(split):
    return [beside(split[0], 1), beside(split[1], 2)]


def plane_sum_more(split, got_first, got_second):
    keep_first, keep_second = split[2], split[3]
    more_first = beside((keep_first[1] + got_first[1]).astype(bf16), 2)
    more_second = beside((keep_second[1] + got_second[1]).astype(bf16), 1)
    return [got_first[0], got_second[0], more_first, more_second]


def plane_sum_end(split, got_first, got_second, more_first, more_second):
    return jnp.stack([split[2][0] + got_first + more_first, split[3][0] + got_second + more_second])


def after(value, *earlier):
    return lax.optimization_barrier((value,) + earlier)[0]


def sync(*values):
    return list(lax.optimization_barrier(values))


def core_halves(full):
    size = lax.axis_size("zed")
    s = lax.axis_index("stream")
    full = full.reshape((2, size, -1) + full.shape[1:])
    mine = lax.dynamic_index_in_dim(full, s, 0, keepdims=False)
    theirs = lax.dynamic_index_in_dim(full, 1 - s, 0, keepdims=False)
    return mine, other_core(theirs)


def core_sum(mine, other):
    return (mine.astype(f32) + other.astype(f32)).astype(bf16)


def ring_part(half, k):
    size = lax.axis_size("zed")
    z = lax.axis_index("zed")
    return lax.dynamic_index_in_dim(half, lax.rem(z - k + size, size), 0, keepdims=False)


def ring_add(half, moved, k):
    return (moved.astype(f32) + ring_part(half, k).astype(f32)).astype(bf16)


def plane_swap(value, split, concat):
    return lax.all_to_all(value, "plane", split_axis=split, concat_axis=concat, tiled=True)


def on_device(inputs, cotangent, seq_lengths, gain_attn, gain_ffn, w_query, w_key, w_value, w_out, w_gate, w_up, w_down):
    size = lax.axis_size("zed")
    s, z, p = lax.axis_index("stream"), lax.axis_index("zed"), lax.axis_index("plane")
    micro, _, tok_rows, width = inputs.shape
    chunk = PLANE * tok_rows
    tokens = micro * chunk
    shard_rows = w_query.shape[0]
    ff_block = w_down.shape[0]
    ff_blocks = 2 * size
    ff_part = ff_blocks * ff_block
    q_part, kv_part = HQ * DH // PLANE, HK * DH // PLANE
    out_part = width // PLANE
    e4, e8 = spread(4), spread(8)

    def by_part(weight):
        return weight.reshape(shard_rows, PLANE, -1)

    def by_ff_part(weight):
        return weight.reshape(shard_rows, ff_blocks, PLANE, ff_block).transpose(0, 2, 1, 3).reshape(shard_rows, PLANE, -1)

    def from_ff_parts(term):
        return term.reshape(shard_rows, PLANE, ff_blocks, ff_block).transpose(0, 2, 1, 3).reshape(shard_rows, -1)

    own_in = inputs[:, 0]
    own_cot = cotangent[:, 0]
    gains = jnp.stack([gain_attn, gain_ffn], axis=1)
    gains = jnp.broadcast_to(jnp.pad(gains, ((0, 0), (0, LANES - 2)))[:, None], (shard_rows, PLANE, LANES))
    qkv_bundle = jnp.concatenate([by_part(w_query), by_part(w_key), by_part(w_value), gains, by_part(w_out)], axis=2)
    qkv_block = plane_swap(qkv_bundle.reshape(shard_rows, -1), 1, 0)
    tiled = (shard_rows, PLANE, FF_TILES, ff_part // FF_TILES)
    ffn_bundle = jnp.stack([by_ff_part(w_gate).reshape(tiled), by_ff_part(w_up).reshape(tiled)], axis=3).reshape(shard_rows, -1)
    qkv_blocks = [qkv_block]
    for _ in range(size - 1):
        qkv_blocks.append(along(qkv_blocks[-1], 1, True))
    qkv_other = [other_core(block) for block in qkv_blocks]
    ffn_block = plane_swap(after(ffn_bundle, qkv_block), 1, 0)
    pieces = sync(*plane_gather_start(after(own_in, qkv_block)))
    gathered_in = plane_gather_end(*sync(*plane_gather_more(*pieces)))
    gu_blocks = [after(ffn_block, qkv_blocks[-1])]
    gu_blocks.append(along(gu_blocks[0], 1, True))

    slot_place = ((jnp.arange(PLANE, dtype=jnp.int32) ^ p)[:, None] * tok_rows + jnp.arange(tok_rows, dtype=jnp.int32)[None, :]).reshape(chunk)
    chunk_place = (z - jnp.arange(size, dtype=jnp.int32))[:, None] * chunk + slot_place[None, :]
    lengths = seq_lengths[:, 0]
    seq_ends = jnp.cumsum(lengths, axis=1)
    begins = jnp.sum(
        jnp.where(seq_ends[:, None, None, :] <= chunk_place[None, :, :, None], lengths[:, None, None, :], 0), axis=-1
    )
    own_begin = begins[:, 0]
    lane = np.arange(LANES)
    place_in_half = lane % (LANES // 2)
    real = place_in_half < DH // 2
    frequency = jnp.where(
        real, rope_base ** (-2.0 * jnp.asarray(np.minimum(place_in_half, DH // 2 - 1), f32) / DH), 0.0
    )
    rope_place = (chunk_place[None] - begins).astype(f32)

    def tables(place):
        angles = jnp.maximum(place, 0.0)[..., None] * frequency
        signs = jnp.asarray(np.where(real, np.where(lane < LANES // 2, -1.0, 1.0), 0.0), f32)
        return jnp.where(real, jnp.cos(angles), 0.0), jnp.sin(angles) * signs

    cos, sin = tables(after(rope_place[:, 0], qkv_block))
    index = jnp.stack([z, s]).astype(jnp.int32)
    info = jnp.concatenate([index, jnp.min(own_begin, axis=1)])
    qpos = jnp.tile(chunk_place[0], 2)[None]
    qbeg = jnp.tile(own_begin, (1, 2))[:, None]
    kpos = slot_place[:, None]

    normed_one, q_rot, kv_own, full_qkv, full_oc, full_gains, in_scale = project(
        index, gathered_in, qkv_blocks + qkv_other, cos.reshape(tokens, LANES), sin.reshape(tokens, LANES), e4, e8
    )
    full_qkv = full_qkv[:, : q_part + 2 * kv_part]
    gain_one, gain_two = full_gains[0:1], full_gains[1:2]
    full_out = plane_swap(full_oc, 0, 1)
    cot_pieces = plane_gather_start(after(own_cot, gathered_in, kv_own))
    q_rot = [(q_rot, (chunk, 4 * LANES), (m, 0)) for m in range(micro)]
    kv_windows = [[(kv_own, (chunk, 4 * DH), (m, 0))] for m in range(micro)]
    kv_pieces = [[piece] for piece in kv_own.reshape(micro, chunk, 4 * DH)]
    qbeg = [(qbeg, (None, 1, 2 * chunk), (m, 0, 0)) for m in range(micro)]
    states = [[] for _ in range(micro)]
    for k in range(size):
        if k < size - 1:
            arrived = [along(kv_pieces[m][k], 1, False) for m in range(micro)]
        for m in range(micro):
            states[m] = attend(m, k, k == size - 1, info, q_rot[m], kv_windows[m][k], qpos, qbeg[m], kpos, e4, states[m])
        if k < size - 1:
            tops = [state[0] for state in states]
            if k == 0:
                tops[0], tops[1], arrived[0], arrived[1], gu_blocks[1], *cot_pieces = sync(
                    *tops, *arrived, gu_blocks[1], *cot_pieces
                )
                cot_pieces = plane_gather_more(*cot_pieces)
            elif k == 1:
                tops[0], tops[1], arrived[0], arrived[1], full_out, *cot_pieces = sync(*tops, *arrived, full_out, *cot_pieces)
            else:
                tops[0], tops[1], arrived[0], arrived[1] = sync(*tops, *arrived)
            for m in range(micro):
                states[m] = [tops[m], states[m][1]]
                kv_pieces[m].append(arrived[m])
                kv_windows[m].append(arrived[m])
    kv_there = [pieces[-1] for pieces in kv_pieces]
    attended, lse = [state[2] for state in states], [state[4] for state in states]
    attn_low = jnp.concatenate([state[3] for state in states], axis=0)
    gathered_cot = plane_gather_end(*cot_pieces)

    gu_blocks[1], down_block, rope_place = sync(gu_blocks[1], w_down, rope_place, *kv_there)[:3]
    down_blocks = [down_block, along(down_block, 1, True)]
    branch_split = dot_split(attn_low, full_out)
    branch_split = sync(*branch_split, down_blocks[1])
    down_blocks[1] = branch_split.pop()
    gu_blocks.append(along(after(gu_blocks[1], down_blocks[1]), 1, True))
    *got, gu_blocks[2] = sync(*plane_sum_start(branch_split), gu_blocks[2])
    down_blocks.append(along(after(down_blocks[1], gu_blocks[2]), 1, True))
    cos_all, sin_all = tables(after(rope_place, gu_blocks[2]))
    *got, down_blocks[2], cos_all, sin_all = sync(*plane_sum_more(branch_split, *got), down_blocks[2], cos_all, sin_all)
    layer_in = own_in.astype(f32)
    middle = layer_in + plane_sum_end(branch_split, *got)
    scale_two = rms_scale(middle)
    pieces = plane_gather_start((middle * scale_two * gain_two).astype(bf16))
    for k in range(2, size - 1):
        down_blocks.append(along(down_blocks[k], 1, True))
    *pieces, down_blocks[-1] = sync(*pieces, down_blocks[-1])
    for k in range(2, size - 1):
        gu_blocks.append(along(after(gu_blocks[k], down_blocks[-1]), 1, True))
    *pieces, gu_blocks[-1] = sync(*plane_gather_more(*pieces), gu_blocks[-1])
    normed_two = plane_gather_end(*pieces)

    gu_all = gu_blocks + [other_core(block) for block in gu_blocks]
    down_all = down_blocks + [other_core(block) for block in down_blocks]
    hidden, *outs = ffn(index, normed_two, gathered_cot, gu_all, down_all)
    normed_split, (gu_theirs, gu_mine, down_theirs, down_mine) = outs[:4], outs[4:]
    got = plane_sum_start(normed_split)
    gu_half = core_sum(gu_mine, other_core(gu_theirs)).reshape(size, -1, 2 * ff_part)
    down_half = core_sum(down_mine, other_core(down_theirs)).reshape(size, -1, width)
    gu_total, down_total = ring_part(gu_half, size - 1), ring_part(down_half, size - 1)
    *got, gu_total, down_total = sync(*got, gu_total, down_total)
    gu_moved, down_moved = along(gu_total, -1, True), along(down_total, -1, True)
    got = sync(*plane_sum_more(normed_split, *got))
    grad_normed_two = plane_sum_end(normed_split, *got)
    grad_y = own_cot.astype(f32)
    grad_gain_two = jnp.sum(grad_normed_two * middle * scale_two, axis=(0, 1))
    weighted = grad_normed_two * gain_two
    grad_middle = (
        grad_y
        + scale_two * weighted
        - middle * scale_two**3 * jnp.mean(middle * weighted, axis=-1, keepdims=True)
    )
    pieces = plane_gather_start(grad_middle.astype(bf16))
    *pieces, gu_moved, down_moved = sync(*pieces, gu_moved, down_moved)
    gu_total, down_total = ring_add(gu_half, gu_moved, size - 2), ring_add(down_half, down_moved, size - 2)
    gu_moved, down_moved = along(gu_total, -1, True), along(down_total, -1, True)
    full_down = assemble(index, [after(down_all[0], gu_total)] + down_all[1:])
    result_split = dot_split(after(hidden, gu_total), full_down)
    pieces = plane_gather_more(*pieces)
    for k in range(size - 3, -1, -1):
        gu_total, down_total = ring_add(gu_half, gu_moved, k), ring_add(down_half, down_moved, k)
        if k == size - 3:
            *pieces, gu_total, down_total, result_split[0] = sync(*pieces, gu_total, down_total, result_split[0])
        if k > 0:
            gu_moved, down_moved = along(gu_total, -1, True), along(down_total, -1, True)
    sum_gu, sum_down = gu_total, down_total
    grad_branch = plane_gather_end(*pieces)
    grad_attn = dot_nt(grad_branch, full_out).astype(bf16)

    attended[-1] = after(attended[-1], sum_down)
    states = [[(grad_attn, (chunk, q_part), (m, 0)), attended[m]] for m in range(micro)]
    grad_query = [None] * micro
    terms = [None] * micro
    for k in range(size - 1, -1, -1):
        first = k == size - 1
        for m in range(micro):
            outs = attend_back(
                m, k, first, k == 0, info, q_rot[m], kv_windows[m][k], lse[m], qpos, qbeg[m], kpos,
                (cos_all, (None, None, chunk, LANES), (m, k, 0, 0)), (sin_all, (None, None, chunk, LANES), (m, k, 0, 0)),
                e4, states[m] if first else states[m] + [moved[m]],
            )
            states[m] = outs[:3] if first else states[m][:2] + [outs[0]]
            terms[m] = outs[3] if first else outs[1]
            if k == 0:
                grad_query[m] = outs[-1]
        if k > 0:
            moved = [along(term, -1, False) for term in terms]
            moved[0] = after(moved[0], terms[-1], *([sum_gu, sum_down] if first else []))
        if first:
            got = plane_sum_start(sync(*result_split[:2], *terms)[:2])
            term_out = plane_swap(dot_tn(attn_low, after(grad_branch, *terms)).astype(bf16), 1, 0)
        elif k == size - 2:
            moved[-1], term_out, *got = sync(moved[-1], term_out, *got)
            out_mine, out_other = core_halves(term_out)
            got = plane_sum_more(result_split, *got)
        elif k == size - 3:
            moved[-1], out_other, *got = sync(moved[-1], out_other, *got)
            output = (middle + plane_sum_end(result_split, *got)).astype(bf16)
            out_half = core_sum(out_mine, out_other)

    grad_qkv = jnp.concatenate([jnp.concatenate(grad_query, axis=0), jnp.concatenate(terms, axis=0)], axis=1)
    *part_split, gain_rows, qkv_theirs, qkv_mine = project_back(index, grad_qkv, full_qkv, normed_one, gathered_in, in_scale)
    got = plane_sum_start(part_split)
    gain_terms = jnp.stack([gain_rows[0], grad_gain_two]).astype(bf16)
    gain_terms = jnp.pad(gain_terms, ((0, LANES - 2), (0, 0))).T
    gain_mine, gain_other = core_halves(gain_terms)
    qkv_half = core_sum(qkv_mine, other_core(qkv_theirs)).reshape(size, shard_rows * PLANE, -1)
    last_half = jnp.concatenate([qkv_half, out_half, core_sum(gain_mine, gain_other)], axis=-1)
    last_total = ring_part(last_half, size - 1)
    sum_gu = plane_swap(after(sum_gu, last_total), 0, 1)
    for k in range(size - 2, -1, -1):
        last_moved = along(last_total, -1, True)
        if k == size - 2:
            *got, last_moved = sync(*got, last_moved)
            got = plane_sum_more(part_split, *got)
        elif k == size - 3:
            *got, last_moved, sum_gu = sync(*got, last_moved, sum_gu)
        last_total = ring_add(last_half, last_moved, k)
    grad_normed_one = plane_sum_end(part_split, *got)
    last_total = plane_swap(last_total, 0, 1).astype(f32).reshape(shard_rows, PLANE, -1)
    scale_one = rms_scale(layer_in)
    weighted = grad_normed_one * gain_one
    input_grad = (
        grad_middle
        + scale_one * weighted
        - layer_in * scale_one**3 * jnp.mean(layer_in * weighted, axis=-1, keepdims=True)
    )
    sum_gu = sum_gu.astype(f32).reshape(shard_rows, PLANE, FF_TILES, 2, ff_part // FF_TILES)
    cuts = np.cumsum([q_part, kv_part, kv_part, out_part])
    sum_query, sum_key, sum_value, sum_out, gain_sum = jnp.split(last_total, cuts, axis=2)
    gain_sum = jnp.sum(gain_sum, axis=1)
    return (
        output[:, None],
        input_grad[:, None],
        gain_sum[:, 0],
        gain_sum[:, 1],
        sum_query.reshape(shard_rows, -1),
        sum_key.reshape(shard_rows, -1),
        sum_value.reshape(shard_rows, -1),
        sum_out.reshape(shard_rows, -1),
        from_ff_parts(sum_gu[:, :, :, 0]),
        from_ff_parts(sum_gu[:, :, :, 1]),
        sum_down.astype(f32),
    )


def solution(mesh):
    blocks = mesh.shape["blk"]
    grid = Mesh(mesh.devices.reshape(2, blocks // PLANE, PLANE), ("stream", "zed", "plane"))
    tokens = P(None, "stream", ("zed", "plane"), None)
    vector = P(("stream", "zed", "plane"))
    matrix = P(("stream", "zed", "plane"), None)
    return jax.shard_map(
        on_device,
        mesh=grid,
        in_specs=(tokens, tokens, P(None, "stream", None), vector, vector) + (matrix,) * 7,
        out_specs=(tokens, tokens, vector, vector) + (matrix,) * 7,
        check_vma=False,
    )
```

```python
import math

import jax
import jax.numpy as jnp
import numpy as np
from jax import lax
from jax.experimental import pallas as pl
from jax.experimental.pallas import tpu as pltpu
from jax.sharding import Mesh
from jax.sharding import PartitionSpec as P

HQ = 16
HK = 8
DH = 96
PLANE = 4
FF_TILES = 2
LANES = 128
VMEM_BYTES = 50 * 1024 * 1024

epsilon = 1e-05
rope_base = 100000.0
masked_score = -1e30
score_scale = 1.0 / math.sqrt(DH)
exp2_scale = score_scale * math.log2(math.e)

LIGHT = pl.CostEstimate(flops=1, bytes_accessed=1, transcendentals=0)
CHUNK_COST = pl.CostEstimate(flops=1, bytes_accessed=6000000, transcendentals=0)

f32 = jnp.float32
bf16 = jnp.bfloat16


def spread(heads):
    table = np.zeros((heads * DH, heads * LANES), np.float32)
    for head in range(heads):
        for i in range(DH):
            lane = i if i < DH // 2 else i + (LANES - DH) // 2
            table[head * DH + i, head * LANES + lane] = 1.0
    return jnp.asarray(table, bf16)


def rms_scale(values):
    return lax.rsqrt(jnp.mean(values * values, axis=-1, keepdims=True) + epsilon)


def dot(a, b):
    return jnp.dot(a, b, preferred_element_type=f32)


def dot_nt(a, b):
    return lax.dot_general(a, b, (((1,), (1,)), ((), ())), preferred_element_type=f32)


def dot_tn(a, b):
    return lax.dot_general(a, b, (((0,), (0,)), ((), ())), preferred_element_type=f32)


def piece_halves(one_ref, one_more_ref, two_ref, two_more_ref):
    return [
        [(one_ref, 0), (one_ref, 1)],
        [(one_more_ref, 0), (one_more_ref, 1)],
        [(two_ref, 0), (two_more_ref, 0)],
        [(two_ref, 1), (two_more_ref, 1)],
    ]


def project_kernel(size, info_ref, one_ref, two_ref, one_more_ref, two_more_ref, cos_ref, sin_ref, e4_ref, e8_ref, *rest):
    blocks, (x_ref, n_ref, q_ref, kv_ref, w_ref, out_w_ref, gains_ref, scale_ref, pad_s) = rest[: 2 * size], rest[2 * size :]
    rows = blocks[0].shape[0]
    heads = 8 * DH

    @pl.when(pl.program_id(0) == 0)
    def _():
        for i, block in enumerate(blocks):
            core = info_ref[1] if i < size else 1 - info_ref[1]
            start = pl.multiple_of((core * size + lax.rem(info_ref[0] - i % size + size, size)) * rows, rows)
            w_ref[pl.ds(start, rows), :] = block[:, : heads + LANES]
            out_w_ref[pl.ds(start, rows), :] = block[:, heads + LANES :]
            pad_s[pl.ds(start, rows), :] = dot(block[:, :heads], e8_ref[...]).astype(bf16)
        rows_to = lax.broadcasted_iota(jnp.int32, (LANES, LANES), 0)
        same = (rows_to == lax.broadcasted_iota(jnp.int32, (LANES, LANES), 1)).astype(bf16)
        gains_ref[...] = dot_nt(same[:8], w_ref[:, heads:])

    tok_rows = one_ref.shape[1]
    for i, halves in enumerate(piece_halves(one_ref, one_more_ref, two_ref, two_more_ref)):

        @pl.when(pl.program_id(0) == i)
        def _(halves=halves):
            for j, (ref, slot) in enumerate(halves):
                x_ref[j * tok_rows : (j + 1) * tok_rows, :] = ref[slot]

    x = x_ref[...].astype(f32)
    scale = rms_scale(x)
    scale_ref[...] = scale
    normed = (x * scale * gains_ref[0:1, :]).astype(bf16)
    n_ref[...] = normed
    pre = dot(normed, pad_s[...])
    cos, sin = cos_ref[...], sin_ref[...]
    parts = []
    for head in range(8):
        piece = pre[:, head * LANES : (head + 1) * LANES]
        if head < 6:
            piece = piece * cos + pltpu.roll(piece, LANES // 2, 1) * sin
        parts.append(piece.astype(bf16))
    q_ref[...] = jnp.concatenate(parts[:4], axis=1)
    kv_ref[...] = dot_nt(jnp.concatenate(parts[4:], axis=1), e4_ref[...]).astype(bf16)


def project(info, pieces, blocks, cos, sin, e4, e8):
    _, tok_rows, width = pieces[0].shape
    rows, step = 2 * PLANE * tok_rows, 2 * tok_rows
    size = len(blocks) // 2
    cols = blocks[0].shape[1]
    first = 8 * DH + LANES
    whole = lambda a: pl.BlockSpec(a.shape, lambda i, n: (0,) * a.ndim)
    by_row = lambda c: pl.BlockSpec((step, c), lambda i, n: (i, 0))
    return pl.pallas_call(
        lambda *refs: project_kernel(size, *refs),
        grid_spec=pltpu.PrefetchScalarGridSpec(
            num_scalar_prefetch=1,
            grid=(rows // step,),
            in_specs=[whole(a) for a in pieces]
            + [by_row(LANES), by_row(LANES), whole(e4), whole(e8)]
            + [whole(b) for b in blocks],
            out_specs=[
                by_row(width),
                by_row(width),
                by_row(4 * LANES),
                by_row(4 * DH),
                pl.BlockSpec((width, first), lambda i, n: (0, 0)),
                pl.BlockSpec((width, cols - first), lambda i, n: (0, 0)),
                pl.BlockSpec((8, width), lambda i, n: (0, 0)),
                by_row(1),
            ],
            scratch_shapes=[pltpu.VMEM((width, 8 * LANES), bf16)],
        ),
        out_shape=[
            jax.ShapeDtypeStruct((rows, width), bf16),
            jax.ShapeDtypeStruct((rows, width), bf16),
            jax.ShapeDtypeStruct((rows, 4 * LANES), bf16),
            jax.ShapeDtypeStruct((rows, 4 * DH), bf16),
            jax.ShapeDtypeStruct((width, first), bf16),
            jax.ShapeDtypeStruct((width, cols - first), bf16),
            jax.ShapeDtypeStruct((8, width), f32),
            jax.ShapeDtypeStruct((rows, 1), f32),
        ],
        compiler_params=pltpu.CompilerParams(vmem_limit_bytes=VMEM_BYTES),
        cost_estimate=LIGHT,
        name="project",
    )(info, *pieces, cos, sin, e4, e8, *blocks)


def assemble_kernel(size, info_ref, *rest):
    blocks, out_ref = rest[: 2 * size], rest[2 * size]
    rows = blocks[0].shape[0]
    for i, block in enumerate(blocks):
        core = info_ref[1] if i < size else 1 - info_ref[1]
        start = pl.multiple_of((core * size + lax.rem(info_ref[0] - i % size + size, size)) * rows, rows)
        out_ref[pl.ds(start, rows), :] = block[...]


def assemble(info, blocks):
    size = len(blocks) // 2
    rows, width = blocks[0].shape
    step = width // 3 if width % 384 == 0 else width // 4
    return pl.pallas_call(
        lambda *refs: assemble_kernel(size, *refs),
        grid_spec=pltpu.PrefetchScalarGridSpec(
            num_scalar_prefetch=1,
            grid=(width // step,),
            in_specs=[pl.BlockSpec((rows, step), lambda i, n: (0, i)) for _ in blocks],
            out_specs=pl.BlockSpec((len(blocks) * rows, step), lambda i, n: (0, i)),
        ),
        out_shape=jax.ShapeDtypeStruct((len(blocks) * rows, width), blocks[0].dtype),
        compiler_params=pltpu.CompilerParams(vmem_limit_bytes=VMEM_BYTES),
        cost_estimate=LIGHT,
        name="assemble",
    )(info, *blocks)


def allowed_of(info_ref, k, chunk, qpos_ref, qbeg_ref, kpos_ref):
    kpos = kpos_ref[...] + (info_ref[0] - k) * chunk
    return (kpos <= qpos_ref[...]) & (kpos >= qbeg_ref[...])


def useful_of(info_ref, m, k, chunk):
    z = info_ref[0]
    return (k <= z) & ((z - k + 1) * chunk - 1 >= info_ref[2 + m])


def stack_heads(block, h):
    return jnp.concatenate(
        [block[:, (2 * h) * LANES : (2 * h + 1) * LANES], block[:, (2 * h + 1) * LANES : (2 * h + 2) * LANES]], axis=0
    )


def run_kernel(body, info, inputs, outs, aliases, name):
    def spec(entry):
        if isinstance(entry, tuple):
            return pl.BlockSpec(entry[1], lambda i, n: entry[2])
        return pl.BlockSpec(entry.shape, lambda i, n: (0,) * entry.ndim)

    return list(
        pl.pallas_call(
            body,
            grid_spec=pltpu.PrefetchScalarGridSpec(
                num_scalar_prefetch=1,
                grid=(1,),
                in_specs=[spec(entry) for entry in inputs],
                out_specs=[pl.BlockSpec(o.shape, lambda i, n, o=o: (0,) * len(o.shape)) for o in outs],
            ),
            out_shape=outs,
            input_output_aliases=aliases,
            compiler_params=pltpu.CompilerParams(vmem_limit_bytes=VMEM_BYTES),
            cost_estimate=CHUNK_COST,
            name=name,
        )(info, *[entry[0] if isinstance(entry, tuple) else entry for entry in inputs])
    )


def attend_kernel(m, k, last, info_ref, q_ref, kv_ref, qpos_ref, qbeg_ref, kpos_ref, e_ref, *rest):
    chunk = kv_ref.shape[0]
    if k > 0:
        top_in, acc_in, rest = rest[0], rest[1], rest[2:]
    top_ref, acc_ref = rest[0], rest[1]

    def run():
        allowed = allowed_of(info_ref, k, chunk, qpos_ref, qbeg_ref, kpos_ref)
        kv = kv_ref[...]
        q = q_ref[...]
        one_lane = (lax.broadcasted_iota(jnp.int32, (1, LANES), 1) == DH // 2).astype(f32)
        for h in range(2):
            keys = dot(kv, e_ref[:, h * LANES : (h + 1) * LANES]).astype(bf16)
            vals = (dot(kv, e_ref[:, (2 + h) * LANES : (3 + h) * LANES]) + one_lane).astype(bf16)
            s = jnp.where(allowed, dot_nt(keys, stack_heads(q, h)), masked_score)
            new = jnp.max(s, axis=0, keepdims=True)
            if k > 0:
                old = top_in[h]
                new = jnp.maximum(old, new)
            w = jnp.where(allowed, jnp.exp2((s - new) * exp2_scale), 0.0).astype(bf16)
            acc = dot_tn(vals, w)
            if k > 0:
                acc = acc_in[h] * jnp.exp2((old - new) * exp2_scale) + acc
            acc_ref[h] = acc
            top_ref[h] = new

    if k == 0:
        run()
    else:
        useful = useful_of(info_ref, m, k, chunk)
        pl.when(useful)(run)

        @pl.when(jnp.logical_not(useful))
        def _():
            top_ref[...] = top_in[...]
            acc_ref[...] = acc_in[...]

    if last:
        att_ref, low_ref, lse_ref = rest[2:]
        parts = []
        for h in range(2):
            acc = acc_ref[h]
            total = acc[DH // 2 : DH // 2 + 1, :]
            lse_ref[h] = top_ref[h] * exp2_scale + jnp.log2(total)
            flat = (acc / total).T
            rows = flat.shape[0] // 2
            parts += [flat[:rows], flat[rows:]]
        att = jnp.concatenate(parts, axis=1)
        att_ref[...] = att
        low_ref[...] = dot_nt(att.astype(bf16), e_ref[...]).astype(bf16)


def attend(m, k, last, info, q, kv, qpos, qbeg, kpos, e4, state):
    rows = q[1][0]
    outs = [jax.ShapeDtypeStruct((2, 1, 2 * rows), f32), jax.ShapeDtypeStruct((2, LANES, 2 * rows), f32)]
    if last:
        outs += [
            jax.ShapeDtypeStruct((rows, 4 * LANES), f32),
            jax.ShapeDtypeStruct((rows, 4 * DH), bf16),
            jax.ShapeDtypeStruct((2, 1, 2 * rows), f32),
        ]
    return run_kernel(
        lambda *refs: attend_kernel(m, k, last, *refs),
        info,
        [q, kv, qpos, qbeg, kpos, e4] + state,
        outs,
        {7: 0, 8: 1} if k > 0 else {},
        "attend",
    )


def attend_back_kernel(
    m, k, first, last, info_ref, q_ref, kv_ref, lse_ref, qpos_ref, qbeg_ref, kpos_ref, cosk_ref, sink_ref, e_ref, *rest
):
    chunk = kv_ref.shape[0]
    if first:
        g_ref, att_ref, rest = rest[0], rest[1], rest[2:]
        go_ref, delta_ref, dq_ref, dkv_ref = rest[:4]
        go = dot(g_ref[...], e_ref[...])
        for h in range(2):
            go_h = stack_heads(go, h)
            go_ref[h] = go_h.astype(bf16)
            prod = go_h * stack_heads(att_ref[...], h)
            delta_ref[h] = jnp.sum(prod.T, axis=0, keepdims=True)
    else:
        go_ref, delta_ref, dq_in, moved_ref, rest = rest[0], rest[1], rest[2], rest[3], rest[4:]
        dq_ref, dkv_ref = rest[:2]

    def run():
        allowed = allowed_of(info_ref, k, chunk, qpos_ref, qbeg_ref, kpos_ref)
        kv = kv_ref[...]
        q = q_ref[...]
        cosk, sink = cosk_ref[...], sink_ref[...]
        grad_keys, grad_vals = [], []
        for h in range(2):
            keys = dot(kv, e_ref[:, h * LANES : (h + 1) * LANES]).astype(bf16)
            vals = dot(kv, e_ref[:, (2 + h) * LANES : (3 + h) * LANES]).astype(bf16)
            q_h = stack_heads(q, h)
            go_h = go_ref[h]
            s = dot_nt(keys, q_h)
            w = jnp.where(allowed, jnp.exp2(s * exp2_scale - lse_ref[h]), 0.0)
            grad_vals.append(dot(w.astype(bf16), go_h).astype(bf16))
            ds = (w * (dot_nt(vals, go_h) - delta_ref[h])).astype(bf16)
            dq = dot_tn(keys, ds)
            dq_ref[h] = dq if first else dq_in[h] + dq
            gk = dot(ds, q_h) * score_scale
            gk = gk * cosk + pltpu.roll(gk * sink, LANES // 2, 1)
            grad_keys.append(gk.astype(bf16))
        total = dot_nt(jnp.concatenate(grad_keys + grad_vals, axis=1), e_ref[...])
        if not first:
            total = total + moved_ref[...].astype(f32)
        dkv_ref[...] = total.astype(bf16)

    if k == 0:
        run()
    else:
        useful = useful_of(info_ref, m, k, chunk)
        pl.when(useful)(run)

        @pl.when(jnp.logical_not(useful))
        def _():
            dkv_ref[...] = jnp.zeros(dkv_ref.shape, bf16) if first else moved_ref[...]
            dq_ref[...] = jnp.zeros(dq_ref.shape, f32) if first else dq_in[...]

    if last:
        out_ref = rest[-1]
        parts = []
        for h in range(2):
            flat = dq_ref[h].T * score_scale
            rows = flat.shape[0] // 2
            for piece in (flat[:rows], flat[rows:]):
                parts.append((piece * cosk_ref[...] + pltpu.roll(piece * sink_ref[...], LANES // 2, 1)).astype(bf16))
        out_ref[...] = dot_nt(jnp.concatenate(parts, axis=1), e_ref[...]).astype(bf16)


def attend_back(m, k, first, last, info, q, kv, lse, qpos, qbeg, kpos, cosk, sink, e4, state):
    rows = q[1][0]
    outs = []
    if first:
        outs += [jax.ShapeDtypeStruct((2, 2 * rows, LANES), bf16), jax.ShapeDtypeStruct((2, 1, 2 * rows), f32)]
    outs += [jax.ShapeDtypeStruct((2, LANES, 2 * rows), f32), jax.ShapeDtypeStruct((rows, 4 * DH), bf16)]
    if last:
        outs += [jax.ShapeDtypeStruct((rows, 4 * DH), bf16)]
    return run_kernel(
        lambda *refs: attend_back_kernel(m, k, first, last, *refs),
        info,
        [q, kv, lse, qpos, qbeg, kpos, cosk, sink, e4] + state,
        outs,
        {} if first else {12: 0},
        "attend_back",
    )


def store_split(sum_of, tok_rows, first_ref, second_ref, keep_first_ref, keep_second_ref):
    for i, slot in enumerate((1, 3)):
        first_ref[i] = sum_of(slot * tok_rows, tok_rows).astype(bf16)
        keep_first_ref[i] = sum_of((slot - 1) * tok_rows, tok_rows)
    for i in range(2):
        second_ref[i] = sum_of((PLANE + 2 + i) * tok_rows, tok_rows).astype(bf16)
        keep_second_ref[i] = sum_of((PLANE + i) * tok_rows, tok_rows)


def split_outs(tok_rows, width):
    return [jax.ShapeDtypeStruct((2, tok_rows, width), kind) for kind in (bf16, bf16, f32, f32)]


def dot_split_kernel(tok_rows, a_ref, w_ref, *rest):
    acc_s = rest[-1]
    acc_s[...] = dot(a_ref[...], w_ref[...])
    store_split(lambda start, n: acc_s[start : start + n, :], tok_rows, *rest[:-1])


def dot_split(a, w):
    rows, inner = a.shape
    tok_rows = rows // (2 * PLANE)
    width = w.shape[1]
    step = width // 3
    outs = split_outs(tok_rows, width)
    return list(
        pl.pallas_call(
            lambda *refs: dot_split_kernel(tok_rows, *refs),
            grid=(3,),
            in_specs=[pl.BlockSpec((rows, inner), lambda i: (0, 0)), pl.BlockSpec((inner, step), lambda i: (0, i))],
            out_specs=[pl.BlockSpec((2, tok_rows, step), lambda i: (0, 0, i)) for _ in outs],
            out_shape=outs,
            scratch_shapes=[pltpu.VMEM((rows, step), f32)],
            compiler_params=pltpu.CompilerParams(vmem_limit_bytes=VMEM_BYTES),
            cost_estimate=LIGHT,
            name="dot_split",
        )(a, w)
    )


def ffn_kernel(size, tok_rows, info_ref, one_ref, two_ref, one_more_ref, two_more_ref, g_ref, *rest):
    gu_blocks, down_blocks, rest = rest[: 2 * size], rest[2 * size : 4 * size], rest[4 * size :]
    hidden_ref, *outs = rest[:5]
    gu_theirs_ref, gu_mine_ref, down_theirs_ref, down_mine_ref = rest[5:9]
    gu_s, down_s, acc_s, flat_s, grad_s, n_ref, sems = rest[9:]
    f, last = pl.program_id(0), pl.num_programs(0) - 1
    units = hidden_ref.shape[1]
    half = flat_s.shape[0] // 2

    def place(i, rows):
        core = info_ref[1] if i < size else 1 - info_ref[1]
        return pl.ds(pl.multiple_of((core * size + lax.rem(info_ref[0] - i % size + size, size)) * rows, rows), rows)

    @pl.when(f == 0)
    def _():
        copies = []
        for i, halves in enumerate(piece_halves(one_ref, one_more_ref, two_ref, two_more_ref)):
            for j, (ref, slot) in enumerate(halves):
                at = pl.ds((2 * i + j) * tok_rows, tok_rows)
                copies.append(pltpu.make_async_copy(ref.at[slot], n_ref.at[at], sems.at[2 * i + j]))
                copies[-1].start()
        acc_s[...] = jnp.zeros(acc_s.shape, f32)
        for copy in copies:
            copy.wait()
        flat_s[...] = n_ref[...].T
        for i, block in enumerate(down_blocks):
            down_s[place(i, block.shape[0]), :] = block[...]

    for i, block in enumerate(gu_blocks):
        gu_s[place(i, block.shape[0]), :] = block[...]
    w_down = down_s.at[pl.ds(pl.multiple_of(f * units, units), units)]
    step = 4 * tok_rows

    @pl.loop(0, n_ref.shape[0] // step)
    def _(r):
        at = pl.ds(pl.multiple_of(r * step, step), step)
        pre = dot(n_ref[at, :], gu_s[...])
        grad_hidden = dot_nt(g_ref[at, :], w_down[...])
        gate_pre, up_pre = pre[:, :units], pre[:, units:]
        sigmoid_gate = jax.nn.sigmoid(gate_pre)
        silu_gate = gate_pre * sigmoid_gate
        hidden_ref[at, :] = (silu_gate * up_pre).astype(bf16)
        grad_gate = grad_hidden * up_pre * sigmoid_gate * (1.0 + gate_pre * (1.0 - sigmoid_gate))
        both = jnp.concatenate([grad_gate.astype(bf16), (grad_hidden * silu_gate).astype(bf16)], axis=1)
        grad_s[at, :] = both
        acc_s[at, :] += dot_nt(both, gu_s[...])

    core = info_ref[1]
    gu_mine_ref[...] = dot(flat_s[pl.ds(pl.multiple_of(core * half, half), half), :], grad_s[...]).astype(bf16)
    gu_theirs_ref[...] = dot(flat_s[pl.ds(pl.multiple_of((1 - core) * half, half), half), :], grad_s[...]).astype(bf16)
    term_down = dot_tn(hidden_ref[...], g_ref[...]).astype(bf16)
    is_mine = lax.div(f, pl.num_programs(0) // 2) == core

    @pl.when(is_mine)
    def _():
        down_mine_ref[...] = term_down

    @pl.when(jnp.logical_not(is_mine))
    def _():
        down_theirs_ref[...] = term_down

    @pl.when(f == last)
    def _():
        store_split(lambda start, n: acc_s[start : start + n, :], tok_rows, *outs)


def ffn(info, pieces, grad_mlp, gu_blocks, down_blocks):
    rows, width = grad_mlp.shape
    size = len(gu_blocks) // 2
    tok_rows = rows // (2 * PLANE)
    ff_part = gu_blocks[0].shape[1] // 2
    units = ff_part // FF_TILES
    whole = lambda a: pl.BlockSpec(a.shape, lambda f, n: (0,) * a.ndim, pipeline_mode=pl.Buffered(1))
    outs = split_outs(tok_rows, width)
    gu_half = pl.BlockSpec((width // 2, 2 * units), lambda f, n: (0, f))

    def down_half(core_of):
        return pl.BlockSpec((units, width), lambda f, n: (jnp.clip(f - core_of(n) * (FF_TILES // 2), 0, FF_TILES // 2 - 1), 0))

    return list(
        pl.pallas_call(
            lambda *refs: ffn_kernel(size, tok_rows, *refs),
            grid_spec=pltpu.PrefetchScalarGridSpec(
                num_scalar_prefetch=1,
                grid=(FF_TILES,),
                in_specs=[pl.BlockSpec(memory_space=pl.ANY) for _ in pieces]
                + [whole(grad_mlp)]
                + [pl.BlockSpec((block.shape[0], 2 * units), lambda f, n: (0, f)) for block in gu_blocks]
                + [whole(block) for block in down_blocks],
                out_specs=[pl.BlockSpec((rows, units), lambda f, n: (0, f))]
                + [pl.BlockSpec(o.shape, lambda f, n: (0, 0, 0), pipeline_mode=pl.Buffered(1)) for o in outs]
                + [gu_half, gu_half, down_half(lambda n: 1 - n[1]), down_half(lambda n: n[1])],
                scratch_shapes=[
                    pltpu.VMEM((width, 2 * units), bf16),
                    pltpu.VMEM((ff_part, width), bf16),
                    pltpu.VMEM((rows, width), f32),
                    pltpu.VMEM((width, rows), bf16),
                    pltpu.VMEM((rows, 2 * units), bf16),
                    pltpu.VMEM((rows, width), bf16),
                    pltpu.SemaphoreType.DMA((2 * PLANE,)),
                ],
            ),
            out_shape=[jax.ShapeDtypeStruct((rows, ff_part), bf16)]
            + outs
            + [jax.ShapeDtypeStruct((width // 2, 2 * ff_part), bf16)] * 2
            + [jax.ShapeDtypeStruct((ff_part // 2, width), bf16)] * 2,
            compiler_params=pltpu.CompilerParams(vmem_limit_bytes=58 * 1024 * 1024),
            cost_estimate=LIGHT,
            name="ffn",
        )(info, *pieces, grad_mlp, *gu_blocks, *down_blocks)
    )


def project_back_kernel(tok_rows, info_ref, g_ref, w_ref, n_ref, x_ref, scale_ref, *rest):
    first_ref, second_ref, keep_first_ref, keep_second_ref, gain_ref, theirs_ref, mine_ref, acc_s = rest
    rows = 2 * tok_rows
    total = jnp.zeros((1, acc_s.shape[1]), f32)
    for i in range(g_ref.shape[0] // rows):
        at = slice(i * rows, (i + 1) * rows)
        acc = dot_nt(g_ref[at, :], w_ref[...])
        acc_s[at, :] = acc
        total = total + jnp.sum(acc * x_ref[at, :].astype(f32) * scale_ref[at, :], axis=0, keepdims=True)
    gain_ref[...] = jnp.broadcast_to(total, gain_ref.shape)
    store_split(lambda start, n: acc_s[start : start + n, :], tok_rows, first_ref, second_ref, keep_first_ref, keep_second_ref)
    term = dot_tn(n_ref[...], g_ref[...]).astype(bf16)
    is_mine = pl.program_id(0) == info_ref[1]

    @pl.when(is_mine)
    def _():
        mine_ref[...] = term

    @pl.when(jnp.logical_not(is_mine))
    def _():
        theirs_ref[...] = term


def project_back(info, grads, w, normed, x, scale):
    rows, inner = grads.shape
    tok_rows = rows // (2 * PLANE)
    width = w.shape[0]
    half = width // 2
    outs = split_outs(tok_rows, width)
    column = pl.BlockSpec((rows, half), lambda i, n: (0, i))
    out_whole = pl.BlockSpec((half, inner), lambda i, n: (0, 0))
    return list(
        pl.pallas_call(
            lambda *refs: project_back_kernel(tok_rows, *refs),
            grid_spec=pltpu.PrefetchScalarGridSpec(
                num_scalar_prefetch=1,
                grid=(2,),
                in_specs=[
                    pl.BlockSpec((rows, inner), lambda i, n: (0, 0)),
                    pl.BlockSpec((half, inner), lambda i, n: (i, 0)),
                    column,
                    column,
                    pl.BlockSpec((rows, 1), lambda i, n: (0, 0)),
                ],
                out_specs=[pl.BlockSpec((2, tok_rows, half), lambda i, n: (0, 0, i)) for _ in outs]
                + [pl.BlockSpec((8, half), lambda i, n: (0, i)), out_whole, out_whole],
                scratch_shapes=[pltpu.VMEM((rows, half), f32)],
            ),
            out_shape=outs
            + [jax.ShapeDtypeStruct((8, width), f32)]
            + [jax.ShapeDtypeStruct((half, inner), bf16)] * 2,
            compiler_params=pltpu.CompilerParams(vmem_limit_bytes=VMEM_BYTES),
            cost_estimate=LIGHT,
            name="project_back",
        )(info, grads, w, normed, x, scale)
    )


def beside(value, bit):
    return lax.ppermute(value, "plane", [(i, i ^ bit) for i in range(PLANE)])


def other_core(value):
    return lax.ppermute(value, "stream", [(0, 1), (1, 0)])


def along(value, step, wrap):
    size = lax.axis_size("zed")
    pairs = [(i, (i + step) % size) for i in range(size) if wrap or 0 <= i + step < size]
    return lax.ppermute(value, "zed", pairs)


def plane_gather_start(own):
    return [own[0], own[1], beside(own[0], 1), beside(own[1], 2)]


def plane_gather_more(first, second, first_got, second_got):
    pair_one, pair_two = jnp.stack([first, first_got]), jnp.stack([second, second_got])
    return [pair_one, pair_two, beside(pair_one, 2), beside(pair_two, 1)]


def plane_gather_end(pair_one, pair_two, first_more, second_more):
    blocks = [pair_one, first_more, pair_two[:1], second_more[:1], pair_two[1:], second_more[1:]]
    return jnp.concatenate(blocks).reshape(-1, pair_one.shape[-1])


def plane_sum_start(split):
    return [beside(split[0], 1), beside(split[1], 2)]


def plane_sum_more(split, got_first, got_second):
    keep_first, keep_second = split[2], split[3]
    more_first = beside((keep_first[1] + got_first[1]).astype(bf16), 2)
    more_second = beside((keep_second[1] + got_second[1]).astype(bf16), 1)
    return [got_first[0], got_second[0], more_first, more_second]


def plane_sum_end(split, got_first, got_second, more_first, more_second):
    return jnp.stack([split[2][0] + got_first + more_first, split[3][0] + got_second + more_second])


def after(value, *earlier):
    return lax.optimization_barrier((value,) + earlier)[0]


def sync(*values):
    return list(lax.optimization_barrier(values))


def core_halves(full):
    size = lax.axis_size("zed")
    s = lax.axis_index("stream")
    full = full.reshape((2, size, -1) + full.shape[1:])
    mine = lax.dynamic_index_in_dim(full, s, 0, keepdims=False)
    theirs = lax.dynamic_index_in_dim(full, 1 - s, 0, keepdims=False)
    return mine, other_core(theirs)


def core_sum(mine, other):
    return (mine.astype(f32) + other.astype(f32)).astype(bf16)


def ring_part(half, k):
    size = lax.axis_size("zed")
    z = lax.axis_index("zed")
    return lax.dynamic_index_in_dim(half, lax.rem(z - k + size, size), 0, keepdims=False)


def ring_add(half, moved, k):
    return (moved.astype(f32) + ring_part(half, k).astype(f32)).astype(bf16)


def plane_swap(value, split, concat):
    return lax.all_to_all(value, "plane", split_axis=split, concat_axis=concat, tiled=True)


def on_device(inputs, cotangent, seq_lengths, gain_attn, gain_ffn, w_query, w_key, w_value, w_out, w_gate, w_up, w_down):
    size = lax.axis_size("zed")
    s, z, p = lax.axis_index("stream"), lax.axis_index("zed"), lax.axis_index("plane")
    micro, _, tok_rows, width = inputs.shape
    chunk = PLANE * tok_rows
    tokens = micro * chunk
    shard_rows = w_query.shape[0]
    ff_block = w_down.shape[0]
    ff_blocks = 2 * size
    ff_part = ff_blocks * ff_block
    q_part, kv_part = HQ * DH // PLANE, HK * DH // PLANE
    out_part = width // PLANE
    e4, e8 = spread(4), spread(8)

    def by_part(weight):
        return weight.reshape(shard_rows, PLANE, -1)

    def by_ff_part(weight):
        return weight.reshape(shard_rows, ff_blocks, PLANE, ff_block).transpose(0, 2, 1, 3).reshape(shard_rows, PLANE, -1)

    def from_ff_parts(term):
        return term.reshape(shard_rows, PLANE, ff_blocks, ff_block).transpose(0, 2, 1, 3).reshape(shard_rows, -1)

    own_in = inputs[:, 0]
    own_cot = cotangent[:, 0]
    gains = jnp.stack([gain_attn, gain_ffn], axis=1)
    gains = jnp.broadcast_to(jnp.pad(gains, ((0, 0), (0, LANES - 2)))[:, None], (shard_rows, PLANE, LANES))
    qkv_bundle = jnp.concatenate([by_part(w_query), by_part(w_key), by_part(w_value), gains, by_part(w_out)], axis=2)
    qkv_block = plane_swap(qkv_bundle.reshape(shard_rows, -1), 1, 0)
    tiled = (shard_rows, PLANE, FF_TILES, ff_part // FF_TILES)
    ffn_bundle = jnp.stack([by_ff_part(w_gate).reshape(tiled), by_ff_part(w_up).reshape(tiled)], axis=3).reshape(shard_rows, -1)
    qkv_blocks = [qkv_block]
    for _ in range(size - 1):
        qkv_blocks.append(along(qkv_blocks[-1], 1, True))
    ffn_block = plane_swap(after(ffn_bundle, qkv_block), 1, 0)
    pieces = sync(*plane_gather_start(after(own_in, qkv_block)))
    *in_pieces, qkv_blocks[-1] = sync(*plane_gather_more(*pieces), qkv_blocks[-1])
    qkv_other = [other_core(block) for block in qkv_blocks]
    gu_blocks = [after(ffn_block, qkv_blocks[-1])]
    gu_blocks.append(along(gu_blocks[0], 1, True))

    slot_place = ((jnp.arange(PLANE, dtype=jnp.int32) ^ p)[:, None] * tok_rows + jnp.arange(tok_rows, dtype=jnp.int32)[None, :]).reshape(chunk)
    chunk_place = (z - jnp.arange(size, dtype=jnp.int32))[:, None] * chunk + slot_place[None, :]
    lengths = seq_lengths[:, 0]
    seq_ends = jnp.cumsum(lengths, axis=1)
    begins = jnp.sum(
        jnp.where(seq_ends[:, None, None, :] <= chunk_place[None, :, :, None], lengths[:, None, None, :], 0), axis=-1
    )
    own_begin = begins[:, 0]
    lane = np.arange(LANES)
    place_in_half = lane % (LANES // 2)
    real = place_in_half < DH // 2
    frequency = jnp.where(
        real, rope_base ** (-2.0 * jnp.asarray(np.minimum(place_in_half, DH // 2 - 1), f32) / DH), 0.0
    )
    rope_place = (chunk_place[None] - begins).astype(f32)

    def tables(place):
        angles = jnp.maximum(place, 0.0)[..., None] * frequency
        signs = jnp.asarray(np.where(real, np.where(lane < LANES // 2, -1.0, 1.0), 0.0), f32)
        return jnp.where(real, jnp.cos(angles), 0.0), jnp.sin(angles) * signs

    cos, sin = tables(after(rope_place[:, 0], qkv_block))
    index = jnp.stack([z, s]).astype(jnp.int32)
    info = jnp.concatenate([index, jnp.min(own_begin, axis=1)])
    qpos = jnp.tile(chunk_place[0], 2)[None]
    qbeg = jnp.tile(own_begin, (1, 2))[:, None]
    kpos = slot_place[:, None]

    gathered_in, normed_one, q_rot, kv_own, full_qkv, full_oc, full_gains, in_scale = project(
        index, in_pieces, qkv_blocks + qkv_other, cos.reshape(tokens, LANES), sin.reshape(tokens, LANES), e4, e8
    )
    gain_one, gain_two = full_gains[0:1], full_gains[1:2]
    full_out = plane_swap(full_oc, 0, 1)
    cot_pieces = plane_gather_start(after(own_cot, kv_own))
    q_rot = [(q_rot, (chunk, 4 * LANES), (m, 0)) for m in range(micro)]
    kv_windows = [[(kv_own, (chunk, 4 * DH), (m, 0))] for m in range(micro)]
    kv_pieces = [[piece] for piece in kv_own.reshape(micro, chunk, 4 * DH)]
    qbeg = [(qbeg, (None, 1, 2 * chunk), (m, 0, 0)) for m in range(micro)]
    states = [[] for _ in range(micro)]
    for k in range(size):
        if k < size - 1:
            arrived = [along(kv_pieces[m][k], 1, False) for m in range(micro)]
        for m in range(micro):
            states[m] = attend(m, k, k == size - 1, info, q_rot[m], kv_windows[m][k], qpos, qbeg[m], kpos, e4, states[m])
        if k < size - 1:
            tops = [state[0] for state in states]
            if k == 0:
                tops[0], tops[1], arrived[0], arrived[1], gu_blocks[1], *cot_pieces = sync(
                    *tops, *arrived, gu_blocks[1], *cot_pieces
                )
                cot_pieces = plane_gather_more(*cot_pieces)
            elif k == 1:
                tops[0], tops[1], arrived[0], arrived[1], full_out, *cot_pieces = sync(*tops, *arrived, full_out, *cot_pieces)
            else:
                tops[0], tops[1], arrived[0], arrived[1] = sync(*tops, *arrived)
            for m in range(micro):
                states[m] = [tops[m], states[m][1]]
                kv_pieces[m].append(arrived[m])
                kv_windows[m].append(arrived[m])
    kv_there = [pieces[-1] for pieces in kv_pieces]
    attended, lse = [state[2] for state in states], [state[4] for state in states]
    attn_low = jnp.concatenate([state[3] for state in states], axis=0)
    gathered_cot = plane_gather_end(*cot_pieces)

    gu_blocks[1], down_block, rope_place = sync(gu_blocks[1], w_down, rope_place, *kv_there)[:3]
    down_blocks = [down_block, along(down_block, 1, True)]
    branch_split = dot_split(attn_low, full_out)
    branch_split = sync(*branch_split, down_blocks[1])
    down_blocks[1] = branch_split.pop()
    gu_blocks.append(along(after(gu_blocks[1], down_blocks[1]), 1, True))
    *got, gu_blocks[2] = sync(*plane_sum_start(branch_split), gu_blocks[2])
    down_blocks.append(along(after(down_blocks[1], gu_blocks[2]), 1, True))
    cos_all, sin_all = tables(after(rope_place, gu_blocks[2]))
    *got, down_blocks[2], cos_all, sin_all = sync(*plane_sum_more(branch_split, *got), down_blocks[2], cos_all, sin_all)
    layer_in = own_in.astype(f32)
    middle = layer_in + plane_sum_end(branch_split, *got)
    scale_two = rms_scale(middle)
    pieces = plane_gather_start((middle * scale_two * gain_two).astype(bf16))
    for k in range(2, size - 1):
        down_blocks.append(along(down_blocks[k], 1, True))
    *pieces, down_blocks[-1] = sync(*pieces, down_blocks[-1])
    for k in range(2, size - 1):
        gu_blocks.append(along(after(gu_blocks[k], down_blocks[-1]), 1, True))
    *pieces, gu_blocks[-1] = sync(*plane_gather_more(*pieces), gu_blocks[-1])

    gu_all = gu_blocks + [other_core(block) for block in gu_blocks]
    down_all = down_blocks + [other_core(block) for block in down_blocks]
    hidden, *outs = ffn(index, pieces, gathered_cot, gu_all, down_all)
    normed_split, (gu_theirs, gu_mine, down_theirs, down_mine) = outs[:4], outs[4:]
    got = plane_sum_start(normed_split)
    gu_half = core_sum(gu_mine, other_core(gu_theirs)).reshape(size, -1, 2 * ff_part)
    down_half = core_sum(down_mine, other_core(down_theirs)).reshape(size, -1, width)
    gu_total, down_total = ring_part(gu_half, size - 1), ring_part(down_half, size - 1)
    *got, gu_total, down_total = sync(*got, gu_total, down_total)
    gu_moved, down_moved = along(gu_total, -1, True), along(down_total, -1, True)
    got = sync(*plane_sum_more(normed_split, *got))
    grad_normed_two = plane_sum_end(normed_split, *got)
    grad_y = own_cot.astype(f32)
    grad_gain_two = jnp.sum(grad_normed_two * middle * scale_two, axis=(0, 1))
    weighted = grad_normed_two * gain_two
    grad_middle = (
        grad_y
        + scale_two * weighted
        - middle * scale_two**3 * jnp.mean(middle * weighted, axis=-1, keepdims=True)
    )
    pieces = plane_gather_start(grad_middle.astype(bf16))
    *pieces, gu_moved, down_moved = sync(*pieces, gu_moved, down_moved)
    gu_total, down_total = ring_add(gu_half, gu_moved, size - 2), ring_add(down_half, down_moved, size - 2)
    gu_moved, down_moved = along(gu_total, -1, True), along(down_total, -1, True)
    full_down = assemble(index, [after(down_all[0], gu_total)] + down_all[1:])
    result_split = dot_split(after(hidden, gu_total), full_down)
    pieces = plane_gather_more(*pieces)
    for k in range(size - 3, -1, -1):
        gu_total, down_total = ring_add(gu_half, gu_moved, k), ring_add(down_half, down_moved, k)
        if k == size - 3:
            *pieces, gu_total, down_total, result_split[0] = sync(*pieces, gu_total, down_total, result_split[0])
        if k > 0:
            gu_moved, down_moved = along(gu_total, -1, True), along(down_total, -1, True)
    sum_gu, sum_down = gu_total, down_total
    grad_branch = plane_gather_end(*pieces)
    grad_attn = dot_nt(grad_branch, full_out).astype(bf16)

    attended[-1] = after(attended[-1], sum_down)
    states = [[(grad_attn, (chunk, q_part), (m, 0)), attended[m]] for m in range(micro)]
    grad_query = [None] * micro
    terms = [None] * micro
    for k in range(size - 1, -1, -1):
        first = k == size - 1
        for m in range(micro):
            outs = attend_back(
                m, k, first, k == 0, info, q_rot[m], kv_windows[m][k], lse[m], qpos, qbeg[m], kpos,
                (cos_all, (None, None, chunk, LANES), (m, k, 0, 0)), (sin_all, (None, None, chunk, LANES), (m, k, 0, 0)),
                e4, states[m] if first else states[m] + [moved[m]],
            )
            states[m] = outs[:3] if first else states[m][:2] + [outs[0]]
            terms[m] = outs[3] if first else outs[1]
            if k == 0:
                grad_query[m] = outs[-1]
        if k > 0:
            moved = [along(term, -1, False) for term in terms]
            moved[0] = after(moved[0], terms[-1], *([sum_gu, sum_down] if first else []))
        if first:
            got = plane_sum_start(sync(*result_split[:2], *terms)[:2])
            term_out = plane_swap(dot_tn(attn_low, after(grad_branch, *terms)).astype(bf16), 1, 0)
        elif k == size - 2:
            moved[-1], term_out, *got = sync(moved[-1], term_out, *got)
            out_mine, out_other = core_halves(term_out)
            got = plane_sum_more(result_split, *got)
        elif k == size - 3:
            moved[-1], out_other, *got = sync(moved[-1], out_other, *got)
            output = (middle + plane_sum_end(result_split, *got)).astype(bf16)
            out_half = core_sum(out_mine, out_other)

    grad_qkv = jnp.concatenate([jnp.concatenate(grad_query, axis=0), jnp.concatenate(terms, axis=0)], axis=1)
    *part_split, gain_rows, qkv_theirs, qkv_mine = project_back(index, grad_qkv, full_qkv, normed_one, gathered_in, in_scale)
    got = plane_sum_start(part_split)
    gain_terms = jnp.stack([gain_rows[0], grad_gain_two]).astype(bf16)
    gain_terms = jnp.pad(gain_terms, ((0, LANES - 2), (0, 0))).T
    gain_mine, gain_other = core_halves(gain_terms)
    qkv_half = core_sum(qkv_mine, other_core(qkv_theirs)).reshape(size, shard_rows * PLANE, -1)
    last_half = jnp.concatenate([qkv_half, out_half, core_sum(gain_mine, gain_other)], axis=-1)
    last_total = ring_part(last_half, size - 1)
    sum_gu = plane_swap(after(sum_gu, last_total), 0, 1)
    for k in range(size - 2, -1, -1):
        last_moved = along(last_total, -1, True)
        if k == size - 2:
            *got, last_moved = sync(*got, last_moved)
            got = plane_sum_more(part_split, *got)
        elif k == size - 3:
            *got, last_moved, sum_gu = sync(*got, last_moved, sum_gu)
        last_total = ring_add(last_half, last_moved, k)
    grad_normed_one = plane_sum_end(part_split, *got)
    last_total = plane_swap(last_total, 0, 1).astype(f32).reshape(shard_rows, PLANE, -1)
    scale_one = rms_scale(layer_in)
    weighted = grad_normed_one * gain_one
    input_grad = (
        grad_middle
        + scale_one * weighted
        - layer_in * scale_one**3 * jnp.mean(layer_in * weighted, axis=-1, keepdims=True)
    )
    sum_gu = sum_gu.astype(f32).reshape(shard_rows, PLANE, FF_TILES, 2, ff_part // FF_TILES)
    cuts = np.cumsum([q_part, kv_part, kv_part, out_part])
    sum_query, sum_key, sum_value, sum_out, gain_sum = jnp.split(last_total, cuts, axis=2)
    gain_sum = jnp.sum(gain_sum, axis=1)
    return (
        output[:, None],
        input_grad[:, None],
        gain_sum[:, 0],
        gain_sum[:, 1],
        sum_query.reshape(shard_rows, -1),
        sum_key.reshape(shard_rows, -1),
        sum_value.reshape(shard_rows, -1),
        sum_out.reshape(shard_rows, -1),
        from_ff_parts(sum_gu[:, :, :, 0]),
        from_ff_parts(sum_gu[:, :, :, 1]),
        sum_down.astype(f32),
    )


def solution(mesh):
    blocks = mesh.shape["blk"]
    grid = Mesh(mesh.devices.reshape(2, blocks // PLANE, PLANE), ("stream", "zed", "plane"))
    tokens = P(None, "stream", ("zed", "plane"), None)
    vector = P(("stream", "zed", "plane"))
    matrix = P(("stream", "zed", "plane"), None)
    return jax.shard_map(
        on_device,
        mesh=grid,
        in_specs=(tokens, tokens, P(None, "stream", None), vector, vector) + (matrix,) * 7,
        out_specs=(tokens, tokens, vector, vector) + (matrix,) * 7,
        check_vma=False,
    )
```

```python
import math

import jax
import jax.numpy as jnp
import numpy as np
from jax import lax
from jax.experimental import pallas as pl
from jax.experimental.pallas import tpu as pltpu
from jax.sharding import Mesh
from jax.sharding import PartitionSpec as P

HQ = 16
HK = 8
DH = 96
PLANE = 4
FF_TILES = 2
LANES = 128
VMEM_BYTES = 50 * 1024 * 1024

epsilon = 1e-05
rope_base = 100000.0
masked_score = -1e30
score_scale = 1.0 / math.sqrt(DH)
exp2_scale = score_scale * math.log2(math.e)

LIGHT = pl.CostEstimate(flops=1, bytes_accessed=1, transcendentals=0)
CHUNK_COST = pl.CostEstimate(flops=1, bytes_accessed=6000000, transcendentals=0)

f32 = jnp.float32
bf16 = jnp.bfloat16


def spread(heads):
    table = np.zeros((heads * DH, heads * LANES), np.float32)
    for head in range(heads):
        for i in range(DH):
            lane = i if i < DH // 2 else i + (LANES - DH) // 2
            table[head * DH + i, head * LANES + lane] = 1.0
    return jnp.asarray(table, bf16)


def rms_scale(values):
    return lax.rsqrt(jnp.mean(values * values, axis=-1, keepdims=True) + epsilon)


def dot(a, b):
    return jnp.dot(a, b, preferred_element_type=f32)


def dot_nt(a, b):
    return lax.dot_general(a, b, (((1,), (1,)), ((), ())), preferred_element_type=f32)


def dot_tn(a, b):
    return lax.dot_general(a, b, (((0,), (0,)), ((), ())), preferred_element_type=f32)


def piece_halves(one_ref, one_more_ref, two_ref, two_more_ref):
    return [
        [(one_ref, 0), (one_ref, 1)],
        [(one_more_ref, 0), (one_more_ref, 1)],
        [(two_ref, 0), (two_more_ref, 0)],
        [(two_ref, 1), (two_more_ref, 1)],
    ]


def project_kernel(size, info_ref, one_ref, two_ref, one_more_ref, two_more_ref, cos_ref, sin_ref, e4_ref, *rest):
    blocks, (x_ref, n_ref, q_ref, kv_first_ref, kv_second_ref, w_ref, out_w_ref, gains_ref, scale_ref, pad_s) = rest[: 2 * size], rest[2 * size :]
    rows = blocks[0].shape[0]
    heads = 8 * DH

    @pl.when(pl.program_id(0) == 0)
    def _():
        for i, block in enumerate(blocks):
            core = info_ref[1] if i < size else 1 - info_ref[1]
            start = pl.multiple_of((core * size + lax.rem(info_ref[0] - i % size + size, size)) * rows, rows)
            w_ref[pl.ds(start, rows), :] = block[:, : heads + LANES]
            out_w_ref[pl.ds(start, rows), :] = block[:, heads + LANES :]
            for j in range(2):
                part = dot(block[:, j * 4 * DH : (j + 1) * 4 * DH], e4_ref[...])
                pad_s[pl.ds(start, rows), j * 4 * LANES : (j + 1) * 4 * LANES] = part.astype(bf16)
        rows_to = lax.broadcasted_iota(jnp.int32, (LANES, LANES), 0)
        same = (rows_to == lax.broadcasted_iota(jnp.int32, (LANES, LANES), 1)).astype(bf16)
        gains_ref[...] = dot_nt(same[:8], w_ref[:, heads:])

    tok_rows = one_ref.shape[1]
    for i, halves in enumerate(piece_halves(one_ref, one_more_ref, two_ref, two_more_ref)):

        @pl.when(pl.program_id(0) == i)
        def _(halves=halves):
            for j, (ref, slot) in enumerate(halves):
                x_ref[j * tok_rows : (j + 1) * tok_rows, :] = ref[slot]

    x = x_ref[...].astype(f32)
    scale = rms_scale(x)
    scale_ref[...] = scale
    normed = (x * scale * gains_ref[0:1, :]).astype(bf16)
    n_ref[...] = normed
    pre = dot(normed, pad_s[...])
    cos, sin = cos_ref[...], sin_ref[...]
    parts = []
    for head in range(8):
        piece = pre[:, head * LANES : (head + 1) * LANES]
        if head < 6:
            piece = piece * cos + pltpu.roll(piece, LANES // 2, 1) * sin
        parts.append(piece.astype(bf16))
    q_ref[...] = jnp.concatenate(parts[:4], axis=1)
    kv = dot_nt(jnp.concatenate(parts[4:], axis=1), e4_ref[...]).astype(bf16)
    in_first = pl.program_id(0) < 2

    @pl.when(in_first)
    def _():
        kv_first_ref[...] = kv

    @pl.when(jnp.logical_not(in_first))
    def _():
        kv_second_ref[...] = kv


def project(info, pieces, blocks, cos, sin, e4):
    _, tok_rows, width = pieces[0].shape
    rows, step = 2 * PLANE * tok_rows, 2 * tok_rows
    size = len(blocks) // 2
    cols = blocks[0].shape[1]
    first = 8 * DH + LANES
    whole = lambda a: pl.BlockSpec(a.shape, lambda i, n: (0,) * a.ndim)
    by_row = lambda c: pl.BlockSpec((step, c), lambda i, n: (i, 0))
    return pl.pallas_call(
        lambda *refs: project_kernel(size, *refs),
        grid_spec=pltpu.PrefetchScalarGridSpec(
            num_scalar_prefetch=1,
            grid=(rows // step,),
            in_specs=[whole(a) for a in pieces]
            + [by_row(LANES), by_row(LANES), whole(e4)]
            + [whole(b) for b in blocks],
            out_specs=[
                by_row(width),
                by_row(width),
                by_row(4 * LANES),
                pl.BlockSpec((step, 4 * DH), lambda i, n: (jnp.minimum(i, 1), 0)),
                pl.BlockSpec((step, 4 * DH), lambda i, n: (jnp.maximum(i - 2, 0), 0)),
                pl.BlockSpec((width, first), lambda i, n: (0, 0)),
                pl.BlockSpec((width, cols - first), lambda i, n: (0, 0)),
                pl.BlockSpec((8, width), lambda i, n: (0, 0)),
                by_row(1),
            ],
            scratch_shapes=[pltpu.VMEM((width, 8 * LANES), bf16)],
        ),
        out_shape=[
            jax.ShapeDtypeStruct((rows, width), bf16),
            jax.ShapeDtypeStruct((rows, width), bf16),
            jax.ShapeDtypeStruct((rows, 4 * LANES), bf16),
            jax.ShapeDtypeStruct((rows // 2, 4 * DH), bf16),
            jax.ShapeDtypeStruct((rows // 2, 4 * DH), bf16),
            jax.ShapeDtypeStruct((width, first), bf16),
            jax.ShapeDtypeStruct((width, cols - first), bf16),
            jax.ShapeDtypeStruct((8, width), f32),
            jax.ShapeDtypeStruct((rows, 1), f32),
        ],
        compiler_params=pltpu.CompilerParams(vmem_limit_bytes=VMEM_BYTES),
        cost_estimate=LIGHT,
        name="project",
    )(info, *pieces, cos, sin, e4, *blocks)


def assemble_kernel(size, info_ref, *rest):
    blocks, out_ref = rest[: 2 * size], rest[2 * size]
    rows = blocks[0].shape[0]
    for i, block in enumerate(blocks):
        core = info_ref[1] if i < size else 1 - info_ref[1]
        start = pl.multiple_of((core * size + lax.rem(info_ref[0] - i % size + size, size)) * rows, rows)
        out_ref[pl.ds(start, rows), :] = block[...]


def assemble(info, blocks):
    size = len(blocks) // 2
    rows, width = blocks[0].shape
    step = width // 3 if width % 384 == 0 else width // 4
    return pl.pallas_call(
        lambda *refs: assemble_kernel(size, *refs),
        grid_spec=pltpu.PrefetchScalarGridSpec(
            num_scalar_prefetch=1,
            grid=(width // step,),
            in_specs=[pl.BlockSpec((rows, step), lambda i, n: (0, i)) for _ in blocks],
            out_specs=pl.BlockSpec((len(blocks) * rows, step), lambda i, n: (0, i)),
        ),
        out_shape=jax.ShapeDtypeStruct((len(blocks) * rows, width), blocks[0].dtype),
        compiler_params=pltpu.CompilerParams(vmem_limit_bytes=VMEM_BYTES),
        cost_estimate=LIGHT,
        name="assemble",
    )(info, *blocks)


def allowed_of(info_ref, k, chunk, qpos_ref, qbeg_ref, kpos_ref):
    kpos = kpos_ref[...] + (info_ref[0] - k) * chunk
    return (kpos <= qpos_ref[...]) & (kpos >= qbeg_ref[...])


def useful_of(info_ref, m, k, chunk):
    z = info_ref[0]
    return (k <= z) & ((z - k + 1) * chunk - 1 >= info_ref[2 + m])


def stack_heads(block, h):
    return jnp.concatenate(
        [block[:, (2 * h) * LANES : (2 * h + 1) * LANES], block[:, (2 * h + 1) * LANES : (2 * h + 2) * LANES]], axis=0
    )


def run_kernel(body, info, inputs, outs, aliases, name):
    def spec(entry):
        if isinstance(entry, tuple):
            return pl.BlockSpec(entry[1], lambda i, n: entry[2])
        return pl.BlockSpec(entry.shape, lambda i, n: (0,) * entry.ndim)

    return list(
        pl.pallas_call(
            body,
            grid_spec=pltpu.PrefetchScalarGridSpec(
                num_scalar_prefetch=1,
                grid=(1,),
                in_specs=[spec(entry) for entry in inputs],
                out_specs=[pl.BlockSpec(o.shape, lambda i, n, o=o: (0,) * len(o.shape)) for o in outs],
            ),
            out_shape=outs,
            input_output_aliases=aliases,
            compiler_params=pltpu.CompilerParams(vmem_limit_bytes=VMEM_BYTES),
            cost_estimate=CHUNK_COST,
            name=name,
        )(info, *[entry[0] if isinstance(entry, tuple) else entry for entry in inputs])
    )


def attend_kernel(m, k, last, info_ref, q_ref, kv_ref, qpos_ref, qbeg_ref, kpos_ref, e_ref, *rest):
    chunk = kv_ref.shape[0]
    if k > 0:
        top_in, acc_in, rest = rest[0], rest[1], rest[2:]
    top_ref, acc_ref = rest[0], rest[1]

    def run():
        allowed = allowed_of(info_ref, k, chunk, qpos_ref, qbeg_ref, kpos_ref)
        kv = kv_ref[...]
        q = q_ref[...]
        one_lane = (lax.broadcasted_iota(jnp.int32, (1, LANES), 1) == DH // 2).astype(f32)
        for h in range(2):
            keys = dot(kv, e_ref[:, h * LANES : (h + 1) * LANES]).astype(bf16)
            vals = (dot(kv, e_ref[:, (2 + h) * LANES : (3 + h) * LANES]) + one_lane).astype(bf16)
            s = jnp.where(allowed, dot_nt(keys, stack_heads(q, h)), masked_score)
            new = jnp.max(s, axis=0, keepdims=True)
            if k > 0:
                old = top_in[h]
                new = jnp.maximum(old, new)
            w = jnp.where(allowed, jnp.exp2((s - new) * exp2_scale), 0.0).astype(bf16)
            acc = dot_tn(vals, w)
            if k > 0:
                acc = acc_in[h] * jnp.exp2((old - new) * exp2_scale) + acc
            acc_ref[h] = acc
            top_ref[h] = new

    if k == 0:
        run()
    else:
        useful = useful_of(info_ref, m, k, chunk)
        pl.when(useful)(run)

        @pl.when(jnp.logical_not(useful))
        def _():
            top_ref[...] = top_in[...]
            acc_ref[...] = acc_in[...]

    if last:
        att_ref, low_ref, lse_ref = rest[2:]
        parts = []
        for h in range(2):
            acc = acc_ref[h]
            total = acc[DH // 2 : DH // 2 + 1, :]
            lse_ref[h] = top_ref[h] * exp2_scale + jnp.log2(total)
            flat = (acc / total).T
            rows = flat.shape[0] // 2
            parts += [flat[:rows], flat[rows:]]
        att = jnp.concatenate(parts, axis=1)
        att_ref[...] = att
        low_ref[...] = dot_nt(att.astype(bf16), e_ref[...]).astype(bf16)


def attend(m, k, last, info, q, kv, qpos, qbeg, kpos, e4, state):
    rows = q[1][0]
    outs = [jax.ShapeDtypeStruct((2, 1, 2 * rows), f32), jax.ShapeDtypeStruct((2, LANES, 2 * rows), f32)]
    if last:
        outs += [
            jax.ShapeDtypeStruct((rows, 4 * LANES), f32),
            jax.ShapeDtypeStruct((rows, 4 * DH), bf16),
            jax.ShapeDtypeStruct((2, 1, 2 * rows), f32),
        ]
    return run_kernel(
        lambda *refs: attend_kernel(m, k, last, *refs),
        info,
        [q, kv, qpos, qbeg, kpos, e4] + state,
        outs,
        {7: 0, 8: 1} if k > 0 else {},
        "attend",
    )


def attend_back_kernel(
    m, k, first, last, info_ref, q_ref, kv_ref, lse_ref, qpos_ref, qbeg_ref, kpos_ref, cosk_ref, sink_ref, e_ref, *rest
):
    chunk = kv_ref.shape[0]
    if first:
        g_ref, att_ref, rest = rest[0], rest[1], rest[2:]
        go_ref, delta_ref, dq_ref, dkv_ref = rest[:4]
        go = dot(g_ref[...], e_ref[...])
        for h in range(2):
            go_h = stack_heads(go, h)
            go_ref[h] = go_h.astype(bf16)
            prod = go_h * stack_heads(att_ref[...], h)
            delta_ref[h] = jnp.sum(prod.T, axis=0, keepdims=True)
    else:
        go_ref, delta_ref, dq_in, moved_ref, rest = rest[0], rest[1], rest[2], rest[3], rest[4:]
        dq_ref, dkv_ref = rest[:2]

    def run():
        allowed = allowed_of(info_ref, k, chunk, qpos_ref, qbeg_ref, kpos_ref)
        kv = kv_ref[...]
        q = q_ref[...]
        cosk, sink = cosk_ref[...], sink_ref[...]
        grad_keys, grad_vals = [], []
        for h in range(2):
            keys = dot(kv, e_ref[:, h * LANES : (h + 1) * LANES]).astype(bf16)
            vals = dot(kv, e_ref[:, (2 + h) * LANES : (3 + h) * LANES]).astype(bf16)
            q_h = stack_heads(q, h)
            go_h = go_ref[h]
            s = dot_nt(keys, q_h)
            w = jnp.where(allowed, jnp.exp2(s * exp2_scale - lse_ref[h]), 0.0)
            grad_vals.append(dot(w.astype(bf16), go_h).astype(bf16))
            ds = (w * (dot_nt(vals, go_h) - delta_ref[h])).astype(bf16)
            dq = dot_tn(keys, ds)
            dq_ref[h] = dq if first else dq_in[h] + dq
            gk = dot(ds, q_h) * score_scale
            gk = gk * cosk + pltpu.roll(gk * sink, LANES // 2, 1)
            grad_keys.append(gk.astype(bf16))
        total = dot_nt(jnp.concatenate(grad_keys + grad_vals, axis=1), e_ref[...])
        if not first:
            total = total + moved_ref[...].astype(f32)
        dkv_ref[...] = total.astype(bf16)

    if k == 0:
        run()
    else:
        useful = useful_of(info_ref, m, k, chunk)
        pl.when(useful)(run)

        @pl.when(jnp.logical_not(useful))
        def _():
            dkv_ref[...] = jnp.zeros(dkv_ref.shape, bf16) if first else moved_ref[...]
            dq_ref[...] = jnp.zeros(dq_ref.shape, f32) if first else dq_in[...]

    if last:
        out_ref = rest[-1]
        parts = []
        for h in range(2):
            flat = dq_ref[h].T * score_scale
            rows = flat.shape[0] // 2
            for piece in (flat[:rows], flat[rows:]):
                parts.append((piece * cosk_ref[...] + pltpu.roll(piece * sink_ref[...], LANES // 2, 1)).astype(bf16))
        out_ref[...] = dot_nt(jnp.concatenate(parts, axis=1), e_ref[...]).astype(bf16)


def attend_back(m, k, first, last, info, q, kv, lse, qpos, qbeg, kpos, cosk, sink, e4, state):
    rows = q[1][0]
    outs = []
    if first:
        outs += [jax.ShapeDtypeStruct((2, 2 * rows, LANES), bf16), jax.ShapeDtypeStruct((2, 1, 2 * rows), f32)]
    outs += [jax.ShapeDtypeStruct((2, LANES, 2 * rows), f32), jax.ShapeDtypeStruct((rows, 4 * DH), bf16)]
    if last:
        outs += [jax.ShapeDtypeStruct((rows, 4 * DH), bf16)]
    return run_kernel(
        lambda *refs: attend_back_kernel(m, k, first, last, *refs),
        info,
        [q, kv, lse, qpos, qbeg, kpos, cosk, sink, e4] + state,
        outs,
        {} if first else {12: 0},
        "attend_back",
    )


def store_split(sum_of, tok_rows, first_ref, second_ref, keep_first_ref, keep_second_ref):
    for i, slot in enumerate((1, 3)):
        first_ref[i] = sum_of(slot * tok_rows, tok_rows).astype(bf16)
        keep_first_ref[i] = sum_of((slot - 1) * tok_rows, tok_rows)
    for i in range(2):
        second_ref[i] = sum_of((PLANE + 2 + i) * tok_rows, tok_rows).astype(bf16)
        keep_second_ref[i] = sum_of((PLANE + i) * tok_rows, tok_rows)


def split_outs(tok_rows, width):
    return [jax.ShapeDtypeStruct((2, tok_rows, width), kind) for kind in (bf16, bf16, f32, f32)]


def dot_split_kernel(tok_rows, a_ref, w_ref, *rest):
    acc_s = rest[-1]
    acc_s[...] = dot(a_ref[...], w_ref[...])
    store_split(lambda start, n: acc_s[start : start + n, :], tok_rows, *rest[:-1])


def dot_split(a, w):
    rows, inner = a.shape
    tok_rows = rows // (2 * PLANE)
    width = w.shape[1]
    step = width // 3
    outs = split_outs(tok_rows, width)
    return list(
        pl.pallas_call(
            lambda *refs: dot_split_kernel(tok_rows, *refs),
            grid=(3,),
            in_specs=[pl.BlockSpec((rows, inner), lambda i: (0, 0)), pl.BlockSpec((inner, step), lambda i: (0, i))],
            out_specs=[pl.BlockSpec((2, tok_rows, step), lambda i: (0, 0, i)) for _ in outs],
            out_shape=outs,
            scratch_shapes=[pltpu.VMEM((rows, step), f32)],
            compiler_params=pltpu.CompilerParams(vmem_limit_bytes=VMEM_BYTES),
            cost_estimate=LIGHT,
            name="dot_split",
        )(a, w)
    )


def ffn_kernel(size, tok_rows, info_ref, one_ref, two_ref, one_more_ref, two_more_ref, g_ref, *rest):
    gu_blocks, down_blocks, rest = rest[: 2 * size], rest[2 * size : 4 * size], rest[4 * size :]
    hidden_ref, *outs = rest[:5]
    gu_theirs_ref, gu_mine_ref, down_theirs_ref, down_mine_ref = rest[5:9]
    gu_s, down_s, acc_s, flat_s, grad_s, n_ref, sems = rest[9:]
    f, last = pl.program_id(0), pl.num_programs(0) - 1
    units = hidden_ref.shape[1]
    half = flat_s.shape[0] // 2

    def place(i, rows):
        core = info_ref[1] if i < size else 1 - info_ref[1]
        return pl.ds(pl.multiple_of((core * size + lax.rem(info_ref[0] - i % size + size, size)) * rows, rows), rows)

    @pl.when(f == 0)
    def _():
        copies = []
        for i, halves in enumerate(piece_halves(one_ref, one_more_ref, two_ref, two_more_ref)):
            for j, (ref, slot) in enumerate(halves):
                at = pl.ds((2 * i + j) * tok_rows, tok_rows)
                copies.append(pltpu.make_async_copy(ref.at[slot], n_ref.at[at], sems.at[2 * i + j]))
                copies[-1].start()
        acc_s[...] = jnp.zeros(acc_s.shape, f32)
        for copy in copies:
            copy.wait()
        flat_s[...] = n_ref[...].T
        for i, block in enumerate(down_blocks):
            down_s[place(i, block.shape[0]), :] = block[...]

    for i, block in enumerate(gu_blocks):
        gu_s[place(i, block.shape[0]), :] = block[...]
    w_down = down_s.at[pl.ds(pl.multiple_of(f * units, units), units)]
    step = 4 * tok_rows

    @pl.loop(0, n_ref.shape[0] // step)
    def _(r):
        at = pl.ds(pl.multiple_of(r * step, step), step)
        pre = dot(n_ref[at, :], gu_s[...])
        grad_hidden = dot_nt(g_ref[at, :], w_down[...])
        gate_pre, up_pre = pre[:, :units], pre[:, units:]
        sigmoid_gate = jax.nn.sigmoid(gate_pre)
        silu_gate = gate_pre * sigmoid_gate
        hidden_ref[at, :] = (silu_gate * up_pre).astype(bf16)
        grad_gate = grad_hidden * up_pre * sigmoid_gate * (1.0 + gate_pre * (1.0 - sigmoid_gate))
        both = jnp.concatenate([grad_gate.astype(bf16), (grad_hidden * silu_gate).astype(bf16)], axis=1)
        grad_s[at, :] = both
        acc_s[at, :] += dot_nt(both, gu_s[...])

    core = info_ref[1]
    gu_mine_ref[...] = dot(flat_s[pl.ds(pl.multiple_of(core * half, half), half), :], grad_s[...]).astype(bf16)
    gu_theirs_ref[...] = dot(flat_s[pl.ds(pl.multiple_of((1 - core) * half, half), half), :], grad_s[...]).astype(bf16)
    term_down = dot_tn(hidden_ref[...], g_ref[...]).astype(bf16)
    is_mine = lax.div(f, pl.num_programs(0) // 2) == core

    @pl.when(is_mine)
    def _():
        down_mine_ref[...] = term_down

    @pl.when(jnp.logical_not(is_mine))
    def _():
        down_theirs_ref[...] = term_down

    @pl.when(f == last)
    def _():
        store_split(lambda start, n: acc_s[start : start + n, :], tok_rows, *outs)


def ffn(info, pieces, grad_mlp, gu_blocks, down_blocks):
    rows, width = grad_mlp.shape
    size = len(gu_blocks) // 2
    tok_rows = rows // (2 * PLANE)
    ff_part = gu_blocks[0].shape[1] // 2
    units = ff_part // FF_TILES
    whole = lambda a: pl.BlockSpec(a.shape, lambda f, n: (0,) * a.ndim, pipeline_mode=pl.Buffered(1))
    outs = split_outs(tok_rows, width)
    gu_half = pl.BlockSpec((width // 2, 2 * units), lambda f, n: (0, f))

    def down_half(core_of):
        return pl.BlockSpec((units, width), lambda f, n: (jnp.clip(f - core_of(n) * (FF_TILES // 2), 0, FF_TILES // 2 - 1), 0))

    return list(
        pl.pallas_call(
            lambda *refs: ffn_kernel(size, tok_rows, *refs),
            grid_spec=pltpu.PrefetchScalarGridSpec(
                num_scalar_prefetch=1,
                grid=(FF_TILES,),
                in_specs=[pl.BlockSpec(memory_space=pl.ANY) for _ in pieces]
                + [whole(grad_mlp)]
                + [pl.BlockSpec((block.shape[0], 2 * units), lambda f, n: (0, f)) for block in gu_blocks]
                + [whole(block) for block in down_blocks],
                out_specs=[pl.BlockSpec((rows, units), lambda f, n: (0, f))]
                + [pl.BlockSpec(o.shape, lambda f, n: (0, 0, 0), pipeline_mode=pl.Buffered(1)) for o in outs]
                + [gu_half, gu_half, down_half(lambda n: 1 - n[1]), down_half(lambda n: n[1])],
                scratch_shapes=[
                    pltpu.VMEM((width, 2 * units), bf16),
                    pltpu.VMEM((ff_part, width), bf16),
                    pltpu.VMEM((rows, width), f32),
                    pltpu.VMEM((width, rows), bf16),
                    pltpu.VMEM((rows, 2 * units), bf16),
                    pltpu.VMEM((rows, width), bf16),
                    pltpu.SemaphoreType.DMA((2 * PLANE,)),
                ],
            ),
            out_shape=[jax.ShapeDtypeStruct((rows, ff_part), bf16)]
            + outs
            + [jax.ShapeDtypeStruct((width // 2, 2 * ff_part), bf16)] * 2
            + [jax.ShapeDtypeStruct((ff_part // 2, width), bf16)] * 2,
            compiler_params=pltpu.CompilerParams(vmem_limit_bytes=58 * 1024 * 1024),
            cost_estimate=LIGHT,
            name="ffn",
        )(info, *pieces, grad_mlp, *gu_blocks, *down_blocks)
    )


def project_back_kernel(tok_rows, parts, info_ref, *rest):
    grads, (w_ref, n_ref, x_ref, scale_ref), rest = rest[:parts], rest[parts : parts + 4], rest[parts + 4 :]
    first_ref, second_ref, keep_first_ref, keep_second_ref, gain_ref, theirs_ref, mine_ref, acc_s, g_ref = rest
    part_rows, part_width = grads[0].shape

    @pl.when(pl.program_id(0) == 0)
    def _():
        for i, grad_ref in enumerate(grads):
            m, j = i % (parts // 2), i // (parts // 2)
            g_ref[m * part_rows : (m + 1) * part_rows, j * part_width : (j + 1) * part_width] = grad_ref[...]

    rows = 2 * tok_rows
    total = jnp.zeros((1, acc_s.shape[1]), f32)
    for i in range(g_ref.shape[0] // rows):
        at = slice(i * rows, (i + 1) * rows)
        acc = dot_nt(g_ref[at, :], w_ref[...])
        acc_s[at, :] = acc
        total = total + jnp.sum(acc * x_ref[at, :].astype(f32) * scale_ref[at, :], axis=0, keepdims=True)
    gain_ref[...] = jnp.broadcast_to(total, gain_ref.shape)
    store_split(lambda start, n: acc_s[start : start + n, :], tok_rows, first_ref, second_ref, keep_first_ref, keep_second_ref)
    term = dot_tn(n_ref[...], g_ref[...]).astype(bf16)
    is_mine = pl.program_id(0) == info_ref[1]

    @pl.when(is_mine)
    def _():
        mine_ref[...] = term

    @pl.when(jnp.logical_not(is_mine))
    def _():
        theirs_ref[...] = term


def project_back(info, grads, w, normed, x, scale):
    rows, width = normed.shape
    inner = 2 * grads[0].shape[1]
    tok_rows = rows // (2 * PLANE)
    half = width // 2
    outs = split_outs(tok_rows, width)
    column = pl.BlockSpec((rows, half), lambda i, n: (0, i))
    out_whole = pl.BlockSpec((half, inner), lambda i, n: (0, 0))
    return list(
        pl.pallas_call(
            lambda *refs: project_back_kernel(tok_rows, len(grads), *refs),
            grid_spec=pltpu.PrefetchScalarGridSpec(
                num_scalar_prefetch=1,
                grid=(2,),
                in_specs=[pl.BlockSpec(g.shape, lambda i, n: (0, 0)) for g in grads]
                + [
                    pl.BlockSpec((half, inner), lambda i, n: (i, 0)),
                    column,
                    column,
                    pl.BlockSpec((rows, 1), lambda i, n: (0, 0)),
                ],
                out_specs=[pl.BlockSpec((2, tok_rows, half), lambda i, n: (0, 0, i)) for _ in outs]
                + [pl.BlockSpec((8, half), lambda i, n: (0, i)), out_whole, out_whole],
                scratch_shapes=[pltpu.VMEM((rows, half), f32), pltpu.VMEM((rows, inner), bf16)],
            ),
            out_shape=outs
            + [jax.ShapeDtypeStruct((8, width), f32)]
            + [jax.ShapeDtypeStruct((half, inner), bf16)] * 2,
            compiler_params=pltpu.CompilerParams(vmem_limit_bytes=VMEM_BYTES),
            cost_estimate=LIGHT,
            name="project_back",
        )(info, *grads, w, normed, x, scale)
    )


def beside(value, bit):
    return lax.ppermute(value, "plane", [(i, i ^ bit) for i in range(PLANE)])


def other_core(value):
    return lax.ppermute(value, "stream", [(0, 1), (1, 0)])


def along(value, step, wrap):
    size = lax.axis_size("zed")
    pairs = [(i, (i + step) % size) for i in range(size) if wrap or 0 <= i + step < size]
    return lax.ppermute(value, "zed", pairs)


def plane_gather_start(own):
    return [own[0], own[1], beside(own[0], 1), beside(own[1], 2)]


def plane_gather_more(first, second, first_got, second_got):
    pair_one, pair_two = jnp.stack([first, first_got]), jnp.stack([second, second_got])
    return [pair_one, pair_two, beside(pair_one, 2), beside(pair_two, 1)]


def plane_gather_end(pair_one, pair_two, first_more, second_more):
    blocks = [pair_one, first_more, pair_two[:1], second_more[:1], pair_two[1:], second_more[1:]]
    return jnp.concatenate(blocks).reshape(-1, pair_one.shape[-1])


def plane_sum_start(split):
    return [beside(split[0], 1), beside(split[1], 2)]


def plane_sum_more(split, got_first, got_second):
    keep_first, keep_second = split[2], split[3]
    more_first = beside((keep_first[1] + got_first[1]).astype(bf16), 2)
    more_second = beside((keep_second[1] + got_second[1]).astype(bf16), 1)
    return [got_first[0], got_second[0], more_first, more_second]


def plane_sum_end(split, got_first, got_second, more_first, more_second):
    return jnp.stack([split[2][0] + got_first + more_first, split[3][0] + got_second + more_second])


def after(value, *earlier):
    return lax.optimization_barrier((value,) + earlier)[0]


def sync(*values):
    return list(lax.optimization_barrier(values))


def core_halves(full):
    size = lax.axis_size("zed")
    s = lax.axis_index("stream")
    full = full.reshape((2, size, -1) + full.shape[1:])
    mine = lax.dynamic_index_in_dim(full, s, 0, keepdims=False)
    theirs = lax.dynamic_index_in_dim(full, 1 - s, 0, keepdims=False)
    return mine, other_core(theirs)


def core_sum(mine, other):
    return (mine.astype(f32) + other.astype(f32)).astype(bf16)


def ring_part(half, k):
    size = lax.axis_size("zed")
    z = lax.axis_index("zed")
    return lax.dynamic_index_in_dim(half, lax.rem(z - k + size, size), 0, keepdims=False)


def ring_add(half, moved, k):
    return (moved.astype(f32) + ring_part(half, k).astype(f32)).astype(bf16)


def plane_swap(value, split, concat):
    return lax.all_to_all(value, "plane", split_axis=split, concat_axis=concat, tiled=True)


def on_device(inputs, cotangent, seq_lengths, gain_attn, gain_ffn, w_query, w_key, w_value, w_out, w_gate, w_up, w_down):
    size = lax.axis_size("zed")
    s, z, p = lax.axis_index("stream"), lax.axis_index("zed"), lax.axis_index("plane")
    micro, _, tok_rows, width = inputs.shape
    chunk = PLANE * tok_rows
    tokens = micro * chunk
    shard_rows = w_query.shape[0]
    ff_block = w_down.shape[0]
    ff_blocks = 2 * size
    ff_part = ff_blocks * ff_block
    q_part, kv_part = HQ * DH // PLANE, HK * DH // PLANE
    out_part = width // PLANE
    e4 = spread(4)

    def by_part(weight):
        return weight.reshape(shard_rows, PLANE, -1)

    def by_ff_part(weight):
        return weight.reshape(shard_rows, ff_blocks, PLANE, ff_block).transpose(0, 2, 1, 3).reshape(shard_rows, PLANE, -1)

    def from_ff_parts(term):
        return term.reshape(shard_rows, PLANE, ff_blocks, ff_block).transpose(0, 2, 1, 3).reshape(shard_rows, -1)

    own_in = inputs[:, 0]
    own_cot = cotangent[:, 0]
    gains = jnp.stack([gain_attn, gain_ffn], axis=1)
    gains = jnp.broadcast_to(jnp.pad(gains, ((0, 0), (0, LANES - 2)))[:, None], (shard_rows, PLANE, LANES))
    qkv_bundle = jnp.concatenate([by_part(w_query), by_part(w_key), by_part(w_value), gains, by_part(w_out)], axis=2)
    qkv_block = plane_swap(qkv_bundle.reshape(shard_rows, -1), 1, 0)
    tiled = (shard_rows, PLANE, FF_TILES, ff_part // FF_TILES)
    ffn_bundle = jnp.stack([by_ff_part(w_gate).reshape(tiled), by_ff_part(w_up).reshape(tiled)], axis=3).reshape(shard_rows, -1)
    qkv_blocks = [qkv_block]
    for _ in range(size - 1):
        qkv_blocks.append(along(qkv_blocks[-1], 1, True))
    ffn_block = plane_swap(after(ffn_bundle, qkv_block), 1, 0)
    pieces = sync(*plane_gather_start(after(own_in, qkv_block)))
    *in_pieces, qkv_blocks[-1] = sync(*plane_gather_more(*pieces), qkv_blocks[-1])
    qkv_other = [other_core(block) for block in qkv_blocks]
    gu_blocks = [after(ffn_block, qkv_blocks[-1])]
    gu_blocks.append(along(gu_blocks[0], 1, True))

    slot_place = ((jnp.arange(PLANE, dtype=jnp.int32) ^ p)[:, None] * tok_rows + jnp.arange(tok_rows, dtype=jnp.int32)[None, :]).reshape(chunk)
    chunk_place = (z - jnp.arange(size, dtype=jnp.int32))[:, None] * chunk + slot_place[None, :]
    lengths = seq_lengths[:, 0]
    seq_ends = jnp.cumsum(lengths, axis=1)
    begins = jnp.sum(
        jnp.where(seq_ends[:, None, None, :] <= chunk_place[None, :, :, None], lengths[:, None, None, :], 0), axis=-1
    )
    own_begin = begins[:, 0]
    lane = np.arange(LANES)
    place_in_half = lane % (LANES // 2)
    real = place_in_half < DH // 2
    frequency = jnp.where(
        real, rope_base ** (-2.0 * jnp.asarray(np.minimum(place_in_half, DH // 2 - 1), f32) / DH), 0.0
    )
    rope_place = (chunk_place[None] - begins).astype(f32)

    def tables(place):
        angles = jnp.maximum(place, 0.0)[..., None] * frequency
        signs = jnp.asarray(np.where(real, np.where(lane < LANES // 2, -1.0, 1.0), 0.0), f32)
        return jnp.where(real, jnp.cos(angles), 0.0), jnp.sin(angles) * signs

    cos, sin = tables(after(rope_place[:, 0], qkv_block))
    index = jnp.stack([z, s]).astype(jnp.int32)
    info = jnp.concatenate([index, jnp.min(own_begin, axis=1)])
    qpos = jnp.tile(chunk_place[0], 2)[None]
    qbeg = jnp.tile(own_begin, (1, 2))[:, None]
    kpos = slot_place[:, None]

    gathered_in, normed_one, q_rot, *kv_own, full_qkv, full_oc, full_gains, in_scale = project(
        index, in_pieces, qkv_blocks + qkv_other, cos.reshape(tokens, LANES), sin.reshape(tokens, LANES), e4
    )
    gain_one, gain_two = full_gains[0:1], full_gains[1:2]
    full_out = plane_swap(full_oc, 0, 1)
    cot_pieces = plane_gather_start(after(own_cot, *kv_own))
    q_rot = [(q_rot, (chunk, 4 * LANES), (m, 0)) for m in range(micro)]
    kv_windows = [[piece] for piece in kv_own]
    kv_pieces = [[piece] for piece in kv_own]
    qbeg = [(qbeg, (None, 1, 2 * chunk), (m, 0, 0)) for m in range(micro)]
    states = [[] for _ in range(micro)]
    for k in range(size):
        if k < size - 1:
            arrived = [along(kv_pieces[m][k], 1, False) for m in range(micro)]
        for m in range(micro):
            states[m] = attend(m, k, k == size - 1, info, q_rot[m], kv_windows[m][k], qpos, qbeg[m], kpos, e4, states[m])
        if k < size - 1:
            tops = [state[0] for state in states]
            if k == 0:
                tops[0], tops[1], arrived[0], arrived[1], gu_blocks[1], *cot_pieces = sync(
                    *tops, *arrived, gu_blocks[1], *cot_pieces
                )
                cot_pieces = plane_gather_more(*cot_pieces)
            elif k == 1:
                tops[0], tops[1], arrived[0], arrived[1], full_out, *cot_pieces = sync(*tops, *arrived, full_out, *cot_pieces)
            else:
                tops[0], tops[1], arrived[0], arrived[1] = sync(*tops, *arrived)
            for m in range(micro):
                states[m] = [tops[m], states[m][1]]
                kv_pieces[m].append(arrived[m])
                kv_windows[m].append(arrived[m])
    kv_there = [pieces[-1] for pieces in kv_pieces]
    attended, lse = [state[2] for state in states], [state[4] for state in states]
    attn_low = jnp.concatenate([state[3] for state in states], axis=0)
    gathered_cot = plane_gather_end(*cot_pieces)

    gu_blocks[1], down_block, rope_place = sync(gu_blocks[1], w_down, rope_place, *kv_there)[:3]
    down_blocks = [down_block, along(down_block, 1, True)]
    branch_split = dot_split(attn_low, full_out)
    branch_split = sync(*branch_split, down_blocks[1])
    down_blocks[1] = branch_split.pop()
    gu_blocks.append(along(after(gu_blocks[1], down_blocks[1]), 1, True))
    *got, gu_blocks[2] = sync(*plane_sum_start(branch_split), gu_blocks[2])
    down_blocks.append(along(after(down_blocks[1], gu_blocks[2]), 1, True))
    cos_all, sin_all = tables(after(rope_place, gu_blocks[2]))
    *got, down_blocks[2], cos_all, sin_all = sync(*plane_sum_more(branch_split, *got), down_blocks[2], cos_all, sin_all)
    layer_in = own_in.astype(f32)
    middle = layer_in + plane_sum_end(branch_split, *got)
    scale_two = rms_scale(middle)
    pieces = plane_gather_start((middle * scale_two * gain_two).astype(bf16))
    for k in range(2, size - 1):
        down_blocks.append(along(down_blocks[k], 1, True))
    *pieces, down_blocks[-1] = sync(*pieces, down_blocks[-1])
    for k in range(2, size - 1):
        gu_blocks.append(along(after(gu_blocks[k], down_blocks[-1]), 1, True))
    *pieces, gu_blocks[-1] = sync(*plane_gather_more(*pieces), gu_blocks[-1])

    gu_all = gu_blocks + [other_core(block) for block in gu_blocks]
    down_all = down_blocks + [other_core(block) for block in down_blocks]
    hidden, *outs = ffn(index, pieces, gathered_cot, gu_all, down_all)
    normed_split, (gu_theirs, gu_mine, down_theirs, down_mine) = outs[:4], outs[4:]
    got = plane_sum_start(normed_split)
    gu_half = core_sum(gu_mine, other_core(gu_theirs)).reshape(size, -1, 2 * ff_part)
    down_half = core_sum(down_mine, other_core(down_theirs)).reshape(size, -1, width)
    gu_total, down_total = ring_part(gu_half, size - 1), ring_part(down_half, size - 1)
    *got, gu_total, down_total = sync(*got, gu_total, down_total)
    gu_moved, down_moved = along(gu_total, -1, True), along(down_total, -1, True)
    got = sync(*plane_sum_more(normed_split, *got))
    grad_normed_two = plane_sum_end(normed_split, *got)
    grad_y = own_cot.astype(f32)
    grad_gain_two = jnp.sum(grad_normed_two * middle * scale_two, axis=(0, 1))
    weighted = grad_normed_two * gain_two
    grad_middle = (
        grad_y
        + scale_two * weighted
        - middle * scale_two**3 * jnp.mean(middle * weighted, axis=-1, keepdims=True)
    )
    pieces = plane_gather_start(grad_middle.astype(bf16))
    *pieces, gu_moved, down_moved = sync(*pieces, gu_moved, down_moved)
    gu_total, down_total = ring_add(gu_half, gu_moved, size - 2), ring_add(down_half, down_moved, size - 2)
    gu_moved, down_moved = along(gu_total, -1, True), along(down_total, -1, True)
    full_down = assemble(index, [after(down_all[0], gu_total)] + down_all[1:])
    result_split = dot_split(after(hidden, gu_total), full_down)
    pieces = plane_gather_more(*pieces)
    for k in range(size - 3, -1, -1):
        gu_total, down_total = ring_add(gu_half, gu_moved, k), ring_add(down_half, down_moved, k)
        if k == size - 3:
            *pieces, gu_total, down_total, result_split[0] = sync(*pieces, gu_total, down_total, result_split[0])
        if k > 0:
            gu_moved, down_moved = along(gu_total, -1, True), along(down_total, -1, True)
    sum_gu, sum_down = gu_total, down_total
    grad_branch = plane_gather_end(*pieces)
    grad_attn = dot_nt(grad_branch, full_out).astype(bf16)

    attended[-1] = after(attended[-1], sum_down)
    states = [[(grad_attn, (chunk, q_part), (m, 0)), attended[m]] for m in range(micro)]
    grad_query = [None] * micro
    terms = [None] * micro
    for k in range(size - 1, -1, -1):
        first = k == size - 1
        for m in range(micro):
            outs = attend_back(
                m, k, first, k == 0, info, q_rot[m], kv_windows[m][k], lse[m], qpos, qbeg[m], kpos,
                (cos_all, (None, None, chunk, LANES), (m, k, 0, 0)), (sin_all, (None, None, chunk, LANES), (m, k, 0, 0)),
                e4, states[m] if first else states[m] + [moved[m]],
            )
            states[m] = outs[:3] if first else states[m][:2] + [outs[0]]
            terms[m] = outs[3] if first else outs[1]
            if k == 0:
                grad_query[m] = outs[-1]
        if k > 0:
            moved = [along(term, -1, False) for term in terms]
            moved[0] = after(moved[0], terms[-1], *([sum_gu, sum_down] if first else []))
        if first:
            got = plane_sum_start(sync(*result_split[:2], *terms)[:2])
            term_out = plane_swap(dot_tn(attn_low, after(grad_branch, *terms)).astype(bf16), 1, 0)
        elif k == size - 2:
            moved[-1], term_out, *got = sync(moved[-1], term_out, *got)
            out_mine, out_other = core_halves(term_out)
            got = plane_sum_more(result_split, *got)
        elif k == size - 3:
            moved[-1], out_other, *got = sync(moved[-1], out_other, *got)
            output = (middle + plane_sum_end(result_split, *got)).astype(bf16)
            out_half = core_sum(out_mine, out_other)

    *part_split, gain_rows, qkv_theirs, qkv_mine = project_back(index, grad_query + terms, full_qkv, normed_one, gathered_in, in_scale)
    got = plane_sum_start(part_split)
    gain_terms = jnp.stack([gain_rows[0], grad_gain_two]).astype(bf16)
    gain_terms = jnp.pad(gain_terms, ((0, LANES - 2), (0, 0))).T
    gain_mine, gain_other = core_halves(gain_terms)
    qkv_half = core_sum(qkv_mine, other_core(qkv_theirs)).reshape(size, shard_rows * PLANE, -1)
    last_half = jnp.concatenate([qkv_half, out_half, core_sum(gain_mine, gain_other)], axis=-1)
    last_total = ring_part(last_half, size - 1)
    sum_gu = plane_swap(after(sum_gu, last_total), 0, 1)
    for k in range(size - 2, -1, -1):
        last_moved = along(last_total, -1, True)
        if k == size - 2:
            *got, last_moved = sync(*got, last_moved)
            got = plane_sum_more(part_split, *got)
        elif k == size - 3:
            *got, last_moved, sum_gu = sync(*got, last_moved, sum_gu)
        last_total = ring_add(last_half, last_moved, k)
    grad_normed_one = plane_sum_end(part_split, *got)
    last_total = plane_swap(last_total, 0, 1).astype(f32).reshape(shard_rows, PLANE, -1)
    scale_one = rms_scale(layer_in)
    weighted = grad_normed_one * gain_one
    input_grad = (
        grad_middle
        + scale_one * weighted
        - layer_in * scale_one**3 * jnp.mean(layer_in * weighted, axis=-1, keepdims=True)
    )
    sum_gu = sum_gu.astype(f32).reshape(shard_rows, PLANE, FF_TILES, 2, ff_part // FF_TILES)
    cuts = np.cumsum([q_part, kv_part, kv_part, out_part])
    sum_query, sum_key, sum_value, sum_out, gain_sum = jnp.split(last_total, cuts, axis=2)
    gain_sum = jnp.sum(gain_sum, axis=1)
    return (
        output[:, None],
        input_grad[:, None],
        gain_sum[:, 0],
        gain_sum[:, 1],
        sum_query.reshape(shard_rows, -1),
        sum_key.reshape(shard_rows, -1),
        sum_value.reshape(shard_rows, -1),
        sum_out.reshape(shard_rows, -1),
        from_ff_parts(sum_gu[:, :, :, 0]),
        from_ff_parts(sum_gu[:, :, :, 1]),
        sum_down.astype(f32),
    )


def solution(mesh):
    blocks = mesh.shape["blk"]
    grid = Mesh(mesh.devices.reshape(2, blocks // PLANE, PLANE), ("stream", "zed", "plane"))
    tokens = P(None, "stream", ("zed", "plane"), None)
    vector = P(("stream", "zed", "plane"))
    matrix = P(("stream", "zed", "plane"), None)
    return jax.shard_map(
        on_device,
        mesh=grid,
        in_specs=(tokens, tokens, P(None, "stream", None), vector, vector) + (matrix,) * 7,
        out_specs=(tokens, tokens, vector, vector) + (matrix,) * 7,
        check_vma=False,
    )
```

```python
import math

import jax
import jax.numpy as jnp
import numpy as np
from jax import lax
from jax.experimental import pallas as pl
from jax.experimental.pallas import tpu as pltpu
from jax.sharding import Mesh
from jax.sharding import PartitionSpec as P

HQ = 16
HK = 8
DH = 96
PLANE = 4
FF_TILES = 2
LANES = 128
VMEM_BYTES = 50 * 1024 * 1024

epsilon = 1e-05
rope_base = 100000.0
masked_score = -1e30
score_scale = 1.0 / math.sqrt(DH)
exp2_scale = score_scale * math.log2(math.e)

LIGHT = pl.CostEstimate(flops=1, bytes_accessed=1, transcendentals=0)
CHUNK_COST = pl.CostEstimate(flops=1, bytes_accessed=6000000, transcendentals=0)

f32 = jnp.float32
bf16 = jnp.bfloat16


def spread(heads):
    table = np.zeros((heads * DH, heads * LANES), np.float32)
    for head in range(heads):
        for i in range(DH):
            lane = i if i < DH // 2 else i + (LANES - DH) // 2
            table[head * DH + i, head * LANES + lane] = 1.0
    return jnp.asarray(table, bf16)


def rms_scale(values):
    return lax.rsqrt(jnp.mean(values * values, axis=-1, keepdims=True) + epsilon)


def dot(a, b):
    return jnp.dot(a, b, preferred_element_type=f32)


def dot_nt(a, b):
    return lax.dot_general(a, b, (((1,), (1,)), ((), ())), preferred_element_type=f32)


def dot_tn(a, b):
    return lax.dot_general(a, b, (((0,), (0,)), ((), ())), preferred_element_type=f32)


def piece_halves(one_ref, one_more_ref, two_ref, two_more_ref):
    return [
        [(one_ref, 0), (one_ref, 1)],
        [(one_more_ref, 0), (one_more_ref, 1)],
        [(two_ref, 0), (two_more_ref, 0)],
        [(two_ref, 1), (two_more_ref, 1)],
    ]


def project_kernel(size, info_ref, one_ref, two_ref, one_more_ref, two_more_ref, cos_ref, sin_ref, e4_ref, *rest):
    blocks, (x_ref, n_ref, q_ref, kv_first_ref, kv_second_ref, w_ref, out_w_ref, gains_ref, scale_ref, pad_s) = rest[: 2 * size], rest[2 * size :]
    rows = blocks[0].shape[0]
    heads = 8 * DH

    @pl.when(pl.program_id(0) == 0)
    def _():
        for i, block in enumerate(blocks):
            core = info_ref[1] if i < size else 1 - info_ref[1]
            start = pl.multiple_of((core * size + lax.rem(info_ref[0] - i % size + size, size)) * rows, rows)
            w_ref[pl.ds(start, rows), :] = block[:, : heads + LANES]
            out_w_ref[pl.ds(start, rows), :] = block[:, heads + LANES :]
            for j in range(2):
                part = dot(block[:, j * 4 * DH : (j + 1) * 4 * DH], e4_ref[...])
                pad_s[pl.ds(start, rows), j * 4 * LANES : (j + 1) * 4 * LANES] = part.astype(bf16)
        rows_to = lax.broadcasted_iota(jnp.int32, (LANES, LANES), 0)
        same = (rows_to == lax.broadcasted_iota(jnp.int32, (LANES, LANES), 1)).astype(bf16)
        gains_ref[...] = dot_nt(same[:8], w_ref[:, heads:])

    tok_rows = one_ref.shape[1]
    for i, halves in enumerate(piece_halves(one_ref, one_more_ref, two_ref, two_more_ref)):

        @pl.when(pl.program_id(0) == i)
        def _(halves=halves):
            for j, (ref, slot) in enumerate(halves):
                x_ref[j * tok_rows : (j + 1) * tok_rows, :] = ref[slot]

    x = x_ref[...].astype(f32)
    scale = rms_scale(x)
    scale_ref[...] = scale
    normed = (x * scale * gains_ref[0:1, :]).astype(bf16)
    n_ref[...] = normed
    pre = dot(normed, pad_s[...])
    cos, sin = cos_ref[...], sin_ref[...]
    parts = []
    for head in range(8):
        piece = pre[:, head * LANES : (head + 1) * LANES]
        if head < 6:
            piece = piece * cos + pltpu.roll(piece, LANES // 2, 1) * sin
        parts.append(piece.astype(bf16))
    q_ref[...] = jnp.concatenate(parts[:4], axis=1)
    kv = dot_nt(jnp.concatenate(parts[4:], axis=1), e4_ref[...]).astype(bf16)
    in_first = pl.program_id(0) < 2

    @pl.when(in_first)
    def _():
        kv_first_ref[...] = kv

    @pl.when(jnp.logical_not(in_first))
    def _():
        kv_second_ref[...] = kv


def project(info, pieces, blocks, cos, sin, e4):
    _, tok_rows, width = pieces[0].shape
    rows, step = 2 * PLANE * tok_rows, 2 * tok_rows
    size = len(blocks) // 2
    cols = blocks[0].shape[1]
    first = 8 * DH + LANES
    whole = lambda a: pl.BlockSpec(a.shape, lambda i, n: (0,) * a.ndim)
    by_row = lambda c: pl.BlockSpec((step, c), lambda i, n: (i, 0))
    return pl.pallas_call(
        lambda *refs: project_kernel(size, *refs),
        grid_spec=pltpu.PrefetchScalarGridSpec(
            num_scalar_prefetch=1,
            grid=(rows // step,),
            in_specs=[whole(a) for a in pieces]
            + [by_row(LANES), by_row(LANES), whole(e4)]
            + [whole(b) for b in blocks],
            out_specs=[
                by_row(width),
                by_row(width),
                by_row(4 * LANES),
                pl.BlockSpec((step, 4 * DH), lambda i, n: (jnp.minimum(i, 1), 0)),
                pl.BlockSpec((step, 4 * DH), lambda i, n: (jnp.maximum(i - 2, 0), 0)),
                pl.BlockSpec((width, first), lambda i, n: (0, 0)),
                pl.BlockSpec((width, cols - first), lambda i, n: (0, 0)),
                pl.BlockSpec((8, width), lambda i, n: (0, 0)),
                by_row(1),
            ],
            scratch_shapes=[pltpu.VMEM((width, 8 * LANES), bf16)],
        ),
        out_shape=[
            jax.ShapeDtypeStruct((rows, width), bf16),
            jax.ShapeDtypeStruct((rows, width), bf16),
            jax.ShapeDtypeStruct((rows, 4 * LANES), bf16),
            jax.ShapeDtypeStruct((rows // 2, 4 * DH), bf16),
            jax.ShapeDtypeStruct((rows // 2, 4 * DH), bf16),
            jax.ShapeDtypeStruct((width, first), bf16),
            jax.ShapeDtypeStruct((width, cols - first), bf16),
            jax.ShapeDtypeStruct((8, width), f32),
            jax.ShapeDtypeStruct((rows, 1), f32),
        ],
        compiler_params=pltpu.CompilerParams(vmem_limit_bytes=VMEM_BYTES),
        cost_estimate=LIGHT,
        name="project",
    )(info, *pieces, cos, sin, e4, *blocks)


def assemble_kernel(size, info_ref, *rest):
    blocks, out_ref = rest[: 2 * size], rest[2 * size]
    rows = blocks[0].shape[0]
    for i, block in enumerate(blocks):
        core = info_ref[1] if i < size else 1 - info_ref[1]
        start = pl.multiple_of((core * size + lax.rem(info_ref[0] - i % size + size, size)) * rows, rows)
        out_ref[pl.ds(start, rows), :] = block[...]


def assemble(info, blocks):
    size = len(blocks) // 2
    rows, width = blocks[0].shape
    step = width // 3 if width % 384 == 0 else width // 4
    return pl.pallas_call(
        lambda *refs: assemble_kernel(size, *refs),
        grid_spec=pltpu.PrefetchScalarGridSpec(
            num_scalar_prefetch=1,
            grid=(width // step,),
            in_specs=[pl.BlockSpec((rows, step), lambda i, n: (0, i)) for _ in blocks],
            out_specs=pl.BlockSpec((len(blocks) * rows, step), lambda i, n: (0, i)),
        ),
        out_shape=jax.ShapeDtypeStruct((len(blocks) * rows, width), blocks[0].dtype),
        compiler_params=pltpu.CompilerParams(vmem_limit_bytes=VMEM_BYTES),
        cost_estimate=LIGHT,
        name="assemble",
    )(info, *blocks)


def allowed_of(info_ref, k, chunk, qpos_ref, qbeg_ref, kpos_ref):
    kpos = kpos_ref[...] + (info_ref[0] - k) * chunk
    return (kpos <= qpos_ref[...]) & (kpos >= qbeg_ref[...])


def useful_of(info_ref, m, k, chunk):
    z = info_ref[0]
    return (k <= z) & ((z - k + 1) * chunk - 1 >= info_ref[2 + m])


def stack_heads(block, h):
    return jnp.concatenate(
        [block[:, (2 * h) * LANES : (2 * h + 1) * LANES], block[:, (2 * h + 1) * LANES : (2 * h + 2) * LANES]], axis=0
    )


def run_kernel(body, info, inputs, outs, aliases, name):
    def spec(entry):
        if isinstance(entry, tuple):
            return pl.BlockSpec(entry[1], lambda i, n: entry[2])
        return pl.BlockSpec(entry.shape, lambda i, n: (0,) * entry.ndim)

    return list(
        pl.pallas_call(
            body,
            grid_spec=pltpu.PrefetchScalarGridSpec(
                num_scalar_prefetch=1,
                grid=(1,),
                in_specs=[spec(entry) for entry in inputs],
                out_specs=[pl.BlockSpec(o.shape, lambda i, n, o=o: (0,) * len(o.shape)) for o in outs],
            ),
            out_shape=outs,
            input_output_aliases=aliases,
            compiler_params=pltpu.CompilerParams(vmem_limit_bytes=VMEM_BYTES),
            cost_estimate=CHUNK_COST,
            name=name,
        )(info, *[entry[0] if isinstance(entry, tuple) else entry for entry in inputs])
    )


def attend_kernel(m, k, last, info_ref, q_ref, kv_ref, qpos_ref, qbeg_ref, kpos_ref, e_ref, *rest):
    chunk = kv_ref.shape[0]
    if k > 0:
        top_in, acc_in, rest = rest[0], rest[1], rest[2:]
    top_ref, acc_ref = rest[0], rest[1]

    def run():
        allowed = allowed_of(info_ref, k, chunk, qpos_ref, qbeg_ref, kpos_ref)
        kv = kv_ref[...]
        q = q_ref[...]
        one_lane = (lax.broadcasted_iota(jnp.int32, (1, LANES), 1) == DH // 2).astype(f32)
        for h in range(2):
            keys = dot(kv, e_ref[:, h * LANES : (h + 1) * LANES]).astype(bf16)
            vals = (dot(kv, e_ref[:, (2 + h) * LANES : (3 + h) * LANES]) + one_lane).astype(bf16)
            s = jnp.where(allowed, dot_nt(keys, stack_heads(q, h)), masked_score)
            new = jnp.max(s, axis=0, keepdims=True)
            if k > 0:
                old = top_in[h]
                new = jnp.maximum(old, new)
            w = jnp.where(allowed, jnp.exp2((s - new) * exp2_scale), 0.0).astype(bf16)
            acc = dot_tn(vals, w)
            if k > 0:
                acc = acc_in[h] * jnp.exp2((old - new) * exp2_scale) + acc
            acc_ref[h] = acc
            top_ref[h] = new

    if k == 0:
        run()
    else:
        useful = useful_of(info_ref, m, k, chunk)
        pl.when(useful)(run)

        @pl.when(jnp.logical_not(useful))
        def _():
            top_ref[...] = top_in[...]
            acc_ref[...] = acc_in[...]

    if last:
        att_ref, low_ref, lse_ref = rest[2:]
        parts = []
        for h in range(2):
            acc = acc_ref[h]
            total = acc[DH // 2 : DH // 2 + 1, :]
            lse_ref[h] = top_ref[h] * exp2_scale + jnp.log2(total)
            flat = (acc / total).T
            rows = flat.shape[0] // 2
            parts += [flat[:rows], flat[rows:]]
        att = jnp.concatenate(parts, axis=1)
        att_ref[...] = att
        low_ref[...] = dot_nt(att.astype(bf16), e_ref[...]).astype(bf16)


def attend(m, k, last, info, q, kv, qpos, qbeg, kpos, e4, state):
    rows = q[1][0]
    outs = [jax.ShapeDtypeStruct((2, 1, 2 * rows), f32), jax.ShapeDtypeStruct((2, LANES, 2 * rows), f32)]
    if last:
        outs += [
            jax.ShapeDtypeStruct((rows, 4 * LANES), f32),
            jax.ShapeDtypeStruct((rows, 4 * DH), bf16),
            jax.ShapeDtypeStruct((2, 1, 2 * rows), f32),
        ]
    return run_kernel(
        lambda *refs: attend_kernel(m, k, last, *refs),
        info,
        [q, kv, qpos, qbeg, kpos, e4] + state,
        outs,
        {7: 0, 8: 1} if k > 0 else {},
        "attend",
    )


def attend_back_kernel(
    m, k, first, last, info_ref, q_ref, kv_ref, lse_ref, qpos_ref, qbeg_ref, kpos_ref, cosk_ref, sink_ref, e_ref, *rest
):
    chunk = kv_ref.shape[0]
    if first:
        g_ref, att_ref, rest = rest[0], rest[1], rest[2:]
        go_ref, delta_ref, dq_ref, dkv_ref = rest[:4]
        go = dot(g_ref[...], e_ref[...])
        for h in range(2):
            go_h = stack_heads(go, h)
            go_ref[h] = go_h.astype(bf16)
            prod = go_h * stack_heads(att_ref[...], h)
            delta_ref[h] = jnp.sum(prod.T, axis=0, keepdims=True)
    else:
        go_ref, delta_ref, dq_in, moved_ref, rest = rest[0], rest[1], rest[2], rest[3], rest[4:]
        dq_ref, dkv_ref = rest[:2]

    def run():
        allowed = allowed_of(info_ref, k, chunk, qpos_ref, qbeg_ref, kpos_ref)
        kv = kv_ref[...]
        q = q_ref[...]
        cosk, sink = cosk_ref[...], sink_ref[...]
        grad_keys, grad_vals = [], []
        for h in range(2):
            keys = dot(kv, e_ref[:, h * LANES : (h + 1) * LANES]).astype(bf16)
            vals = dot(kv, e_ref[:, (2 + h) * LANES : (3 + h) * LANES]).astype(bf16)
            q_h = stack_heads(q, h)
            go_h = go_ref[h]
            s = dot_nt(keys, q_h)
            w = jnp.where(allowed, jnp.exp2(s * exp2_scale - lse_ref[h]), 0.0)
            grad_vals.append(dot(w.astype(bf16), go_h).astype(bf16))
            ds = (w * (dot_nt(vals, go_h) - delta_ref[h])).astype(bf16)
            dq = dot_tn(keys, ds)
            dq_ref[h] = dq if first else dq_in[h] + dq
            gk = dot(ds, q_h) * score_scale
            gk = gk * cosk + pltpu.roll(gk * sink, LANES // 2, 1)
            grad_keys.append(gk.astype(bf16))
        total = dot_nt(jnp.concatenate(grad_keys + grad_vals, axis=1), e_ref[...])
        if not first:
            total = total + moved_ref[...].astype(f32)
        dkv_ref[...] = total.astype(bf16)

    if k == 0:
        run()
    else:
        useful = useful_of(info_ref, m, k, chunk)
        pl.when(useful)(run)

        @pl.when(jnp.logical_not(useful))
        def _():
            dkv_ref[...] = jnp.zeros(dkv_ref.shape, bf16) if first else moved_ref[...]
            dq_ref[...] = jnp.zeros(dq_ref.shape, f32) if first else dq_in[...]

    if last:
        out_ref = rest[-1]
        parts = []
        for h in range(2):
            flat = dq_ref[h].T * score_scale
            rows = flat.shape[0] // 2
            for piece in (flat[:rows], flat[rows:]):
                parts.append((piece * cosk_ref[...] + pltpu.roll(piece * sink_ref[...], LANES // 2, 1)).astype(bf16))
        out_ref[...] = dot_nt(jnp.concatenate(parts, axis=1), e_ref[...]).astype(bf16)


def attend_back(m, k, first, last, info, q, kv, lse, qpos, qbeg, kpos, cosk, sink, e4, state):
    rows = q[1][0]
    outs = []
    if first:
        outs += [jax.ShapeDtypeStruct((2, 2 * rows, LANES), bf16), jax.ShapeDtypeStruct((2, 1, 2 * rows), f32)]
    outs += [jax.ShapeDtypeStruct((2, LANES, 2 * rows), f32), jax.ShapeDtypeStruct((rows, 4 * DH), bf16)]
    if last:
        outs += [jax.ShapeDtypeStruct((rows, 4 * DH), bf16)]
    return run_kernel(
        lambda *refs: attend_back_kernel(m, k, first, last, *refs),
        info,
        [q, kv, lse, qpos, qbeg, kpos, cosk, sink, e4] + state,
        outs,
        {} if first else {12: 0},
        "attend_back",
    )


def store_split(sum_of, tok_rows, first_ref, second_ref, keep_first_ref, keep_second_ref):
    for i, slot in enumerate((1, 3)):
        first_ref[i] = sum_of(slot * tok_rows, tok_rows).astype(bf16)
        keep_first_ref[i] = sum_of((slot - 1) * tok_rows, tok_rows)
    for i in range(2):
        second_ref[i] = sum_of((PLANE + 2 + i) * tok_rows, tok_rows).astype(bf16)
        keep_second_ref[i] = sum_of((PLANE + i) * tok_rows, tok_rows)


def split_outs(tok_rows, width):
    return [jax.ShapeDtypeStruct((2, tok_rows, width), kind) for kind in (bf16, bf16, f32, f32)]


def dot_split_kernel(tok_rows, parts, *refs):
    w_ref, rest = refs[parts], refs[parts + 1 :]
    acc_s = rest[-1]
    rows = refs[0].shape[0]
    for i in range(parts):
        acc_s[i * rows : (i + 1) * rows, :] = dot(refs[i][...], w_ref[...])
    store_split(lambda start, n: acc_s[start : start + n, :], tok_rows, *rest[:-1])


def dot_split(parts, w):
    part_rows, inner = parts[0].shape
    rows = len(parts) * part_rows
    tok_rows = rows // (2 * PLANE)
    width = w.shape[1]
    step = width // 3
    outs = split_outs(tok_rows, width)
    return list(
        pl.pallas_call(
            lambda *refs: dot_split_kernel(tok_rows, len(parts), *refs),
            grid=(3,),
            in_specs=[pl.BlockSpec((part_rows, inner), lambda i: (0, 0)) for _ in parts]
            + [pl.BlockSpec((inner, step), lambda i: (0, i))],
            out_specs=[pl.BlockSpec((2, tok_rows, step), lambda i: (0, 0, i)) for _ in outs],
            out_shape=outs,
            scratch_shapes=[pltpu.VMEM((rows, step), f32)],
            compiler_params=pltpu.CompilerParams(vmem_limit_bytes=VMEM_BYTES),
            cost_estimate=LIGHT,
            name="dot_split",
        )(*parts, w)
    )


def ffn_kernel(size, tok_rows, info_ref, one_ref, two_ref, one_more_ref, two_more_ref, g_ref, *rest):
    gu_blocks, down_blocks, rest = rest[: 2 * size], rest[2 * size : 4 * size], rest[4 * size :]
    hidden_ref, *outs = rest[:5]
    gu_theirs_ref, gu_mine_ref, down_theirs_ref, down_mine_ref = rest[5:9]
    gu_s, down_s, acc_s, flat_s, grad_s, n_ref, sems = rest[9:]
    f, last = pl.program_id(0), pl.num_programs(0) - 1
    units = hidden_ref.shape[1]
    half = flat_s.shape[0] // 2

    def place(i, rows):
        core = info_ref[1] if i < size else 1 - info_ref[1]
        return pl.ds(pl.multiple_of((core * size + lax.rem(info_ref[0] - i % size + size, size)) * rows, rows), rows)

    @pl.when(f == 0)
    def _():
        copies = []
        for i, halves in enumerate(piece_halves(one_ref, one_more_ref, two_ref, two_more_ref)):
            for j, (ref, slot) in enumerate(halves):
                at = pl.ds((2 * i + j) * tok_rows, tok_rows)
                copies.append(pltpu.make_async_copy(ref.at[slot], n_ref.at[at], sems.at[2 * i + j]))
                copies[-1].start()
        acc_s[...] = jnp.zeros(acc_s.shape, f32)
        for copy in copies:
            copy.wait()
        flat_s[...] = n_ref[...].T
        for i, block in enumerate(down_blocks):
            down_s[place(i, block.shape[0]), :] = block[...]

    for i, block in enumerate(gu_blocks):
        gu_s[place(i, block.shape[0]), :] = block[...]
    w_down = down_s.at[pl.ds(pl.multiple_of(f * units, units), units)]
    step = 4 * tok_rows

    @pl.loop(0, n_ref.shape[0] // step)
    def _(r):
        at = pl.ds(pl.multiple_of(r * step, step), step)
        pre = dot(n_ref[at, :], gu_s[...])
        grad_hidden = dot_nt(g_ref[at, :], w_down[...])
        gate_pre, up_pre = pre[:, :units], pre[:, units:]
        sigmoid_gate = jax.nn.sigmoid(gate_pre)
        silu_gate = gate_pre * sigmoid_gate
        hidden_ref[at, :] = (silu_gate * up_pre).astype(bf16)
        grad_gate = grad_hidden * up_pre * sigmoid_gate * (1.0 + gate_pre * (1.0 - sigmoid_gate))
        both = jnp.concatenate([grad_gate.astype(bf16), (grad_hidden * silu_gate).astype(bf16)], axis=1)
        grad_s[at, :] = both
        acc_s[at, :] += dot_nt(both, gu_s[...])

    core = info_ref[1]
    gu_mine_ref[...] = dot(flat_s[pl.ds(pl.multiple_of(core * half, half), half), :], grad_s[...]).astype(bf16)
    gu_theirs_ref[...] = dot(flat_s[pl.ds(pl.multiple_of((1 - core) * half, half), half), :], grad_s[...]).astype(bf16)
    term_down = dot_tn(hidden_ref[...], g_ref[...]).astype(bf16)
    is_mine = lax.div(f, pl.num_programs(0) // 2) == core

    @pl.when(is_mine)
    def _():
        down_mine_ref[...] = term_down

    @pl.when(jnp.logical_not(is_mine))
    def _():
        down_theirs_ref[...] = term_down

    @pl.when(f == last)
    def _():
        store_split(lambda start, n: acc_s[start : start + n, :], tok_rows, *outs)


def ffn(info, pieces, grad_mlp, gu_blocks, down_blocks):
    rows, width = grad_mlp.shape
    size = len(gu_blocks) // 2
    tok_rows = rows // (2 * PLANE)
    ff_part = gu_blocks[0].shape[1] // 2
    units = ff_part // FF_TILES
    whole = lambda a: pl.BlockSpec(a.shape, lambda f, n: (0,) * a.ndim, pipeline_mode=pl.Buffered(1))
    outs = split_outs(tok_rows, width)
    gu_half = pl.BlockSpec((width // 2, 2 * units), lambda f, n: (0, f))

    def down_half(core_of):
        return pl.BlockSpec((units, width), lambda f, n: (jnp.clip(f - core_of(n) * (FF_TILES // 2), 0, FF_TILES // 2 - 1), 0))

    return list(
        pl.pallas_call(
            lambda *refs: ffn_kernel(size, tok_rows, *refs),
            grid_spec=pltpu.PrefetchScalarGridSpec(
                num_scalar_prefetch=1,
                grid=(FF_TILES,),
                in_specs=[pl.BlockSpec(memory_space=pl.ANY) for _ in pieces]
                + [whole(grad_mlp)]
                + [pl.BlockSpec((block.shape[0], 2 * units), lambda f, n: (0, f)) for block in gu_blocks]
                + [whole(block) for block in down_blocks],
                out_specs=[pl.BlockSpec((rows, units), lambda f, n: (0, f))]
                + [pl.BlockSpec(o.shape, lambda f, n: (0, 0, 0), pipeline_mode=pl.Buffered(1)) for o in outs]
                + [gu_half, gu_half, down_half(lambda n: 1 - n[1]), down_half(lambda n: n[1])],
                scratch_shapes=[
                    pltpu.VMEM((width, 2 * units), bf16),
                    pltpu.VMEM((ff_part, width), bf16),
                    pltpu.VMEM((rows, width), f32),
                    pltpu.VMEM((width, rows), bf16),
                    pltpu.VMEM((rows, 2 * units), bf16),
                    pltpu.VMEM((rows, width), bf16),
                    pltpu.SemaphoreType.DMA((2 * PLANE,)),
                ],
            ),
            out_shape=[jax.ShapeDtypeStruct((rows, ff_part), bf16)]
            + outs
            + [jax.ShapeDtypeStruct((width // 2, 2 * ff_part), bf16)] * 2
            + [jax.ShapeDtypeStruct((ff_part // 2, width), bf16)] * 2,
            compiler_params=pltpu.CompilerParams(vmem_limit_bytes=58 * 1024 * 1024),
            cost_estimate=LIGHT,
            name="ffn",
        )(info, *pieces, grad_mlp, *gu_blocks, *down_blocks)
    )


def project_back_kernel(tok_rows, parts, info_ref, *rest):
    grads, (w_ref, n_ref, x_ref, scale_ref), rest = rest[:parts], rest[parts : parts + 4], rest[parts + 4 :]
    first_ref, second_ref, keep_first_ref, keep_second_ref, gain_ref, theirs_ref, mine_ref, acc_s, g_ref = rest
    part_rows, part_width = grads[0].shape

    @pl.when(pl.program_id(0) == 0)
    def _():
        for i, grad_ref in enumerate(grads):
            m, j = i % (parts // 2), i // (parts // 2)
            g_ref[m * part_rows : (m + 1) * part_rows, j * part_width : (j + 1) * part_width] = grad_ref[...]

    rows = 2 * tok_rows
    total = jnp.zeros((1, acc_s.shape[1]), f32)
    for i in range(g_ref.shape[0] // rows):
        at = slice(i * rows, (i + 1) * rows)
        acc = dot_nt(g_ref[at, :], w_ref[...])
        acc_s[at, :] = acc
        total = total + jnp.sum(acc * x_ref[at, :].astype(f32) * scale_ref[at, :], axis=0, keepdims=True)
    gain_ref[...] = jnp.broadcast_to(total, gain_ref.shape)
    store_split(lambda start, n: acc_s[start : start + n, :], tok_rows, first_ref, second_ref, keep_first_ref, keep_second_ref)
    term = dot_tn(n_ref[...], g_ref[...]).astype(bf16)
    is_mine = pl.program_id(0) == info_ref[1]

    @pl.when(is_mine)
    def _():
        mine_ref[...] = term

    @pl.when(jnp.logical_not(is_mine))
    def _():
        theirs_ref[...] = term


def project_back(info, grads, w, normed, x, scale):
    rows, width = normed.shape
    inner = 2 * grads[0].shape[1]
    tok_rows = rows // (2 * PLANE)
    half = width // 2
    outs = split_outs(tok_rows, width)
    column = pl.BlockSpec((rows, half), lambda i, n: (0, i))
    out_whole = pl.BlockSpec((half, inner), lambda i, n: (0, 0))
    return list(
        pl.pallas_call(
            lambda *refs: project_back_kernel(tok_rows, len(grads), *refs),
            grid_spec=pltpu.PrefetchScalarGridSpec(
                num_scalar_prefetch=1,
                grid=(2,),
                in_specs=[pl.BlockSpec(g.shape, lambda i, n: (0, 0)) for g in grads]
                + [
                    pl.BlockSpec((half, inner), lambda i, n: (i, 0)),
                    column,
                    column,
                    pl.BlockSpec((rows, 1), lambda i, n: (0, 0)),
                ],
                out_specs=[pl.BlockSpec((2, tok_rows, half), lambda i, n: (0, 0, i)) for _ in outs]
                + [pl.BlockSpec((8, half), lambda i, n: (0, i)), out_whole, out_whole],
                scratch_shapes=[pltpu.VMEM((rows, half), f32), pltpu.VMEM((rows, inner), bf16)],
            ),
            out_shape=outs
            + [jax.ShapeDtypeStruct((8, width), f32)]
            + [jax.ShapeDtypeStruct((half, inner), bf16)] * 2,
            compiler_params=pltpu.CompilerParams(vmem_limit_bytes=VMEM_BYTES),
            cost_estimate=LIGHT,
            name="project_back",
        )(info, *grads, w, normed, x, scale)
    )


def beside(value, bit):
    return lax.ppermute(value, "plane", [(i, i ^ bit) for i in range(PLANE)])


def other_core(value):
    return lax.ppermute(value, "stream", [(0, 1), (1, 0)])


def along(value, step, wrap):
    size = lax.axis_size("zed")
    pairs = [(i, (i + step) % size) for i in range(size) if wrap or 0 <= i + step < size]
    return lax.ppermute(value, "zed", pairs)


def plane_gather_start(own):
    return [own[0], own[1], beside(own[0], 1), beside(own[1], 2)]


def plane_gather_more(first, second, first_got, second_got):
    pair_one, pair_two = jnp.stack([first, first_got]), jnp.stack([second, second_got])
    return [pair_one, pair_two, beside(pair_one, 2), beside(pair_two, 1)]


def plane_gather_end(pair_one, pair_two, first_more, second_more):
    blocks = [pair_one, first_more, pair_two[:1], second_more[:1], pair_two[1:], second_more[1:]]
    return jnp.concatenate(blocks).reshape(-1, pair_one.shape[-1])


def plane_sum_start(split):
    return [beside(split[0], 1), beside(split[1], 2)]


def plane_sum_more(split, got_first, got_second):
    keep_first, keep_second = split[2], split[3]
    more_first = beside((keep_first[1] + got_first[1]).astype(bf16), 2)
    more_second = beside((keep_second[1] + got_second[1]).astype(bf16), 1)
    return [got_first[0], got_second[0], more_first, more_second]


def plane_sum_end(split, got_first, got_second, more_first, more_second):
    return jnp.stack([split[2][0] + got_first + more_first, split[3][0] + got_second + more_second])


def after(value, *earlier):
    return lax.optimization_barrier((value,) + earlier)[0]


def sync(*values):
    return list(lax.optimization_barrier(values))


def core_halves(full):
    size = lax.axis_size("zed")
    s = lax.axis_index("stream")
    full = full.reshape((2, size, -1) + full.shape[1:])
    mine = lax.dynamic_index_in_dim(full, s, 0, keepdims=False)
    theirs = lax.dynamic_index_in_dim(full, 1 - s, 0, keepdims=False)
    return mine, other_core(theirs)


def core_sum(mine, other):
    return (mine.astype(f32) + other.astype(f32)).astype(bf16)


def ring_part(half, k):
    size = lax.axis_size("zed")
    z = lax.axis_index("zed")
    return lax.dynamic_index_in_dim(half, lax.rem(z - k + size, size), 0, keepdims=False)


def ring_add(half, moved, k):
    return (moved.astype(f32) + ring_part(half, k).astype(f32)).astype(bf16)


def plane_swap(value, split, concat):
    return lax.all_to_all(value, "plane", split_axis=split, concat_axis=concat, tiled=True)


def on_device(inputs, cotangent, seq_lengths, gain_attn, gain_ffn, w_query, w_key, w_value, w_out, w_gate, w_up, w_down):
    size = lax.axis_size("zed")
    s, z, p = lax.axis_index("stream"), lax.axis_index("zed"), lax.axis_index("plane")
    micro, _, tok_rows, width = inputs.shape
    chunk = PLANE * tok_rows
    tokens = micro * chunk
    shard_rows = w_query.shape[0]
    ff_block = w_down.shape[0]
    ff_blocks = 2 * size
    ff_part = ff_blocks * ff_block
    q_part, kv_part = HQ * DH // PLANE, HK * DH // PLANE
    out_part = width // PLANE
    e4 = spread(4)

    def by_part(weight):
        return weight.reshape(shard_rows, PLANE, -1)

    def by_ff_part(weight):
        return weight.reshape(shard_rows, ff_blocks, PLANE, ff_block).transpose(0, 2, 1, 3).reshape(shard_rows, PLANE, -1)

    def from_ff_parts(term):
        return term.reshape(shard_rows, PLANE, ff_blocks, ff_block).transpose(0, 2, 1, 3).reshape(shard_rows, -1)

    own_in = inputs[:, 0]
    own_cot = cotangent[:, 0]
    gains = jnp.stack([gain_attn, gain_ffn], axis=1)
    gains = jnp.broadcast_to(jnp.pad(gains, ((0, 0), (0, LANES - 2)))[:, None], (shard_rows, PLANE, LANES))
    qkv_bundle = jnp.concatenate([by_part(w_query), by_part(w_key), by_part(w_value), gains, by_part(w_out)], axis=2)
    qkv_block = plane_swap(qkv_bundle.reshape(shard_rows, -1), 1, 0)
    tiled = (shard_rows, PLANE, FF_TILES, ff_part // FF_TILES)
    ffn_bundle = jnp.stack([by_ff_part(w_gate).reshape(tiled), by_ff_part(w_up).reshape(tiled)], axis=3).reshape(shard_rows, -1)
    qkv_blocks = [qkv_block]
    for _ in range(size - 1):
        qkv_blocks.append(along(qkv_blocks[-1], 1, True))
    ffn_block = plane_swap(after(ffn_bundle, qkv_block), 1, 0)
    pieces = sync(*plane_gather_start(after(own_in, qkv_block)))
    *in_pieces, qkv_blocks[-1] = sync(*plane_gather_more(*pieces), qkv_blocks[-1])
    qkv_other = [other_core(block) for block in qkv_blocks]
    gu_blocks = [after(ffn_block, qkv_blocks[-1])]
    gu_blocks.append(along(gu_blocks[0], 1, True))

    slot_place = ((jnp.arange(PLANE, dtype=jnp.int32) ^ p)[:, None] * tok_rows + jnp.arange(tok_rows, dtype=jnp.int32)[None, :]).reshape(chunk)
    chunk_place = (z - jnp.arange(size, dtype=jnp.int32))[:, None] * chunk + slot_place[None, :]
    lengths = seq_lengths[:, 0]
    seq_ends = jnp.cumsum(lengths, axis=1)
    begins = jnp.sum(
        jnp.where(seq_ends[:, None, None, :] <= chunk_place[None, :, :, None], lengths[:, None, None, :], 0), axis=-1
    )
    own_begin = begins[:, 0]
    lane = np.arange(LANES)
    place_in_half = lane % (LANES // 2)
    real = place_in_half < DH // 2
    frequency = jnp.where(
        real, rope_base ** (-2.0 * jnp.asarray(np.minimum(place_in_half, DH // 2 - 1), f32) / DH), 0.0
    )
    rope_place = (chunk_place[None] - begins).astype(f32)

    def tables(place):
        angles = jnp.maximum(place, 0.0)[..., None] * frequency
        signs = jnp.asarray(np.where(real, np.where(lane < LANES // 2, -1.0, 1.0), 0.0), f32)
        return jnp.where(real, jnp.cos(angles), 0.0), jnp.sin(angles) * signs

    cos, sin = tables(after(rope_place[:, 0], qkv_block))
    index = jnp.stack([z, s]).astype(jnp.int32)
    info = jnp.concatenate([index, jnp.min(own_begin, axis=1)])
    qpos = jnp.tile(chunk_place[0], 2)[None]
    qbeg = jnp.tile(own_begin, (1, 2))[:, None]
    kpos = slot_place[:, None]

    gathered_in, normed_one, q_rot, *kv_own, full_qkv, full_oc, full_gains, in_scale = project(
        index, in_pieces, qkv_blocks + qkv_other, cos.reshape(tokens, LANES), sin.reshape(tokens, LANES), e4
    )
    gain_one, gain_two = full_gains[0:1], full_gains[1:2]
    full_out = plane_swap(full_oc, 0, 1)
    cot_pieces = plane_gather_start(after(own_cot, *kv_own))
    q_rot = [(q_rot, (chunk, 4 * LANES), (m, 0)) for m in range(micro)]
    kv_windows = [[piece] for piece in kv_own]
    kv_pieces = [[piece] for piece in kv_own]
    qbeg = [(qbeg, (None, 1, 2 * chunk), (m, 0, 0)) for m in range(micro)]
    states = [[] for _ in range(micro)]
    for k in range(size):
        if k < size - 1:
            arrived = [along(kv_pieces[m][k], 1, False) for m in range(micro)]
        for m in range(micro):
            states[m] = attend(m, k, k == size - 1, info, q_rot[m], kv_windows[m][k], qpos, qbeg[m], kpos, e4, states[m])
        if k < size - 1:
            tops = [state[0] for state in states]
            if k == 0:
                tops[0], tops[1], arrived[0], arrived[1], gu_blocks[1], *cot_pieces = sync(
                    *tops, *arrived, gu_blocks[1], *cot_pieces
                )
                cot_pieces = plane_gather_more(*cot_pieces)
            elif k == 1:
                tops[0], tops[1], arrived[0], arrived[1], full_out, *cot_pieces = sync(*tops, *arrived, full_out, *cot_pieces)
            else:
                tops[0], tops[1], arrived[0], arrived[1] = sync(*tops, *arrived)
            for m in range(micro):
                states[m] = [tops[m], states[m][1]]
                kv_pieces[m].append(arrived[m])
                kv_windows[m].append(arrived[m])
    kv_there = [pieces[-1] for pieces in kv_pieces]
    attended, lse = [state[2] for state in states], [state[4] for state in states]
    attn_low = jnp.concatenate([state[3] for state in states], axis=0)
    gathered_cot = plane_gather_end(*cot_pieces)

    gu_blocks[1], down_block, rope_place = sync(gu_blocks[1], w_down, rope_place, *kv_there)[:3]
    down_blocks = [down_block, along(down_block, 1, True)]
    branch_split = dot_split([state[3] for state in states], full_out)
    branch_split = sync(*branch_split, down_blocks[1])
    down_blocks[1] = branch_split.pop()
    gu_blocks.append(along(after(gu_blocks[1], down_blocks[1]), 1, True))
    *got, gu_blocks[2] = sync(*plane_sum_start(branch_split), gu_blocks[2])
    down_blocks.append(along(after(down_blocks[1], gu_blocks[2]), 1, True))
    cos_all, sin_all = tables(after(rope_place, gu_blocks[2]))
    *got, down_blocks[2], cos_all, sin_all = sync(*plane_sum_more(branch_split, *got), down_blocks[2], cos_all, sin_all)
    layer_in = own_in.astype(f32)
    middle = layer_in + plane_sum_end(branch_split, *got)
    scale_two = rms_scale(middle)
    pieces = plane_gather_start((middle * scale_two * gain_two).astype(bf16))
    for k in range(2, size - 1):
        down_blocks.append(along(down_blocks[k], 1, True))
    *pieces, down_blocks[-1] = sync(*pieces, down_blocks[-1])
    for k in range(2, size - 1):
        gu_blocks.append(along(after(gu_blocks[k], down_blocks[-1]), 1, True))
    *pieces, gu_blocks[-1] = sync(*plane_gather_more(*pieces), gu_blocks[-1])

    gu_all = gu_blocks + [other_core(block) for block in gu_blocks]
    down_all = down_blocks + [other_core(block) for block in down_blocks]
    hidden, *outs = ffn(index, pieces, gathered_cot, gu_all, down_all)
    normed_split, (gu_theirs, gu_mine, down_theirs, down_mine) = outs[:4], outs[4:]
    got = plane_sum_start(normed_split)
    gu_half = core_sum(gu_mine, other_core(gu_theirs)).reshape(size, -1, 2 * ff_part)
    down_half = core_sum(down_mine, other_core(down_theirs)).reshape(size, -1, width)
    gu_total, down_total = ring_part(gu_half, size - 1), ring_part(down_half, size - 1)
    *got, gu_total, down_total = sync(*got, gu_total, down_total)
    gu_moved, down_moved = along(gu_total, -1, True), along(down_total, -1, True)
    got = sync(*plane_sum_more(normed_split, *got))
    grad_normed_two = plane_sum_end(normed_split, *got)
    grad_y = own_cot.astype(f32)
    grad_gain_two = jnp.sum(grad_normed_two * middle * scale_two, axis=(0, 1))
    weighted = grad_normed_two * gain_two
    grad_middle = (
        grad_y
        + scale_two * weighted
        - middle * scale_two**3 * jnp.mean(middle * weighted, axis=-1, keepdims=True)
    )
    pieces = plane_gather_start(grad_middle.astype(bf16))
    *pieces, gu_moved, down_moved = sync(*pieces, gu_moved, down_moved)
    gu_total, down_total = ring_add(gu_half, gu_moved, size - 2), ring_add(down_half, down_moved, size - 2)
    gu_moved, down_moved = along(gu_total, -1, True), along(down_total, -1, True)
    full_down = assemble(index, [after(down_all[0], gu_total)] + down_all[1:])
    result_split = dot_split([after(hidden, gu_total)], full_down)
    pieces = plane_gather_more(*pieces)
    for k in range(size - 3, -1, -1):
        gu_total, down_total = ring_add(gu_half, gu_moved, k), ring_add(down_half, down_moved, k)
        if k == size - 3:
            *pieces, gu_total, down_total, result_split[0] = sync(*pieces, gu_total, down_total, result_split[0])
        if k > 0:
            gu_moved, down_moved = along(gu_total, -1, True), along(down_total, -1, True)
    sum_gu, sum_down = gu_total, down_total
    grad_branch = plane_gather_end(*pieces)
    grad_attn = dot_nt(grad_branch, full_out).astype(bf16)

    attended[-1] = after(attended[-1], sum_down)
    states = [[(grad_attn, (chunk, q_part), (m, 0)), attended[m]] for m in range(micro)]
    grad_query = [None] * micro
    terms = [None] * micro
    for k in range(size - 1, -1, -1):
        first = k == size - 1
        for m in range(micro):
            outs = attend_back(
                m, k, first, k == 0, info, q_rot[m], kv_windows[m][k], lse[m], qpos, qbeg[m], kpos,
                (cos_all, (None, None, chunk, LANES), (m, k, 0, 0)), (sin_all, (None, None, chunk, LANES), (m, k, 0, 0)),
                e4, states[m] if first else states[m] + [moved[m]],
            )
            states[m] = outs[:3] if first else states[m][:2] + [outs[0]]
            terms[m] = outs[3] if first else outs[1]
            if k == 0:
                grad_query[m] = outs[-1]
        if k > 0:
            moved = [along(term, -1, False) for term in terms]
            moved[0] = after(moved[0], terms[-1], *([sum_gu, sum_down] if first else []))
        if first:
            got = plane_sum_start(sync(*result_split[:2], *terms)[:2])
            term_out = plane_swap(dot_tn(attn_low, after(grad_branch, *terms)).astype(bf16), 1, 0)
        elif k == size - 2:
            moved[-1], term_out, *got = sync(moved[-1], term_out, *got)
            out_mine, out_other = core_halves(term_out)
            got = plane_sum_more(result_split, *got)
        elif k == size - 3:
            moved[-1], out_other, *got = sync(moved[-1], out_other, *got)
            output = (middle + plane_sum_end(result_split, *got)).astype(bf16)
            out_half = core_sum(out_mine, out_other)

    *part_split, gain_rows, qkv_theirs, qkv_mine = project_back(index, grad_query + terms, full_qkv, normed_one, gathered_in, in_scale)
    got = plane_sum_start(part_split)
    gain_terms = jnp.stack([gain_rows[0], grad_gain_two]).astype(bf16)
    gain_terms = jnp.pad(gain_terms, ((0, LANES - 2), (0, 0))).T
    gain_mine, gain_other = core_halves(gain_terms)
    qkv_half = core_sum(qkv_mine, other_core(qkv_theirs)).reshape(size, shard_rows * PLANE, -1)
    last_half = jnp.concatenate([qkv_half, out_half, core_sum(gain_mine, gain_other)], axis=-1)
    last_total = ring_part(last_half, size - 1)
    sum_gu = plane_swap(after(sum_gu, last_total), 0, 1)
    for k in range(size - 2, -1, -1):
        last_moved = along(last_total, -1, True)
        if k == size - 2:
            *got, last_moved = sync(*got, last_moved)
            got = plane_sum_more(part_split, *got)
        elif k == size - 3:
            *got, last_moved, sum_gu = sync(*got, last_moved, sum_gu)
        last_total = ring_add(last_half, last_moved, k)
    grad_normed_one = plane_sum_end(part_split, *got)
    last_total = plane_swap(last_total, 0, 1).astype(f32).reshape(shard_rows, PLANE, -1)
    scale_one = rms_scale(layer_in)
    weighted = grad_normed_one * gain_one
    input_grad = (
        grad_middle
        + scale_one * weighted
        - layer_in * scale_one**3 * jnp.mean(layer_in * weighted, axis=-1, keepdims=True)
    )
    sum_gu = sum_gu.astype(f32).reshape(shard_rows, PLANE, FF_TILES, 2, ff_part // FF_TILES)
    cuts = np.cumsum([q_part, kv_part, kv_part, out_part])
    sum_query, sum_key, sum_value, sum_out, gain_sum = jnp.split(last_total, cuts, axis=2)
    gain_sum = jnp.sum(gain_sum, axis=1)
    return (
        output[:, None],
        input_grad[:, None],
        gain_sum[:, 0],
        gain_sum[:, 1],
        sum_query.reshape(shard_rows, -1),
        sum_key.reshape(shard_rows, -1),
        sum_value.reshape(shard_rows, -1),
        sum_out.reshape(shard_rows, -1),
        from_ff_parts(sum_gu[:, :, :, 0]),
        from_ff_parts(sum_gu[:, :, :, 1]),
        sum_down.astype(f32),
    )


def solution(mesh):
    blocks = mesh.shape["blk"]
    grid = Mesh(mesh.devices.reshape(2, blocks // PLANE, PLANE), ("stream", "zed", "plane"))
    tokens = P(None, "stream", ("zed", "plane"), None)
    vector = P(("stream", "zed", "plane"))
    matrix = P(("stream", "zed", "plane"), None)
    return jax.shard_map(
        on_device,
        mesh=grid,
        in_specs=(tokens, tokens, P(None, "stream", None), vector, vector) + (matrix,) * 7,
        out_specs=(tokens, tokens, vector, vector) + (matrix,) * 7,
        check_vma=False,
    )
```
